256 devices in a mesh: dp: 16 (over z, x_hi), group: 16 (over x_lo, y, core).
Axes of the slice: x: 4 (x_hi: 2, x_lo: 2; x = x_hi * 2 + x_lo), y: 4, z: 8, core: 2. Of those that a mesh axis runs over, the one named last changes fastest.
Arguments:
- prefix_keys: bfloat16 [16, 384, 512], P('dp', 'group'), may hold values from -6 to 6
- prefix_values: bfloat16 [16, 384, 512], P('dp', 'group'), may hold values from -6 to 6
- resp_queries: bfloat16 [16, 16, 128, 4096], P('dp', 'group'), may hold values from -6 to 6
- resp_keys: bfloat16 [16, 16, 128, 512], P('dp', 'group'), may hold values from -6 to 6
- resp_values: bfloat16 [16, 16, 128, 512], P('dp', 'group'), may hold values from -6 to 6
- grad_out: bfloat16 [16, 16, 128, 4096], P('dp', 'group'), may hold values from -6 to 6
- lengths: int32 [16, 16], P('dp', 'group'), may hold values from 1 to 128
- buckets: int32 [16, 16], P('dp', 'group'), may hold values from 0 to 4
Outputs:
- grad_queries: bfloat16 [16, 16, 128, 4096], P('dp', 'group')
- grad_resp_keys: bfloat16 [16, 16, 128, 512], P('dp', 'group')
- grad_resp_values: bfloat16 [16, 16, 128, 512], P('dp', 'group')
- grad_prefix_keys: bfloat16 [16, 384, 512], P('dp', 'group')
- grad_prefix_values: bfloat16 [16, 384, 512], P('dp', 'group')
The draws below stay inside these ranges and needn't reach their ends.
All inputs are finite; a program needn't handle non-finite values.
Results may differ from the reference program's by a relative error of at most 0.0092.
Values may be sent and summed in bfloat16 or wider, within the bound.
No kernel may reach another device: no remote copies, remote signals or barrier semaphores. Data moves between devices by JAX's collectives and lax.ppermute only.
A program may use at most 128 MiB of HBM per device.

```python
import math
import jax
import jax.numpy as jnp
from jax import lax

HEADS = 32
KV_HEADS = 4
HEAD_DIM = 128
PREFIX = 384
RESP = 128
BUCKETS = 5
RESPONSES = 16
PROMPTS = 16


def draw_prefix_keys(key, part):
    key = jax.random.fold_in(key, 21)
    base_key = jax.random.fold_in(key, 0)
    shape = (PROMPTS, PREFIX, KV_HEADS * HEAD_DIM)
    base = jnp.clip(jax.random.normal(base_key, shape, jnp.float32), -6.0, 6.0)
    return base.astype(jnp.bfloat16)


def draw_resp_queries(key, part):
    key = jax.random.fold_in(key, 22)
    base_key = jax.random.fold_in(key, 0)
    shape = (PROMPTS, RESPONSES, RESP, HEADS * HEAD_DIM)
    base = jnp.clip(jax.random.normal(base_key, shape, jnp.float32), -6.0, 6.0)
    return base.astype(jnp.bfloat16)


def plant(result, stream_key, least, top_value):
    dims = result.shape
    spot = [jax.random.randint(jax.random.fold_in(stream_key, axis), (), 0, dims[axis]) for axis in range(len(dims))]
    result = result.at[tuple(spot)].set(least)
    longest = dims.index(max(dims))
    spot[longest] = (spot[longest] + 1) % dims[longest]
    return result.at[tuple(spot)].set(top_value)


def levels(key, extent, cuts, least, high):
    factor_of = 1.0
    for dim, parts in cuts:
        heights = jax.random.uniform(jax.random.fold_in(jax.random.fold_in(key, 6), dim), (parts,), jnp.float32, least / len(cuts), high / len(cuts))
        factor_of = factor_of * jnp.repeat(jnp.exp(heights), extent[dim] // parts).reshape((-1,) + (1,) * (len(extent) - 1 - dim))
    return factor_of


def bell_draw(own_key, extent, deviation, bound, pieces=(), dtype=jnp.bfloat16):
    drawn = jax.random.normal(own_key, extent, jnp.float32) * deviation
    if len(pieces) > 0:
        drawn = levels(own_key, extent, pieces, -0.22, 0.18) * drawn
    return jnp.clip(drawn, min=-bound, max=bound).astype(dtype)


def setup_inputs(seed: int = 0) -> dict:
    arg_keys = jax.random.split(jax.random.key(seed), 9)
    return {
        "prefix_keys": draw_prefix_keys(jax.random.fold_in(arg_keys[8], 71), 0),
        "prefix_values": bell_draw(arg_keys[1], (PROMPTS, PREFIX, KV_HEADS * HEAD_DIM), 1.0, 6.0, ((0, 16), (1, 16))),
        "resp_queries": draw_resp_queries(jax.random.fold_in(arg_keys[8], 71), 0),
        "resp_keys": bell_draw(arg_keys[3], (PROMPTS, RESPONSES, RESP, KV_HEADS * HEAD_DIM), 1.0, 6.0, ((0, 16), (1, 16))),
        "resp_values": bell_draw(arg_keys[4], (PROMPTS, RESPONSES, RESP, KV_HEADS * HEAD_DIM), 1.0, 6.0, ((0, 16), (1, 16))),
        "grad_out": bell_draw(arg_keys[5], (PROMPTS, RESPONSES, RESP, HEADS * HEAD_DIM), 1.0, 6.0, ((0, 16), (1, 16))),
        "lengths": plant(jax.random.randint(arg_keys[6], (PROMPTS, RESPONSES), 1, RESP + 1), jax.random.fold_in(arg_keys[6], 1), 1, RESP).astype(jnp.int32),
        "buckets": plant(jax.random.randint(arg_keys[7], (PROMPTS, RESPONSES), 0, BUCKETS), jax.random.fold_in(arg_keys[7], 1), 0, BUCKETS - 1).astype(jnp.int32),
    }


def low_copy(values):
    rounded = lax.optimization_barrier(values.astype(jnp.bfloat16))
    return rounded.astype(jnp.float32)

def prompt_backward(operands):
    weighted, queries, near_keys, near_values, far_keys, far_values = operands
    responses = queries.shape[0]
    resp_slots = queries.shape[1]
    group_heads = HEADS // KV_HEADS
    score_scale = 1.0 / math.sqrt(HEAD_DIM)
    queries = queries.reshape(responses, resp_slots, KV_HEADS, group_heads, HEAD_DIM).astype(jnp.float32)
    grads = weighted.reshape(responses, resp_slots, KV_HEADS, group_heads, HEAD_DIM).astype(jnp.float32)
    near_keys = near_keys.reshape(responses, resp_slots, KV_HEADS, HEAD_DIM).astype(jnp.float32)
    near_values = near_values.reshape(responses, resp_slots, KV_HEADS, HEAD_DIM).astype(jnp.float32)
    far_keys = far_keys.reshape(-1, KV_HEADS, HEAD_DIM).astype(jnp.float32)
    far_values = far_values.reshape(-1, KV_HEADS, HEAD_DIM).astype(jnp.float32)
    row_ids = lax.broadcasted_iota(jnp.int32, (resp_slots, resp_slots), 0)
    col_ids = lax.broadcasted_iota(jnp.int32, (resp_slots, resp_slots), 1)
    causal = col_ids <= row_ids
    query_parts, key_parts, value_parts, far_key_parts, far_value_parts = ([], [], [], [], [])
    for kv_head in range(KV_HEADS):
        query_block = queries[:, :, kv_head]
        grad_block = grads[:, :, kv_head]
        key_far = far_keys[:, kv_head]
        value_far = far_values[:, kv_head]
        key_near = near_keys[:, :, kv_head]
        value_near = near_values[:, :, kv_head]
        far_scores = jnp.einsum('rtgd,kd->rtgk', query_block, key_far) * score_scale
        near_scores = jnp.einsum('rtgd,rud->rtgu', query_block, key_near) * score_scale
        near_scores = jnp.where(causal[None, :, None, :], near_scores, -jnp.inf)
        log_total = jnp.logaddexp(jax.nn.logsumexp(far_scores, axis=-1), jax.nn.logsumexp(near_scores, axis=-1))
        far_probs = jnp.exp(far_scores - log_total[..., None])
        near_probs = jnp.exp(near_scores - log_total[..., None])
        far_dprobs = jnp.einsum('rtgd,kd->rtgk', grad_block, value_far)
        near_dprobs = jnp.einsum('rtgd,rud->rtgu', grad_block, value_near)
        delta = lax.optimization_barrier(jnp.sum(far_probs * far_dprobs, axis=-1)) + lax.optimization_barrier(jnp.sum(near_probs * near_dprobs, axis=-1))
        far_slopes = low_copy(far_probs * (far_dprobs - delta[..., None]) * score_scale)
        near_slopes = low_copy(near_probs * (near_dprobs - delta[..., None]) * score_scale)
        far_low = low_copy(far_probs)
        near_low = low_copy(near_probs)
        query_parts.append(jnp.einsum('rtgk,kd->rtgd', far_slopes, key_far) + jnp.einsum('rtgu,rud->rtgd', near_slopes, key_near))
        key_parts.append(jnp.einsum('rtgu,rtgd->rud', near_slopes, query_block))
        value_parts.append(jnp.einsum('rtgu,rtgd->rud', near_low, grad_block))
        far_key_parts.append(jnp.einsum('rtgk,rtgd->kd', far_slopes, query_block))
        far_value_parts.append(jnp.einsum('rtgk,rtgd->kd', far_low, grad_block))
    grad_queries = jnp.stack(query_parts, 2).reshape(responses, resp_slots, HEADS * HEAD_DIM)
    grad_keys = jnp.stack(key_parts, 2).reshape(responses, resp_slots, KV_HEADS * HEAD_DIM)
    grad_values = jnp.stack(value_parts, 2).reshape(responses, resp_slots, KV_HEADS * HEAD_DIM)
    grad_far_keys = jnp.stack(far_key_parts, 1).reshape(-1, KV_HEADS * HEAD_DIM)
    grad_far_values = jnp.stack(far_value_parts, 1).reshape(-1, KV_HEADS * HEAD_DIM)
    return (grad_queries.astype(jnp.bfloat16), grad_keys.astype(jnp.bfloat16), grad_values.astype(jnp.bfloat16), grad_far_keys.astype(jnp.bfloat16), grad_far_values.astype(jnp.bfloat16))

def reference(prefix_keys, prefix_values, resp_queries, resp_keys, resp_values, grad_out, lengths, buckets):
    reward = buckets.astype(jnp.float32) / (BUCKETS - 1)
    reward_mean = lax.optimization_barrier(jnp.sum(reward, axis=1)) / RESPONSES
    token_total = jnp.sum(lengths.astype(jnp.float32))
    every_slot = PROMPTS * RESPONSES * RESP
    factor = (reward - reward_mean[:, None]) * every_slot / token_total
    position = lax.broadcasted_iota(jnp.int32, (PROMPTS, RESPONSES, RESP), 2)
    weight = jnp.where(position < lengths[:, :, None], factor[:, :, None], 0.0)
    weighted = (grad_out.astype(jnp.float32) * weight[..., None]).astype(jnp.bfloat16)
    results = lax.map(prompt_backward, (weighted, resp_queries, resp_keys, resp_values, prefix_keys, prefix_values))
    return (results[0], results[1], results[2], results[3], results[4])
```

```python
import functools
import math

import jax
import jax.numpy as jnp
from jax import lax
from jax.experimental import pallas as pl
from jax.experimental.pallas import tpu as pltpu
from jax.sharding import PartitionSpec as P

HEADS = 32
KV_HEADS = 4
HEAD_DIM = 128
BUCKETS = 5
GROUP_HEADS = HEADS // KV_HEADS
LANES = GROUP_HEADS * HEAD_DIM
SCALE = 1.0 / math.sqrt(HEAD_DIM)
EXP2_SCALE = SCALE * math.log2(math.e)
VMEM = 48 * 1024 * 1024


def dot_nt(a, b):
    return lax.dot_general(a, b, (((1,), (1,)), ((), ())), preferred_element_type=jnp.float32)


def dot_nn(a, b):
    return lax.dot_general(a, b, (((1,), (0,)), ((), ())), preferred_element_type=jnp.float32)


def dot_tn(a, b):
    return lax.dot_general(a, b, (((0,), (0,)), ((), ())), preferred_element_type=jnp.float32)


def stacked(ref):
    return jnp.concatenate(
        [ref[:, h * HEAD_DIM : (h + 1) * HEAD_DIM] for h in range(GROUP_HEADS)], axis=0
    )


def stacked_masked(ref, length):
    slots = ref.shape[0]
    rows = lax.broadcasted_iota(jnp.int32, (slots, HEAD_DIM), 0)
    mask = jnp.where(rows < length, 1.0, 0.0).astype(jnp.bfloat16)
    return jnp.concatenate(
        [ref[:, h * HEAD_DIM : (h + 1) * HEAD_DIM] * mask for h in range(GROUP_HEADS)], axis=0
    )


def causal(scores):
    slots = scores.shape[0]
    keys = lax.broadcasted_iota(jnp.int32, scores.shape, 0)
    queries = lax.broadcasted_iota(jnp.int32, scores.shape, 1) % slots
    return jnp.where(keys <= queries, scores, -jnp.inf)


def near_stats_kernel(len_ref, q_ref, g_ref, k_ref, v_ref, stats_ref):
    length = len_ref[0, 0]
    queries = stacked(q_ref)
    grads = stacked_masked(g_ref, length)
    scores = causal(dot_nt(k_ref[...], queries) * EXP2_SCALE)
    dprobs = dot_nt(v_ref[...], grads)
    top = jnp.max(scores, axis=0, keepdims=True)
    terms = jnp.exp2(scores - top)
    total = jnp.sum(terms, axis=0, keepdims=True)
    delta = jnp.sum(terms * dprobs, axis=0, keepdims=True)
    stats_ref[0, 0:1] = top
    stats_ref[0, 1:2] = total
    stats_ref[0, 2:3] = delta


def far_kernel(
    len_ref, bucket_ref, q_ref, g_ref, k_ref, v_ref, extra_ref, stats_ref,
    part_ref, slopes_ref, out_stats_ref, probs_ref,
):
    kv = pl.program_id(0)
    length = len_ref[0, 0]
    queries = stacked(q_ref)
    grads = stacked_masked(g_ref, length)
    keys, values = k_ref[...], v_ref[...]
    chunk = 256
    for c in range(0, LANES, chunk):
        cols = slice(c, c + chunk)
        scores = dot_nt(keys, queries[cols]) * EXP2_SCALE
        dprobs = dot_nt(values, grads[cols])
        near_top = stats_ref[0, 0:1, cols]
        top = jnp.maximum(jnp.max(scores, axis=0, keepdims=True), near_top)
        near_shift = jnp.exp2(near_top - top)
        terms = jnp.exp2(scores - top)
        total = jnp.sum(terms, axis=0, keepdims=True) + stats_ref[0, 1:2, cols] * near_shift
        delta = jnp.sum(terms * dprobs, axis=0, keepdims=True)
        delta = delta + stats_ref[0, 2:3, cols] * near_shift
        inverse = 1.0 / total
        delta = delta * inverse
        probs = terms * inverse
        probs_ref[:, cols] = probs.astype(jnp.bfloat16)
        slopes_ref[0, :, cols] = (probs * (dprobs - delta)).astype(jnp.bfloat16)
        out_stats_ref[0, 0:1, cols] = top
        out_stats_ref[0, 1:2, cols] = inverse
        out_stats_ref[0, 2:3, cols] = delta
    members = 16
    rows = extra_ref.shape[0]
    reward_sum = jnp.sum(extra_ref[...].astype(jnp.float32), axis=0, keepdims=True) * (
        members / rows / (BUCKETS - 1)
    )
    reward = bucket_ref[0, 0].astype(jnp.float32) / (BUCKETS - 1)
    advantage = reward - reward_sum / members
    key_part = dot_nn(slopes_ref[0], queries) * (advantage * SCALE)
    value_part = dot_nn(probs_ref[...], grads) * advantage
    at = pl.multiple_of(kv * HEAD_DIM, HEAD_DIM)
    part_ref[:, pl.ds(at, HEAD_DIM)] = key_part.astype(jnp.bfloat16)
    at = pl.multiple_of((kv + KV_HEADS) * HEAD_DIM, HEAD_DIM)
    part_ref[:, pl.ds(at, HEAD_DIM)] = value_part.astype(jnp.bfloat16)

    @pl.when(kv == 0)
    def _():
        part_ref[:, 2 * KV_HEADS * HEAD_DIM :] = jnp.zeros(
            (part_ref.shape[0], HEAD_DIM), jnp.bfloat16
        )


def own_kernel(
    len_ref, q_ref, g_ref, k_ref, v_ref, far_k_ref, slopes_ref, stats_ref,
    gq_ref, gk_ref, gv_ref,
):
    length = len_ref[0, 0]
    queries = stacked(q_ref)
    grads = stacked_masked(g_ref, length)
    top, inverse, delta = stats_ref[0, 0:1], stats_ref[0, 1:2], stats_ref[0, 2:3]
    scores = causal(dot_nt(k_ref[...], queries) * EXP2_SCALE)
    dprobs = dot_nt(v_ref[...], grads)
    probs = jnp.exp2(scores - top) * inverse
    slopes = (probs * (dprobs - delta)).astype(jnp.bfloat16)
    gk_ref[...] = dot_nn(slopes, queries)
    gv_ref[...] = dot_nn(probs.astype(jnp.bfloat16), grads)
    gq = dot_tn(far_k_ref[...], slopes_ref[0]) + dot_tn(k_ref[...], slopes)
    slots = q_ref.shape[0]
    for h in range(GROUP_HEADS):
        gq_ref[:, h * HEAD_DIM : (h + 1) * HEAD_DIM] = gq[:, h * slots : (h + 1) * slots].T.astype(
            jnp.bfloat16
        )


def finish_kernel(
    bucket_ref, extra_ref, recv_ref, gq_in, gk_in, gv_in,
    gq_ref, gk_ref, gv_ref, far_k_ref, far_v_ref,
):
    members = recv_ref.shape[0]
    rows = extra_ref.shape[0]
    width = KV_HEADS * HEAD_DIM
    reward_sum = jnp.sum(extra_ref[...].astype(jnp.float32), axis=0, keepdims=True) * (
        members / rows / (BUCKETS - 1)
    )
    reward = bucket_ref[0, 0].astype(jnp.float32) / (BUCKETS - 1)
    advantage = (reward - reward_sum / members)[:, 0:1]
    lengths = jnp.sum(recv_ref[:, 0:1, 2 * width :].astype(jnp.float32), axis=0)
    token_total = lengths[:, 0:1] * 256.0 + lengths[:, 64:65]
    every_slot = 16 * 16 * gq_ref.shape[0]
    norm = every_slot / token_total
    factor = advantage * norm
    gq_ref[...] = (gq_in[...].astype(jnp.float32) * (factor * SCALE)).astype(jnp.bfloat16)

    @pl.when(pl.program_id(0) == 0)
    def _():
        gk_ref[...] = (gk_in[...] * (factor * SCALE)).astype(jnp.bfloat16)
        gv_ref[...] = (gv_in[...] * factor).astype(jnp.bfloat16)
        sums = jnp.sum(recv_ref[:, :, : 2 * width].astype(jnp.float32), axis=0) * norm
        far_k_ref[...] = sums[:, :width].astype(jnp.bfloat16)
        far_v_ref[...] = sums[:, width:].astype(jnp.bfloat16)


def smem():
    return pl.BlockSpec(memory_space=pltpu.SMEM)


def params():
    return pltpu.CompilerParams(vmem_limit_bytes=VMEM, dimension_semantics=("arbitrary",))


def cost(flops, nbytes):
    return pl.CostEstimate(flops=flops, bytes_accessed=nbytes, transcendentals=0)


def head_block(rows, shift=0, width=HEAD_DIM):
    return pl.BlockSpec((rows, width), lambda i: (0, i + shift))


def whole(shape):
    return pl.BlockSpec(shape, lambda i: (0,) * len(shape))


def per_head(shape):
    return pl.BlockSpec((1,) + shape, lambda i: (i,) + (0,) * len(shape))


def body(
    prefix_keys, prefix_values, resp_queries, resp_keys, resp_values, grad_out, lengths, buckets
):
    slots = resp_queries.shape[2]
    own_rows = prefix_keys.shape[1]
    members = lax.axis_size("group")
    rows = own_rows * members
    width = KV_HEADS * HEAD_DIM
    q, g = resp_queries[0, 0], grad_out[0, 0]
    kn, vn = resp_keys[0, 0], resp_values[0, 0]
    f32, bf16 = jnp.float32, jnp.bfloat16

    extra = jnp.broadcast_to(buckets.astype(bf16), (own_rows, HEAD_DIM))
    send = jnp.concatenate([prefix_keys[0], prefix_values[0], extra], axis=1)
    send = jnp.broadcast_to(send[None], (members,) + send.shape)
    gathered = lax.all_to_all(send, "group", 0, 0, tiled=True).reshape(rows, -1)

    tokens = jnp.broadcast_to(lengths.astype(f32), (8, HEAD_DIM))
    dp = lax.axis_size("dp")
    step = 1
    while step < dp:
        tokens = tokens + lax.ppermute(tokens, "dp", [(i, i ^ step) for i in range(dp)])
        step *= 2

    near_stats = pl.pallas_call(
        near_stats_kernel,
        grid=(KV_HEADS,),
        in_specs=[smem(), head_block(slots, 0, LANES), head_block(slots, 0, LANES),
                  head_block(slots), head_block(slots)],
        out_specs=per_head((8, LANES)),
        out_shape=jax.ShapeDtypeStruct((KV_HEADS, 8, LANES), f32),
        compiler_params=params(),
        cost_estimate=cost(2 * 2 * 4096 * 128 * 128, 3 << 20),
    )(lengths, q, g, kn, vn)

    part, slopes, stats = pl.pallas_call(
        far_kernel,
        grid=(KV_HEADS,),
        in_specs=[smem(), smem(), head_block(slots, 0, LANES), head_block(slots, 0, LANES),
                  head_block(rows), head_block(rows, KV_HEADS),
                  pl.BlockSpec((rows, HEAD_DIM), lambda i: (0, 2 * KV_HEADS)),
                  per_head((8, LANES))],
        out_specs=[whole((rows, 2 * width + HEAD_DIM)), per_head((rows, LANES)),
                   per_head((8, LANES))],
        out_shape=[jax.ShapeDtypeStruct((rows, 2 * width + HEAD_DIM), bf16),
                   jax.ShapeDtypeStruct((KV_HEADS, rows, LANES), bf16),
                   jax.ShapeDtypeStruct((KV_HEADS, 8, LANES), f32)],
        scratch_shapes=[pltpu.VMEM((rows, LANES), bf16)],
        compiler_params=params(),
        cost_estimate=cost(4 * 2 * 4096 * 384 * 128, 8 << 20),
    )(lengths, buckets, q, g, gathered, gathered, gathered, near_stats)

    high = jnp.floor(tokens[0, 0] * (1.0 / 256.0))
    low = tokens[0, 0] - high * 256.0
    lane = lax.broadcasted_iota(jnp.int32, (rows, HEAD_DIM), 1)
    part = part.at[:, 2 * width :].set(jnp.where(lane < 64, high, low).astype(bf16))
    recv = lax.all_to_all(part, "group", 0, 0, tiled=True).reshape(members, own_rows, -1)

    gq, gk, gv = pl.pallas_call(
        own_kernel,
        grid=(KV_HEADS,),
        in_specs=[smem(), head_block(slots, 0, LANES), head_block(slots, 0, LANES),
                  head_block(slots), head_block(slots), head_block(rows),
                  per_head((rows, LANES)), per_head((8, LANES))],
        out_specs=[head_block(slots, 0, LANES), head_block(slots), head_block(slots)],
        out_shape=[jax.ShapeDtypeStruct((slots, HEADS * HEAD_DIM), bf16),
                   jax.ShapeDtypeStruct((slots, width), f32),
                   jax.ShapeDtypeStruct((slots, width), f32)],
        compiler_params=params(),
        cost_estimate=cost(3 * 2 * 4096 * 512 * 128, 8 << 20),
    )(lengths, q, g, kn, vn, gathered, slopes, stats)

    outs = pl.pallas_call(
        finish_kernel,
        grid=(KV_HEADS,),
        in_specs=[smem(), pl.BlockSpec((rows, HEAD_DIM), lambda i: (0, 2 * KV_HEADS)),
                  whole((members, own_rows, 2 * width + HEAD_DIM)),
                  head_block(slots, 0, LANES), whole((slots, width)), whole((slots, width))],
        out_specs=[head_block(slots, 0, LANES), whole((slots, width)), whole((slots, width)),
                   whole((own_rows, width)), whole((own_rows, width))],
        out_shape=[jax.ShapeDtypeStruct((slots, HEADS * HEAD_DIM), bf16),
                   jax.ShapeDtypeStruct((slots, width), bf16),
                   jax.ShapeDtypeStruct((slots, width), bf16),
                   jax.ShapeDtypeStruct((own_rows, width), bf16),
                   jax.ShapeDtypeStruct((own_rows, width), bf16)],
        compiler_params=params(),
    )(buckets, gathered, recv, gq, gk, gv)
    gq, gk, gv, far_k, far_v = outs
    return gq[None, None], gk[None, None], gv[None, None], far_k[None], far_v[None]


def solution(mesh):
    in_specs = (
        P("dp", "group", None),
        P("dp", "group", None),
        P("dp", "group", None, None),
        P("dp", "group", None, None),
        P("dp", "group", None, None),
        P("dp", "group", None, None),
        P("dp", "group"),
        P("dp", "group"),
    )
    out_specs = (
        P("dp", "group", None, None),
        P("dp", "group", None, None),
        P("dp", "group", None, None),
        P("dp", "group", None),
        P("dp", "group", None),
    )
    return jax.shard_map(body, mesh=mesh, in_specs=in_specs, out_specs=out_specs, check_vma=False)
```

```python
import functools
import math

import jax
import jax.numpy as jnp
from jax import lax
from jax.experimental import pallas as pl
from jax.experimental.pallas import tpu as pltpu
from jax.sharding import PartitionSpec as P

HEADS = 32
KV_HEADS = 4
HEAD_DIM = 128
BUCKETS = 5
GROUP_HEADS = HEADS // KV_HEADS
LANES = GROUP_HEADS * HEAD_DIM
SCALE = 1.0 / math.sqrt(HEAD_DIM)
EXP2_SCALE = SCALE * math.log2(math.e)
VMEM = 24 * 1024 * 1024
CORES = 2


def dot_nt(a, b):
    return lax.dot_general(a, b, (((1,), (1,)), ((), ())), preferred_element_type=jnp.float32)


def dot_nn(a, b):
    return lax.dot_general(a, b, (((1,), (0,)), ((), ())), preferred_element_type=jnp.float32)


def dot_tn(a, b):
    return lax.dot_general(a, b, (((0,), (0,)), ((), ())), preferred_element_type=jnp.float32)


def causal(scores):
    slots = scores.shape[0]
    keys = lax.broadcasted_iota(jnp.int32, scores.shape, 0)
    queries = lax.broadcasted_iota(jnp.int32, scores.shape, 1) % slots
    return jnp.where(keys <= queries, scores, -jnp.inf)


def metadata(bucket_ref, len_ref, shape):
    lanes = lax.broadcasted_iota(jnp.int32, shape, len(shape) - 1)
    values = jnp.where(lanes < HEAD_DIM // 2, bucket_ref[0, 0], len_ref[0, 0])
    return values.astype(jnp.float32).astype(jnp.bfloat16)


def wait_all(copies):
    for copy in copies:
        copy.start()
    for copy in copies:
        copy.wait()


def spread_kernel(bucket_ref, len_ref, k_ref, v_ref, out_ref, meta_ref, sems):
    members, rows, _ = out_ref.shape
    half = k_ref.shape[1] // CORES
    meta_ref[...] = metadata(bucket_ref, len_ref, meta_ref.shape)
    copies = []
    for m in range(members):
        cols = pl.ds((m % CORES) * half, half)
        copies += [
            pltpu.make_async_copy(k_ref.at[:, cols], out_ref.at[m, :, pl.ds(0, half)], sems.at[0]),
            pltpu.make_async_copy(v_ref.at[:, cols], out_ref.at[m, :, pl.ds(half, half)], sems.at[1]),
            pltpu.make_async_copy(meta_ref, out_ref.at[m, :, pl.ds(2 * half, HEAD_DIM)], sems.at[2]),
        ]
    wait_all(copies)


def swap_kernel(
    core_ref, bucket_ref, len_ref, q_ref, g_ref, k_ref, v_ref, out_ref, meta_ref, sems
):
    meta_ref[...] = metadata(bucket_ref, len_ref, meta_ref.shape)
    other = 1 - core_ref[0, 0]
    at, copies = 0, []
    for i, ref in enumerate((q_ref, g_ref, k_ref, v_ref)):
        half = ref.shape[1] // CORES
        cols = pl.ds(pl.multiple_of(other * half, half), half)
        copies.append(
            pltpu.make_async_copy(ref.at[:, cols], out_ref.at[:, pl.ds(at, half)], sems.at[i])
        )
        at += half
    copies.append(pltpu.make_async_copy(meta_ref, out_ref.at[:, pl.ds(at, HEAD_DIM)], sems.at[4]))
    wait_all(copies)


def near_kernel(
    core_ref, bucket_ref, len_ref, q_ref, g_ref, k_ref, v_ref, swap_ref,
    qs_ref, gs_ref, ks_ref, vs_ref, stats_ref,
):
    core = core_ref[0, 0]
    slots = q_ref.shape[0]
    heads = KV_HEADS // CORES
    wide = heads * LANES
    rows = lax.broadcasted_iota(jnp.int32, (slots, HEAD_DIM), 0).astype(jnp.float32)
    for r in range(CORES):
        if r == 0:
            length = len_ref[0, 0].astype(jnp.float32)
        else:
            at = 2 * wide + 2 * heads * HEAD_DIM + HEAD_DIM // 2
            length = swap_ref[0:1, at : at + HEAD_DIM // 2].astype(jnp.float32)[:, 0:1]
        mask = jnp.where(rows < length, 1.0, 0.0).astype(jnp.bfloat16)
        for h in range(heads):
            i = h * CORES + r
            q_parts, g_parts = [], []
            for n in range(GROUP_HEADS):
                at = h * LANES + n * HEAD_DIM
                if r == 0:
                    cols = pl.ds(pl.multiple_of(core * wide + at, HEAD_DIM), HEAD_DIM)
                    q, g = q_ref[:, cols], g_ref[:, cols]
                else:
                    q = swap_ref[:, at : at + HEAD_DIM]
                    g = swap_ref[:, wide + at : wide + at + HEAD_DIM]
                q_parts.append(q)
                g_parts.append(g * mask)
            queries = jnp.concatenate(q_parts, axis=0)
            grads = jnp.concatenate(g_parts, axis=0)
            if r == 0:
                cols = pl.ds(pl.multiple_of((core * heads + h) * HEAD_DIM, HEAD_DIM), HEAD_DIM)
                keys, values = k_ref[:, cols], v_ref[:, cols]
            else:
                at = 2 * wide + h * HEAD_DIM
                keys = swap_ref[:, at : at + HEAD_DIM]
                at += heads * HEAD_DIM
                values = swap_ref[:, at : at + HEAD_DIM]
            qs_ref[i], gs_ref[i], ks_ref[i], vs_ref[i] = queries, grads, keys, values
            scores = causal(dot_nt(keys, queries) * EXP2_SCALE)
            dprobs = dot_nt(values, grads)
            top = jnp.max(scores, axis=0, keepdims=True)
            terms = jnp.exp2(scores - top)
            stats_ref[i, 0:1] = top
            stats_ref[i, 1:2] = jnp.sum(terms, axis=0, keepdims=True)
            stats_ref[i, 2:3] = jnp.sum(terms * dprobs, axis=0, keepdims=True)


def advantages(bucket_ref, swap_meta, extra):
    rows = extra.shape[0]
    members = 16
    unit = 1.0 / (BUCKETS - 1)
    sums = jnp.sum(extra.astype(jnp.float32), axis=0, keepdims=True)[:, 0:1]
    mean = sums * (unit / rows)
    own = jnp.full((1, 1), bucket_ref[0, 0], jnp.int32).astype(jnp.float32) * unit - mean
    other = swap_meta.astype(jnp.float32)[:, 0:1] * unit - mean
    return own, other


def far_kernel(
    bucket_ref, meta_ref, qs_ref, gs_ref, near_ref, gathered_ref,
    part_ref, slopes_ref, stats_ref, probs_ref, send_ref, sems,
):
    heads = KV_HEADS // CORES
    width = heads * HEAD_DIM
    scale = advantages(bucket_ref, meta_ref[0:1], gathered_ref[:, 2 * width :])
    chunk = 256
    copies = []
    for h in range(heads):
        keys = gathered_ref[:, h * HEAD_DIM : (h + 1) * HEAD_DIM]
        values = gathered_ref[:, width + h * HEAD_DIM : width + (h + 1) * HEAD_DIM]
        key_part, value_part = 0.0, 0.0
        for r in range(CORES):
            i = h * CORES + r
            for c in range(0, LANES, chunk):
                cols = slice(c, c + chunk)
                scores = dot_nt(keys, qs_ref[i, cols]) * EXP2_SCALE
                dprobs = dot_nt(values, gs_ref[i, cols])
                near_top = near_ref[i, 0:1, cols]
                top = jnp.maximum(jnp.max(scores, axis=0, keepdims=True), near_top)
                shift = jnp.exp2(near_top - top)
                terms = jnp.exp2(scores - top)
                total = jnp.sum(terms, axis=0, keepdims=True) + near_ref[i, 1:2, cols] * shift
                delta = jnp.sum(terms * dprobs, axis=0, keepdims=True)
                delta = delta + near_ref[i, 2:3, cols] * shift
                inverse = 1.0 / total
                delta = delta * inverse
                probs = terms * inverse
                probs_ref[:, cols] = probs.astype(jnp.bfloat16)
                slopes_ref[i, :, cols] = (probs * (dprobs - delta)).astype(jnp.bfloat16)
                stats_ref[i, 0:1, cols] = top
                stats_ref[i, 1:2, cols] = inverse
                stats_ref[i, 2:3, cols] = delta
            key_part = key_part + dot_nn(slopes_ref[i], qs_ref[i]) * (scale[r] * SCALE)
            value_part = value_part + dot_nn(probs_ref[...], gs_ref[i]) * scale[r]
        for n, part in enumerate((key_part, value_part)):
            at = n * width + h * HEAD_DIM
            send_ref[:, at : at + HEAD_DIM] = part.astype(jnp.bfloat16)
            cols = pl.ds(at, HEAD_DIM)
            copy = pltpu.make_async_copy(
                send_ref.at[:, cols], part_ref.at[:, cols], sems.at[2 * h + n]
            )
            copy.start()
            copies.append(copy)
    for copy in copies:
        copy.wait()


def own_kernel(
    qs_ref, gs_ref, ks_ref, vs_ref, gathered_ref, slopes_ref, stats_ref, own_ref, swap_ref
):
    heads = KV_HEADS // CORES
    slots = ks_ref.shape[1]
    wide = heads * LANES
    for r in (1, 0):
        out_ref = own_ref if r == 0 else swap_ref
        for h in range(heads):
            i = h * CORES + r
            queries, grads = qs_ref[i], gs_ref[i]
            keys, values = ks_ref[i], vs_ref[i]
            top, inverse, delta = stats_ref[i, 0:1], stats_ref[i, 1:2], stats_ref[i, 2:3]
            scores = causal(dot_nt(keys, queries) * EXP2_SCALE)
            dprobs = dot_nt(values, grads)
            probs = jnp.exp2(scores - top) * inverse
            slopes = (probs * (dprobs - delta)).astype(jnp.bfloat16)
            far_keys = gathered_ref[:, h * HEAD_DIM : (h + 1) * HEAD_DIM]
            gq = dot_tn(far_keys, slopes_ref[i]) + dot_tn(keys, slopes)
            for n in range(GROUP_HEADS):
                at = h * LANES + n * HEAD_DIM
                out_ref[:, at : at + HEAD_DIM] = gq[:, n * slots : (n + 1) * slots].T.astype(
                    jnp.bfloat16
                )
            at = wide + h * HEAD_DIM
            out_ref[:, at : at + HEAD_DIM] = dot_nn(slopes, queries).astype(jnp.bfloat16)
            at += heads * HEAD_DIM
            out_ref[:, at : at + HEAD_DIM] = dot_nn(
                probs.astype(jnp.bfloat16), grads
            ).astype(jnp.bfloat16)


def finish_kernel(
    core_ref, bucket_ref, tokens_ref, meta_ref, gathered_ref, recv_ref, own_ref, swap_ref,
    gq_ref, gk_ref, gv_ref, far_k_ref, far_v_ref,
):
    core = core_ref[0, 0]
    members, own_rows, both = recv_ref.shape
    width = both // 2
    slots = own_ref.shape[0]
    wide = gq_ref.shape[1] // CORES
    advantage, _ = advantages(bucket_ref, meta_ref[0:1], gathered_ref[:, 2 * width :])
    token_total = tokens_ref[0:1, HEAD_DIM // 2 : HEAD_DIM // 2 + 1]
    norm = (16 * 16 * slots) / token_total
    factor = advantage * norm
    for ref, at_core in ((own_ref, core), (swap_ref, 1 - core)):
        cols = pl.ds(pl.multiple_of(at_core * wide, wide), wide)
        gq_ref[:, cols] = (ref[:, :wide].astype(jnp.float32) * (factor * SCALE)).astype(
            jnp.bfloat16
        )
        cols = pl.ds(pl.multiple_of(at_core * width, width), width)
        gk_ref[:, cols] = (ref[:, wide : wide + width].astype(jnp.float32) * (factor * SCALE)).astype(
            jnp.bfloat16
        )
        gv_ref[:, cols] = (ref[:, wide + width :].astype(jnp.float32) * factor).astype(jnp.bfloat16)
    for c in range(CORES):
        total = recv_ref[c].astype(jnp.float32)
        for m in range(c + CORES, members, CORES):
            total = total + recv_ref[m].astype(jnp.float32)
        total = total * norm
        far_k_ref[:, c * width : (c + 1) * width] = total[:, :width].astype(jnp.bfloat16)
        far_v_ref[:, c * width : (c + 1) * width] = total[:, width:].astype(jnp.bfloat16)


def smem():
    return pl.BlockSpec(memory_space=pltpu.SMEM)


def vmem():
    return pl.BlockSpec(memory_space=pltpu.VMEM)


def anywhere():
    return pl.BlockSpec(memory_space=pl.ANY)


def near_memory(x):
    return pltpu.with_memory_space_constraint(x, pltpu.VMEM)


def far_memory(x):
    return pltpu.with_memory_space_constraint(x, pltpu.HBM)


def call(kernel, in_specs, out_specs, out_shape, flops, nbytes, scratch=()):
    return pl.pallas_call(
        kernel,
        in_specs=in_specs,
        out_specs=out_specs,
        out_shape=out_shape,
        scratch_shapes=list(scratch),
        compiler_params=pltpu.CompilerParams(vmem_limit_bytes=VMEM),
        cost_estimate=pl.CostEstimate(flops=flops, bytes_accessed=nbytes, transcendentals=0),
    )


def body(
    prefix_keys, prefix_values, resp_queries, resp_keys, resp_values, grad_out, lengths, buckets
):
    slots = resp_queries.shape[2]
    own_rows = prefix_keys.shape[1]
    members = lax.axis_size("group")
    rows = own_rows * members
    heads = KV_HEADS // CORES
    width = heads * HEAD_DIM
    wide = heads * LANES
    jobs = heads * CORES
    q, g = resp_queries[0, 0], grad_out[0, 0]
    kn, vn = resp_keys[0, 0], resp_values[0, 0]
    f32, bf16 = jnp.float32, jnp.bfloat16
    core = jnp.full((1, 1), lax.axis_index("group") % CORES, jnp.int32)
    pairs = [(i, i ^ 1) for i in range(members)]

    spread = call(
        spread_kernel,
        [smem(), smem(), anywhere(), anywhere()],
        anywhere(),
        pltpu.HBM((members, own_rows, 2 * width + HEAD_DIM), bf16),
        0, 1 << 20,
        [pltpu.VMEM((own_rows, HEAD_DIM), bf16), pltpu.SemaphoreType.DMA((3,))],
    )(buckets, lengths, far_memory(prefix_keys[0]), far_memory(prefix_values[0]))
    gathered3 = lax.all_to_all(spread, "group", 0, 0, tiled=True)
    gathered = gathered3.reshape(rows, -1)

    swap = call(
        swap_kernel,
        [smem(), smem(), smem(), anywhere(), anywhere(), anywhere(), anywhere()],
        anywhere(),
        pltpu.HBM((slots, 2 * wide + 2 * width + HEAD_DIM), bf16),
        0, 3 << 20,
        [pltpu.VMEM((slots, HEAD_DIM), bf16), pltpu.SemaphoreType.DMA((5,))],
    )(core, buckets, lengths, far_memory(q), far_memory(g), far_memory(kn), far_memory(vn))
    swapped = lax.ppermute(swap, "group", pairs)
    meta = swapped[:16, 2 * wide + 2 * width :]

    qs, gs, ks, vs, near = call(
        near_kernel,
        [smem(), smem(), smem()] + [vmem()] * 5,
        [vmem()] * 5,
        [pltpu.VMEM((jobs, LANES, HEAD_DIM), bf16), pltpu.VMEM((jobs, LANES, HEAD_DIM), bf16),
         pltpu.VMEM((jobs, slots, HEAD_DIM), bf16), pltpu.VMEM((jobs, slots, HEAD_DIM), bf16),
         pltpu.VMEM((jobs, 8, LANES), f32)],
        2 * 2 * 4096 * 128 * 128, 3 << 20,
    )(core, buckets, lengths, near_memory(q), near_memory(g), near_memory(kn), near_memory(vn),
      near_memory(swapped))

    tokens = jnp.sum(gathered3[:, :8, 2 * width :].astype(f32), axis=0)

    part, slopes, stats = call(
        far_kernel,
        [smem()] + [vmem()] * 5,
        [anywhere(), vmem(), vmem()],
        [pltpu.HBM((rows, 2 * width), bf16), pltpu.VMEM((jobs, rows, LANES), bf16),
         pltpu.VMEM((jobs, 8, LANES), f32)],
        4 * 2 * 4096 * 384 * 128, 8 << 20,
        [pltpu.VMEM((rows, LANES), bf16), pltpu.VMEM((rows, 2 * width), bf16),
         pltpu.SemaphoreType.DMA((4,))],
    )(buckets, near_memory(meta), near_memory(qs), near_memory(gs), near_memory(near),
      near_memory(gathered))

    dp = lax.axis_size("dp")
    for step in (8, 1, 2, 4):
        tokens = tokens + lax.ppermute(tokens, "dp", [(i, i ^ step) for i in range(dp)])

    recv = lax.all_to_all(part.reshape(members, own_rows, -1), "group", 0, 0, tiled=True)

    own, swap_out = call(
        own_kernel,
        [vmem()] * 7,
        [vmem(), vmem()],
        [pltpu.VMEM((slots, wide + 2 * width), bf16), pltpu.HBM((slots, wide + 2 * width), bf16)],
        3 * 2 * 4096 * 512 * 128, 8 << 20,
    )(near_memory(qs), near_memory(gs), near_memory(ks), near_memory(vs), near_memory(gathered),
      near_memory(slopes), near_memory(stats))
    swap_in = lax.ppermute(swap_out, "group", pairs)

    outs = call(
        finish_kernel,
        [smem(), smem()] + [vmem()] * 6,
        [vmem()] * 5,
        [jax.ShapeDtypeStruct((slots, HEADS * HEAD_DIM), bf16),
         jax.ShapeDtypeStruct((slots, CORES * width), bf16),
         jax.ShapeDtypeStruct((slots, CORES * width), bf16),
         jax.ShapeDtypeStruct((own_rows, CORES * width), bf16),
         jax.ShapeDtypeStruct((own_rows, CORES * width), bf16)],
        0, 4 << 20,
    )(core, buckets, near_memory(tokens), near_memory(meta), near_memory(gathered),
      near_memory(recv), near_memory(own), near_memory(swap_in))
    gq, gk, gv, far_k, far_v = outs
    return gq[None, None], gk[None, None], gv[None, None], far_k[None], far_v[None]


def solution(mesh):
    in_specs = (
        P("dp", "group", None),
        P("dp", "group", None),
        P("dp", "group", None, None),
        P("dp", "group", None, None),
        P("dp", "group", None, None),
        P("dp", "group", None, None),
        P("dp", "group"),
        P("dp", "group"),
    )
    out_specs = (
        P("dp", "group", None, None),
        P("dp", "group", None, None),
        P("dp", "group", None, None),
        P("dp", "group", None),
        P("dp", "group", None),
    )
    return jax.shard_map(body, mesh=mesh, in_specs=in_specs, out_specs=out_specs, check_vma=False)
```

```python
import functools
import math

import jax
import jax.numpy as jnp
from jax import lax
from jax.experimental import pallas as pl
from jax.experimental.pallas import tpu as pltpu
from jax.sharding import PartitionSpec as P

HEADS = 32
KV_HEADS = 4
HEAD_DIM = 128
BUCKETS = 5
GROUP_HEADS = HEADS // KV_HEADS
LANES = GROUP_HEADS * HEAD_DIM
SCALE = 1.0 / math.sqrt(HEAD_DIM)
EXP2_SCALE = SCALE * math.log2(math.e)
VMEM = 16 * 1024 * 1024
CORES = 2


def dot_nt(a, b):
    return lax.dot_general(a, b, (((1,), (1,)), ((), ())), preferred_element_type=jnp.float32)


def dot_nn(a, b):
    return lax.dot_general(a, b, (((1,), (0,)), ((), ())), preferred_element_type=jnp.float32)


def dot_tn(a, b):
    return lax.dot_general(a, b, (((0,), (0,)), ((), ())), preferred_element_type=jnp.float32)


def causal(scores):
    slots = scores.shape[0]
    keys = lax.broadcasted_iota(jnp.int32, scores.shape, 0)
    queries = lax.broadcasted_iota(jnp.int32, scores.shape, 1) % slots
    return jnp.where(keys <= queries, scores, -jnp.inf)


def spread_kernel(k_ref, v_ref, bucket_ref, len_ref, out_ref, send_ref, in_sems, sems):
    half = k_ref.shape[1] // CORES
    loads = []
    for c in range(CORES):
        for n, ref in enumerate((k_ref, v_ref)):
            loads.append(
                pltpu.make_async_copy(
                    ref.at[:, pl.ds(c * half, half)],
                    send_ref.at[c, :, pl.ds(n * half, half)],
                    in_sems.at[2 * c + n],
                )
            )
            loads[-1].start()
    lanes = lax.broadcasted_iota(jnp.int32, (k_ref.shape[0], HEAD_DIM), 1)
    payload = jnp.where(lanes < HEAD_DIM // 2, bucket_ref[0, 0], len_ref[0, 0])
    copies = []
    for c in range(CORES):
        send_ref[c, :, 2 * half :] = payload.astype(jnp.float32).astype(jnp.bfloat16)
        loads[2 * c].wait()
        loads[2 * c + 1].wait()
        for m in range(c, out_ref.shape[0], CORES):
            copies.append(pltpu.make_async_copy(send_ref.at[c], out_ref.at[m], sems.at[m]))
            copies[-1].start()
    for copy in copies:
        copy.wait()


def swap_kernel(core_ref, q_ref, g_ref, k_ref, v_ref, _after, q_0, q_1, g_0, g_1, kv_ref, sems):
    other = 1 - core_ref[0, 0]
    copies = []
    for ref, outs in ((q_ref, (q_0, q_1)), (g_ref, (g_0, g_1))):
        for h, out in enumerate(outs):
            at = pl.multiple_of((other * len(outs) + h) * LANES, LANES)
            copies.append((ref.at[:, pl.ds(at, LANES)], out))
    half = k_ref.shape[1] // CORES
    cols = pl.ds(pl.multiple_of(other * half, half), half)
    copies.append((k_ref.at[:, cols], kv_ref.at[:, pl.ds(0, half)]))
    copies.append((v_ref.at[:, cols], kv_ref.at[:, pl.ds(half, half)]))
    copies = [pltpu.make_async_copy(a, b, sems.at[n]) for n, (a, b) in enumerate(copies)]
    for copy in copies:
        copy.start()
    for copy in copies:
        copy.wait()


def near_kernel(
    core_ref, len_ref, own_q, own_g, own_k, own_v, q_0, q_1, g_0, g_1, kv_ref, meta_ref,
    qs_ref, gs_ref, ks_ref, vs_ref, stats_ref, held_ref, sems,
):
    core = core_ref[0, 0]
    slots = own_q.shape[0]
    at, copies = 0, []
    for i, ref in enumerate((own_q, own_g, own_k, own_v)):
        half = ref.shape[1] // CORES
        cols = pl.ds(pl.multiple_of(core * half, half), half)
        to = held_ref.at[:, pl.ds(at, half)]
        copies.append(pltpu.make_async_copy(ref.at[:, cols], to, sems.at[i]))
        copies[-1].start()
        at += half
    heads = KV_HEADS // CORES
    wide = heads * LANES
    rows = lax.broadcasted_iota(jnp.int32, (slots, HEAD_DIM), 0).astype(jnp.float32)

    for r in (1, 0):
        if r == 0:
            length = len_ref[0, 0].astype(jnp.float32)
            for copy in copies:
                copy.wait()
        else:
            length = meta_ref[0:1, 64:65]
        mask = jnp.where(rows < length, 1.0, 0.0).astype(jnp.bfloat16)
        for h in range(heads):
            i = h * CORES + r
            if r == 0:
                refs = (held_ref, held_ref, held_ref, held_ref)
                starts = (h * LANES, wide + h * LANES, 2 * wide + h * HEAD_DIM)
                starts += (2 * wide + (heads + h) * HEAD_DIM,)
            else:
                refs = ((q_0, q_1)[h], (g_0, g_1)[h], kv_ref, kv_ref)
                starts = (0, 0, h * HEAD_DIM, (heads + h) * HEAD_DIM)

            def piece(n, at=0, refs=refs, starts=starts):
                return refs[n][:, starts[n] + at : starts[n] + at + HEAD_DIM]

            spots = range(0, LANES, HEAD_DIM)
            queries = jnp.concatenate([piece(0, at) for at in spots], axis=0)
            grads = jnp.concatenate([piece(1, at) * mask for at in spots], axis=0)
            keys, values = piece(2), piece(3)
            qs_ref[i], gs_ref[i], ks_ref[i], vs_ref[i] = queries, grads, keys, values
            scores = causal(dot_nt(keys, queries) * EXP2_SCALE)
            dprobs = dot_nt(values, grads)
            top = jnp.max(scores, axis=0, keepdims=True)
            terms = jnp.exp2(scores - top)
            stats_ref[i, 0:1] = top
            stats_ref[i, 1:2] = jnp.sum(terms, axis=0, keepdims=True)
            stats_ref[i, 2:3] = jnp.sum(terms * dprobs, axis=0, keepdims=True)


def advantages(bucket_ref, swap_meta, extra):
    rows = extra.shape[0]
    members = 16
    unit = 1.0 / (BUCKETS - 1)
    sums = jnp.sum(extra.astype(jnp.float32), axis=0, keepdims=True)[:, 0:1]
    mean = sums * (unit / rows)
    own = jnp.full((1, 1), bucket_ref[0, 0], jnp.int32).astype(jnp.float32) * unit - mean
    other = swap_meta.astype(jnp.float32)[:, 0:1] * unit - mean
    return own, other


def far_kernel(
    h, bucket_ref, meta_ref, tokens_ref, near_ref, gathered_ref, _part, _qs, _gs, _ks, _vs,
    slopes_out, stats_out, part_ref, qs_ref, gs_ref, _ks_out, _vs_out,
    slopes_ref, stats_ref, probs_ref, send_ref, sems,
):
    heads = KV_HEADS // CORES
    width = heads * HEAD_DIM
    scale = advantages(bucket_ref, meta_ref[0:1], gathered_ref[:, 2 * width :])
    chunk = 256
    copies = []

    def send(n, value, at):
        send_ref[n] = value
        copy = pltpu.make_async_copy(
            send_ref.at[n], part_ref.at[:, pl.ds(at, HEAD_DIM)], sems.at[n]
        )
        copy.start()
        copies.append(copy)

    if tokens_ref is not None:
        tokens = jnp.broadcast_to(tokens_ref[0:1, HEAD_DIM // 2 : HEAD_DIM // 2 + 1], (1, HEAD_DIM))
        high = jnp.floor(tokens * (1.0 / 256.0))
        lanes = lax.broadcasted_iota(jnp.int32, tokens.shape, 1)
        tokens = jnp.where(lanes < HEAD_DIM // 2, high, tokens - high * 256.0)
        tokens = jnp.broadcast_to(tokens, send_ref.shape[1:])
        send(2, tokens.astype(jnp.bfloat16), 2 * width)
    keys = gathered_ref[:, h * HEAD_DIM : (h + 1) * HEAD_DIM]
    values = gathered_ref[:, width + h * HEAD_DIM : width + (h + 1) * HEAD_DIM]
    key_part, value_part = 0.0, 0.0
    for r in range(CORES):
        i = h * CORES + r
        for c in range(0, LANES, chunk):
            cols = slice(c, c + chunk)
            scores = dot_nt(keys, qs_ref[i, cols]) * EXP2_SCALE
            dprobs = dot_nt(values, gs_ref[i, cols])
            near_top = near_ref[i, 0:1, cols]
            top = jnp.maximum(jnp.max(scores, axis=0, keepdims=True), near_top)
            shift = jnp.exp2(near_top - top)
            terms = jnp.exp2(scores - top)
            total = jnp.sum(terms, axis=0, keepdims=True) + near_ref[i, 1:2, cols] * shift
            delta = jnp.sum(terms * dprobs, axis=0, keepdims=True)
            delta = delta + near_ref[i, 2:3, cols] * shift
            inverse = 1.0 / total
            delta = delta * inverse
            probs = terms * inverse
            probs_ref[:, cols] = probs.astype(jnp.bfloat16)
            slopes_ref[r, :, cols] = (probs * (dprobs - delta)).astype(jnp.bfloat16)
            stats_ref[r, 0:1, cols] = top
            stats_ref[r, 1:2, cols] = inverse
            stats_ref[r, 2:3, cols] = delta
        key_part = key_part + dot_nn(slopes_ref[r], qs_ref[i]) * (scale[r] * SCALE)
        value_part = value_part + dot_nn(probs_ref[...], gs_ref[i]) * scale[r]
        for n, (held, out) in enumerate(((slopes_ref, slopes_out), (stats_ref, stats_out))):
            copy = pltpu.make_async_copy(held.at[r], out.at[r], sems.at[3 + 2 * r + n])
            copy.start()
            copies.append(copy)
    send(0, key_part.astype(jnp.bfloat16), h * HEAD_DIM)
    send(1, value_part.astype(jnp.bfloat16), width + h * HEAD_DIM)
    for copy in copies:
        copy.wait()


def first_far_kernel(bucket_ref, meta_ref, near_ref, gathered_ref, qs, gs, ks, vs, *refs):
    far_kernel(
        0, bucket_ref, meta_ref, None, near_ref, gathered_ref, None, qs, gs, ks, vs, *refs
    )


def second_far_kernel(*refs):
    far_kernel(1, *refs)


def own_kernel(
    qs_ref, gs_ref, ks_ref, vs_ref, gathered_ref, slopes_0, stats_0, slopes_1, stats_1,
    own_out, swap_0, swap_1, swap_kv, own_ref, slopes_ref, stats_ref, sems, out_sems,
):
    heads = KV_HEADS // CORES
    slots = ks_ref.shape[1]
    loads = {}
    for r in (1, 0):
        for h, (slopes_in, stats_in) in enumerate(((slopes_0, stats_0), (slopes_1, stats_1))):
            i = h * CORES + r
            loads[i] = (
                pltpu.make_async_copy(slopes_in.at[r], slopes_ref.at[i], sems.at[0, i]),
                pltpu.make_async_copy(stats_in.at[r], stats_ref.at[i], sems.at[1, i]),
            )
            for load in loads[i]:
                load.start()
    copies = []
    for r in (1, 0):
        for h in range(heads):
            i = h * CORES + r
            if r:
                gq_ref, gq_at, kv_ref, kv_at = (swap_0, swap_1)[h], 0, swap_kv, 0
            else:
                gq_ref, gq_at, kv_ref, kv_at = own_ref, h * LANES, own_ref, heads * LANES
            queries, grads = qs_ref[i], gs_ref[i]
            keys, values = ks_ref[i], vs_ref[i]
            scores = causal(dot_nt(keys, queries) * EXP2_SCALE)
            dprobs = dot_nt(values, grads)
            loads[i][1].wait()
            top, inverse, delta = stats_ref[i, 0:1], stats_ref[i, 1:2], stats_ref[i, 2:3]
            probs = jnp.exp2(scores - top) * inverse
            slopes = (probs * (dprobs - delta)).astype(jnp.bfloat16)
            far_keys = gathered_ref[:, h * HEAD_DIM : (h + 1) * HEAD_DIM]
            loads[i][0].wait()
            gq = dot_tn(far_keys, slopes_ref[i]) + dot_tn(keys, slopes)
            for n in range(GROUP_HEADS):
                at = gq_at + n * HEAD_DIM
                gq_ref[:, at : at + HEAD_DIM] = gq[:, n * slots : (n + 1) * slots].T.astype(
                    jnp.bfloat16
                )
            at = kv_at + h * HEAD_DIM
            kv_ref[:, at : at + HEAD_DIM] = dot_nn(slopes, queries).astype(jnp.bfloat16)
            at += heads * HEAD_DIM
            kv_ref[:, at : at + HEAD_DIM] = dot_nn(probs.astype(jnp.bfloat16), grads).astype(
                jnp.bfloat16
            )
    copy = pltpu.make_async_copy(own_ref, own_out, out_sems.at[0])
    copy.start()
    copy.wait()


def finish_kernel(
    core_ref, bucket_ref, meta_ref, gathered_ref, recv_ref, own_in,
    swap_0, swap_1, swap_kv, gq_out, gk_ref, gv_ref, far_k_ref, far_v_ref,
    own_ref, gq_ref, in_sem, sems,
):
    load = pltpu.make_async_copy(own_in, own_ref, in_sem.at[0])
    load.start()
    core = core_ref[0, 0]
    members = recv_ref.shape[0]
    width = gk_ref.shape[1] // CORES
    slots = own_ref.shape[0]
    wide = gq_ref.shape[1] // CORES
    advantage, _ = advantages(bucket_ref, meta_ref[0:1], gathered_ref[:, 2 * width :])
    tokens = jnp.sum(recv_ref[:, 0:1, 2 * width :].astype(jnp.float32), axis=0)
    token_total = tokens[:, 0:1] * 256.0 + tokens[:, HEAD_DIM // 2 : HEAD_DIM // 2 + 1]
    norm = (16 * 16 * slots) / token_total
    factor = advantage * norm
    copies = []

    def put(ref, at, value, scale):
        cols = pl.ds(pl.multiple_of(at, HEAD_DIM), value.shape[1])
        ref[:, cols] = (value.astype(jnp.float32) * scale).astype(jnp.bfloat16)

    def put_queries(at, value):
        put(gq_ref, at, value, factor * SCALE)
        cols = pl.ds(pl.multiple_of(at, HEAD_DIM), value.shape[1])
        copy = pltpu.make_async_copy(
            gq_ref.at[:, cols], gq_out.at[:, cols], sems.at[len(copies)]
        )
        copy.start()
        copies.append(copy)

    other = 1 - core
    put_queries(other * wide, swap_0[...])
    put_queries(other * wide + LANES, swap_1[...])
    put(gk_ref, other * width, swap_kv[:, :width], factor * SCALE)
    put(gv_ref, other * width, swap_kv[:, width:], factor)
    for c in range(CORES):
        total = recv_ref[c, :, : 2 * width].astype(jnp.float32)
        for m in range(c + CORES, members, CORES):
            total = total + recv_ref[m, :, : 2 * width].astype(jnp.float32)
        total = total * norm
        far_k_ref[:, c * width : (c + 1) * width] = total[:, :width].astype(jnp.bfloat16)
        far_v_ref[:, c * width : (c + 1) * width] = total[:, width:].astype(jnp.bfloat16)
    load.wait()
    put_queries(core * wide, own_ref[:, :LANES])
    put_queries(core * wide + LANES, own_ref[:, LANES:wide])
    put(gk_ref, core * width, own_ref[:, wide : wide + width], factor * SCALE)
    put(gv_ref, core * width, own_ref[:, wide + width :], factor)
    for copy in copies:
        copy.wait()


def smem():
    return pl.BlockSpec(memory_space=pltpu.SMEM)


def vmem():
    return pl.BlockSpec(memory_space=pltpu.VMEM)


def anywhere():
    return pl.BlockSpec(memory_space=pl.ANY)


def near_memory(x):
    return pltpu.with_memory_space_constraint(x, pltpu.VMEM)


def far_memory(x):
    return pltpu.with_memory_space_constraint(x, pltpu.HBM)


def call(kernel, in_specs, out_specs, out_shape, flops, nbytes, scratch=(), aliases=None):
    return pl.pallas_call(
        kernel,
        in_specs=in_specs,
        out_specs=out_specs,
        out_shape=out_shape,
        scratch_shapes=list(scratch),
        input_output_aliases=aliases or {},
        compiler_params=pltpu.CompilerParams(vmem_limit_bytes=VMEM),
        cost_estimate=pl.CostEstimate(flops=flops, bytes_accessed=nbytes, transcendentals=0),
    )


def body(
    prefix_keys, prefix_values, resp_queries, resp_keys, resp_values, grad_out, lengths, buckets
):
    slots = resp_queries.shape[2]
    own_rows = prefix_keys.shape[1]
    members = lax.axis_size("group")
    rows = own_rows * members
    heads = KV_HEADS // CORES
    width = heads * HEAD_DIM
    wide = heads * LANES
    jobs = heads * CORES
    q, g = resp_queries[0, 0], grad_out[0, 0]
    kn, vn = resp_keys[0, 0], resp_values[0, 0]
    f32, bf16 = jnp.float32, jnp.bfloat16
    core = jnp.full((1, 1), lax.axis_index("group") % CORES, jnp.int32)
    pairs = [(i, i ^ 1) for i in range(members)]

    spread = call(
        spread_kernel,
        [anywhere(), anywhere(), smem(), smem()],
        anywhere(),
        pltpu.HBM((members, own_rows, 2 * width + HEAD_DIM), bf16),
        0, 1 << 20,
        [pltpu.VMEM((CORES, own_rows, 2 * width + HEAD_DIM), bf16),
         pltpu.SemaphoreType.DMA((4,)), pltpu.SemaphoreType.DMA((members,))],
    )(far_memory(prefix_keys[0]), far_memory(prefix_values[0]), buckets, lengths)
    gathered3 = lax.all_to_all(spread, "group", 0, 0, tiled=True)
    gathered = gathered3.reshape(rows, -1)

    lanes = lax.broadcasted_iota(jnp.int32, (8, HEAD_DIM), 1)
    meta = jnp.where(lanes < HEAD_DIM // 2, buckets, lengths).astype(f32)
    meta_in = lax.ppermute(meta, "group", pairs)
    swap = call(
        swap_kernel,
        [smem()] + [anywhere()] * 5,
        [vmem()] * 5,
        [pltpu.VMEM((slots, LANES), bf16)] * 4 + [pltpu.VMEM((slots, 2 * width), bf16)],
        0, 2 << 20,
        [pltpu.SemaphoreType.DMA((6,))],
    )(core, *(far_memory(x) for x in (q, g, kn, vn, spread)))
    swapped = [lax.ppermute(x, "group", pairs) for x in swap]

    qs, gs, ks, vs, near = call(
        near_kernel,
        [smem(), smem()] + [anywhere()] * 4 + [vmem()] * 6,
        [vmem()] * 5,
        [pltpu.VMEM((jobs, LANES, HEAD_DIM), bf16), pltpu.VMEM((jobs, LANES, HEAD_DIM), bf16),
         pltpu.VMEM((jobs, slots, HEAD_DIM), bf16), pltpu.VMEM((jobs, slots, HEAD_DIM), bf16),
         pltpu.VMEM((jobs, 8, LANES), f32)],
        2 * 2 * 4096 * 128 * 128, 3 << 20,
        [pltpu.VMEM((slots, 2 * wide + 2 * width), bf16), pltpu.SemaphoreType.DMA((4,))],
    )(core, lengths, *(far_memory(x) for x in (q, g, kn, vn)),
      *(near_memory(x) for x in (*swapped, meta_in)))

    dp = lax.axis_size("dp")
    payload, _ = lax.optimization_barrier((gathered3, near))
    tokens = jnp.sum(payload[:, :8, 2 * width :].astype(f32), axis=0)
    pairs_dp = [
        (d * members + i, (d ^ (i % dp)) * members + i) for d in range(dp) for i in range(members)
    ]
    tokens = lax.ppermute(tokens, ("dp", "group"), pairs_dp)

    part, saved = None, []
    for h in range(heads):
        kept = (qs, gs, ks, vs)
        args = [buckets, near_memory(meta_in)]
        args += [near_memory(tokens)] if h else []
        args += [near_memory(near), near_memory(gathered)]
        args += [far_memory(part)] if h else []
        aliases = {len(args) + n: 3 + n for n in range(len(kept))}
        if h:
            aliases[len(args) - 1] = 2
        outs = call(
            second_far_kernel if h else first_far_kernel,
            [smem()] + [vmem()] * (len(args) - 1 - h) + [anywhere()] * h + [vmem()] * 4,
            [anywhere()] * 3 + [vmem()] * 4,
            [pltpu.HBM((CORES, rows, LANES), bf16), pltpu.HBM((CORES, 8, LANES), f32),
             pltpu.HBM((rows, 2 * width + HEAD_DIM), bf16)]
            + [pltpu.VMEM(x.shape, x.dtype) for x in kept],
            2 * 2 * 4096 * 384 * 128, 4 << 20,
            [pltpu.VMEM((CORES, rows, LANES), bf16), pltpu.VMEM((CORES, 8, LANES), f32),
             pltpu.VMEM((rows, LANES), bf16), pltpu.VMEM((3, rows, HEAD_DIM), bf16),
             pltpu.SemaphoreType.DMA((7,))],
            aliases,
        )(*args, *(near_memory(x) for x in kept))
        slopes, stats, part, qs, gs, ks, vs = outs
        saved += [slopes, stats]

    recv = lax.all_to_all(part.reshape(members, own_rows, -1), "group", 0, 0, tiled=True)

    own, *swap_out = call(
        own_kernel,
        [vmem()] * 5 + [anywhere()] * 4,
        [anywhere()] + [vmem()] * 3,
        [pltpu.HBM((slots, wide + 2 * width), bf16), pltpu.VMEM((slots, LANES), bf16),
         pltpu.VMEM((slots, LANES), bf16), pltpu.VMEM((slots, 2 * width), bf16)],
        3 * 2 * 4096 * 512 * 128, 8 << 20,
        [pltpu.VMEM((slots, wide + 2 * width), bf16), pltpu.VMEM((jobs, rows, LANES), bf16),
         pltpu.VMEM((jobs, 8, LANES), f32), pltpu.SemaphoreType.DMA((2, jobs)),
         pltpu.SemaphoreType.DMA((1,))],
    )(*(near_memory(x) for x in (qs, gs, ks, vs, gathered)), *(far_memory(x) for x in saved))
    swap_in = [lax.ppermute(x, "group", pairs) for x in swap_out]

    outs = call(
        finish_kernel,
        [smem(), smem()] + [vmem()] * 3 + [anywhere()] + [vmem()] * 3,
        [anywhere()] + [vmem()] * 4,
        [pltpu.HBM((slots, HEADS * HEAD_DIM), bf16),
         jax.ShapeDtypeStruct((slots, CORES * width), bf16),
         jax.ShapeDtypeStruct((slots, CORES * width), bf16),
         jax.ShapeDtypeStruct((own_rows, CORES * width), bf16),
         jax.ShapeDtypeStruct((own_rows, CORES * width), bf16)],
        0, 4 << 20,
        [pltpu.VMEM((slots, wide + 2 * width), bf16), pltpu.VMEM((slots, HEADS * HEAD_DIM), bf16),
         pltpu.SemaphoreType.DMA((1,)), pltpu.SemaphoreType.DMA((4,))],
    )(core, buckets, *(near_memory(x) for x in (meta_in, gathered, recv)),
      far_memory(own), *(near_memory(x) for x in swap_in))
    gq, gk, gv, far_k, far_v = outs
    return gq[None, None], gk[None, None], gv[None, None], far_k[None], far_v[None]


def solution(mesh):
    in_specs = (
        P("dp", "group", None),
        P("dp", "group", None),
        P("dp", "group", None, None),
        P("dp", "group", None, None),
        P("dp", "group", None, None),
        P("dp", "group", None, None),
        P("dp", "group"),
        P("dp", "group"),
    )
    out_specs = (
        P("dp", "group", None, None),
        P("dp", "group", None, None),
        P("dp", "group", None, None),
        P("dp", "group", None),
        P("dp", "group", None),
    )
    return jax.shard_map(body, mesh=mesh, in_specs=in_specs, out_specs=out_specs, check_vma=False)
```

```python
import functools
import math

import jax
import jax.numpy as jnp
from jax import lax
from jax.experimental import pallas as pl
from jax.experimental.pallas import tpu as pltpu
from jax.sharding import PartitionSpec as P

HEADS = 32
KV_HEADS = 4
HEAD_DIM = 128
BUCKETS = 5
GROUP_HEADS = HEADS // KV_HEADS
LANES = GROUP_HEADS * HEAD_DIM
SCALE = 1.0 / math.sqrt(HEAD_DIM)
EXP2_SCALE = SCALE * math.log2(math.e)
VMEM = 16 * 1024 * 1024
CORES = 2


def dot_nt(a, b):
    return lax.dot_general(a, b, (((1,), (1,)), ((), ())), preferred_element_type=jnp.float32)


def dot_nn(a, b):
    return lax.dot_general(a, b, (((1,), (0,)), ((), ())), preferred_element_type=jnp.float32)


def dot_tn(a, b):
    return lax.dot_general(a, b, (((0,), (0,)), ((), ())), preferred_element_type=jnp.float32)


def causal(scores):
    slots = scores.shape[0]
    keys = lax.broadcasted_iota(jnp.int32, scores.shape, 0)
    queries = lax.broadcasted_iota(jnp.int32, scores.shape, 1) % slots
    return jnp.where(keys <= queries, scores, -jnp.inf)


def spread_kernel(
    k_ref, v_ref, bucket_in, len_in, out_ref, send_ref, bucket_ref, len_ref, in_sems, sems
):
    half = k_ref.shape[1] // CORES
    loads = []
    for c in range(CORES):
        for n, ref in enumerate((k_ref, v_ref)):
            loads.append(
                pltpu.make_async_copy(
                    ref.at[:, pl.ds(c * half, half)],
                    send_ref.at[c, :, pl.ds(n * half, half)],
                    in_sems.at[2 * c + n],
                )
            )
            loads[-1].start()
    for n, (ref, held) in enumerate(((bucket_in, bucket_ref), (len_in, len_ref))):
        loads.append(pltpu.make_async_copy(ref, held, in_sems.at[4 + n]))
        loads[-1].start()
    loads[4].wait()
    loads[5].wait()
    lanes = lax.broadcasted_iota(jnp.int32, (k_ref.shape[0], HEAD_DIM), 1)
    payload = jnp.where(lanes < HEAD_DIM // 2, bucket_ref[...], len_ref[...])
    copies = []
    for c in range(CORES):
        send_ref[c, :, 2 * half :] = payload.astype(jnp.float32).astype(jnp.bfloat16)
        loads[2 * c].wait()
        loads[2 * c + 1].wait()
        for m in range(c, out_ref.shape[0], CORES):
            copies.append(pltpu.make_async_copy(send_ref.at[c], out_ref.at[m], sems.at[m]))
            copies[-1].start()
    for copy in copies:
        copy.wait()


def swap_kernel(q_ref, g_ref, k_ref, v_ref, _after, q_0, q_1, g_0, g_1, kv_ref, sems):
    other = 1 - lax.axis_index("group") % CORES
    copies = []
    for ref, outs in ((q_ref, (q_0, q_1)), (g_ref, (g_0, g_1))):
        for h, out in enumerate(outs):
            at = pl.multiple_of((other * len(outs) + h) * LANES, LANES)
            copies.append((ref.at[:, pl.ds(at, LANES)], out))
    half = k_ref.shape[1] // CORES
    cols = pl.ds(pl.multiple_of(other * half, half), half)
    copies.append((k_ref.at[:, cols], kv_ref.at[:, pl.ds(0, half)]))
    copies.append((v_ref.at[:, cols], kv_ref.at[:, pl.ds(half, half)]))
    copies = [pltpu.make_async_copy(a, b, sems.at[n]) for n, (a, b) in enumerate(copies)]
    for copy in copies:
        copy.start()
    for copy in copies:
        copy.wait()


def near_kernel(
    own_q, own_g, own_k, own_v, q_0, q_1, g_0, g_1, kv_ref, meta_ref, own_meta_ref,
    qs_ref, gs_ref, ks_ref, vs_ref, stats_ref, held_ref, sems,
):
    core = lax.axis_index("group") % CORES
    slots = own_q.shape[0]
    at, copies = 0, []
    for i, ref in enumerate((own_q, own_g, own_k, own_v)):
        half = ref.shape[1] // CORES
        cols = pl.ds(pl.multiple_of(core * half, half), half)
        to = held_ref.at[:, pl.ds(at, half)]
        copies.append(pltpu.make_async_copy(ref.at[:, cols], to, sems.at[i]))
        copies[-1].start()
        at += half
    heads = KV_HEADS // CORES
    wide = heads * LANES
    rows = lax.broadcasted_iota(jnp.int32, (slots, HEAD_DIM), 0).astype(jnp.float32)

    for r in (1, 0):
        if r == 0:
            length = own_meta_ref[0:1, 64:65]
            for copy in copies:
                copy.wait()
        else:
            length = meta_ref[0:1, 64:65]
        mask = jnp.where(rows < length, 1.0, 0.0).astype(jnp.bfloat16)
        for h in range(heads):
            i = h * CORES + r
            if r == 0:
                refs = (held_ref, held_ref, held_ref, held_ref)
                starts = (h * LANES, wide + h * LANES, 2 * wide + h * HEAD_DIM)
                starts += (2 * wide + (heads + h) * HEAD_DIM,)
            else:
                refs = ((q_0, q_1)[h], (g_0, g_1)[h], kv_ref, kv_ref)
                starts = (0, 0, h * HEAD_DIM, (heads + h) * HEAD_DIM)

            def piece(n, at=0, refs=refs, starts=starts):
                return refs[n][:, starts[n] + at : starts[n] + at + HEAD_DIM]

            spots = range(0, LANES, HEAD_DIM)
            queries = jnp.concatenate([piece(0, at) for at in spots], axis=0)
            grads = jnp.concatenate([piece(1, at) * mask for at in spots], axis=0)
            keys, values = piece(2), piece(3)
            qs_ref[i], gs_ref[i], ks_ref[i], vs_ref[i] = queries, grads, keys, values
            scores = causal(dot_nt(keys, queries) * EXP2_SCALE)
            dprobs = dot_nt(values, grads)
            top = jnp.max(scores, axis=0, keepdims=True)
            terms = jnp.exp2(scores - top)
            stats_ref[i, 0:1] = top
            stats_ref[i, 1:2] = jnp.sum(terms, axis=0, keepdims=True)
            stats_ref[i, 2:3] = jnp.sum(terms * dprobs, axis=0, keepdims=True)


def advantages(own_meta, swap_meta, extra):
    rows = extra.shape[0]
    members = 16
    unit = 1.0 / (BUCKETS - 1)
    sums = jnp.sum(extra.astype(jnp.float32), axis=0, keepdims=True)[:, 0:1]
    mean = sums * (unit / rows)
    own = own_meta[:, 0:1] * unit - mean
    other = swap_meta[:, 0:1] * unit - mean
    return own, other


def far_jobs(
    first, last, own_meta_ref, meta_ref, near_ref, gathered_ref, qs_ref, gs_ref, acc_ref,
    slopes_out, stats_out, part_ref, slopes_ref, stats_ref, probs_ref, send_ref, sems, part_sems,
):
    width = KV_HEADS // CORES * HEAD_DIM
    own_scale, other_scale = advantages(
        own_meta_ref[0:1], meta_ref[0:1], gathered_ref[:, 2 * width :]
    )

    def saves(i):
        return (
            pltpu.make_async_copy(slopes_ref.at[i], slopes_out.at[i], sems.at[0, i]),
            pltpu.make_async_copy(stats_ref.at[i], stats_out.at[i], sems.at[1, i]),
        )

    def sends(h):
        copies = []
        for n in range(2):
            cols = pl.ds(pl.multiple_of(n * width + h * HEAD_DIM, HEAD_DIM), HEAD_DIM)
            copies.append(
                pltpu.make_async_copy(send_ref.at[h, n], part_ref.at[:, cols], part_sems.at[h, n])
            )
        return copies

    def job(i, _):
        h, r = i // CORES, i % CORES
        keys = gathered_ref[:, pl.ds(pl.multiple_of(h * HEAD_DIM, HEAD_DIM), HEAD_DIM)]
        values = gathered_ref[:, pl.ds(pl.multiple_of(width + h * HEAD_DIM, HEAD_DIM), HEAD_DIM)]
        scores = dot_nt(keys, qs_ref[i]) * EXP2_SCALE
        dprobs = dot_nt(values, gs_ref[i])
        near_top = near_ref[i, 0:1]
        top = jnp.maximum(jnp.max(scores, axis=0, keepdims=True), near_top)
        shift = jnp.exp2(near_top - top)
        terms = jnp.exp2(scores - top)
        total = jnp.sum(terms, axis=0, keepdims=True) + near_ref[i, 1:2] * shift
        delta = jnp.sum(terms * dprobs, axis=0, keepdims=True) + near_ref[i, 2:3] * shift
        inverse = 1.0 / total
        delta = delta * inverse
        probs = terms * inverse
        probs_ref[...] = probs.astype(jnp.bfloat16)
        slopes_ref[i] = (probs * (dprobs - delta)).astype(jnp.bfloat16)
        stats_ref[i, 0:1] = top
        stats_ref[i, 1:2] = inverse
        stats_ref[i, 2:3] = delta
        for copy in saves(i):
            copy.start()
        scale = jnp.where(r == 0, own_scale, other_scale)
        key_part = dot_nn(slopes_ref[i], qs_ref[i]) * (scale * SCALE)
        value_part = dot_nn(probs_ref[...], gs_ref[i]) * scale

        @pl.when(r == 0)
        def _():
            acc_ref[0], acc_ref[1] = key_part, value_part

        @pl.when(r == 1)
        def _():
            send_ref[h, 0] = (acc_ref[0] + key_part).astype(jnp.bfloat16)
            send_ref[h, 1] = (acc_ref[1] + value_part).astype(jnp.bfloat16)
            for copy in sends(h):
                copy.start()

        return 0

    def drain(i, _):
        for copy in saves(i):
            copy.wait()

        @pl.when(i % CORES == 1)
        def _():
            for copy in sends(i // CORES):
                copy.wait()

        return 0

    lax.fori_loop(first, last, job, 0)
    lax.fori_loop(first, last, drain, 0)


def jobs_before():
    z = lax.axis_index("dp") // 2
    return jnp.where(z < 2, 2, jnp.where(z < 4, 1, 0))


def first_far_kernel(
    own_meta_ref, meta_ref, near_ref, gathered_ref, _qs, _gs, _ks, _vs,
    slopes_out, stats_out, part_ref, acc_ref, qs_ref, gs_ref, _ks_out, _vs_out, *scratch,
):
    far_jobs(
        0, jobs_before(), own_meta_ref, meta_ref, near_ref, gathered_ref, qs_ref, gs_ref, acc_ref,
        slopes_out, stats_out, part_ref, *scratch,
    )


def second_far_kernel(
    own_meta_ref, meta_ref, near_ref, gathered_ref, _slopes, _stats, _part,
    _acc, _qs, _gs, _ks, _vs,
    slopes_out, stats_out, part_ref, acc_ref, qs_ref, gs_ref, _ks_out, _vs_out, *scratch,
):
    far_jobs(
        jobs_before(), KV_HEADS, own_meta_ref, meta_ref, near_ref, gathered_ref, qs_ref, gs_ref,
        acc_ref, slopes_out, stats_out, part_ref, *scratch,
    )


def tokens_kernel(tokens_ref, _part, part_ref, send_ref, sem):
    tokens = jnp.broadcast_to(tokens_ref[0:1, HEAD_DIM // 2 : HEAD_DIM // 2 + 1], (1, HEAD_DIM))
    high = jnp.floor(tokens * (1.0 / 256.0))
    lanes = lax.broadcasted_iota(jnp.int32, tokens.shape, 1)
    tokens = jnp.where(lanes < HEAD_DIM // 2, high, tokens - high * 256.0)
    send_ref[...] = jnp.broadcast_to(tokens, send_ref.shape).astype(jnp.bfloat16)
    at = part_ref.shape[1] - HEAD_DIM
    copy = pltpu.make_async_copy(send_ref, part_ref.at[:, pl.ds(at, HEAD_DIM)], sem.at[0])
    copy.start()
    copy.wait()


def own_kernel(
    qs_ref, gs_ref, ks_ref, vs_ref, gathered_ref, slopes_in, stats_in, own_out, swap_0, swap_1, swap_kv, own_ref, slopes_ref, stats_ref, sems, out_sems,
):
    heads = KV_HEADS // CORES
    slots = ks_ref.shape[1]
    loads = {}
    for r in (1, 0):
        for h in range(heads):
            i = h * CORES + r
            loads[i] = (
                pltpu.make_async_copy(slopes_in.at[i], slopes_ref.at[i], sems.at[0, i]),
                pltpu.make_async_copy(stats_in.at[i], stats_ref.at[i], sems.at[1, i]),
            )
            for load in loads[i]:
                load.start()
    copies = []
    for r in (1, 0):
        for h in range(heads):
            i = h * CORES + r
            if r:
                gq_ref, gq_at, kv_ref, kv_at = (swap_0, swap_1)[h], 0, swap_kv, 0
            else:
                gq_ref, gq_at, kv_ref, kv_at = own_ref, h * LANES, own_ref, heads * LANES
            queries, grads = qs_ref[i], gs_ref[i]
            keys, values = ks_ref[i], vs_ref[i]
            scores = causal(dot_nt(keys, queries) * EXP2_SCALE)
            dprobs = dot_nt(values, grads)
            loads[i][1].wait()
            top, inverse, delta = stats_ref[i, 0:1], stats_ref[i, 1:2], stats_ref[i, 2:3]
            probs = jnp.exp2(scores - top) * inverse
            slopes = (probs * (dprobs - delta)).astype(jnp.bfloat16)
            far_keys = gathered_ref[:, h * HEAD_DIM : (h + 1) * HEAD_DIM]
            loads[i][0].wait()
            gq = dot_tn(far_keys, slopes_ref[i]) + dot_tn(keys, slopes)
            for n in range(GROUP_HEADS):
                at = gq_at + n * HEAD_DIM
                gq_ref[:, at : at + HEAD_DIM] = gq[:, n * slots : (n + 1) * slots].T.astype(
                    jnp.bfloat16
                )
            at = kv_at + h * HEAD_DIM
            kv_ref[:, at : at + HEAD_DIM] = dot_nn(slopes, queries).astype(jnp.bfloat16)
            at += heads * HEAD_DIM
            kv_ref[:, at : at + HEAD_DIM] = dot_nn(probs.astype(jnp.bfloat16), grads).astype(
                jnp.bfloat16
            )
    copy = pltpu.make_async_copy(own_ref, own_out, out_sems.at[0])
    copy.start()
    copy.wait()


def finish_kernel(
    own_meta_ref, meta_ref, gathered_ref, recv_ref, own_in, swap_0, swap_1, swap_kv,
    gq_out, gk_out, gv_out, far_k_out, far_v_out,
    own_ref, gq_ref, gk_ref, gv_ref, far_k_ref, far_v_ref, in_sem, sems,
):
    load = pltpu.make_async_copy(own_in, own_ref, in_sem.at[0])
    load.start()
    core = lax.axis_index("group") % CORES
    members = recv_ref.shape[0]
    width = gk_ref.shape[1] // CORES
    slots = own_ref.shape[0]
    wide = gq_ref.shape[1] // CORES
    advantage, _ = advantages(own_meta_ref[0:1], meta_ref[0:1], gathered_ref[:, 2 * width :])
    tokens = jnp.sum(recv_ref[:, 0:1, 2 * width :].astype(jnp.float32), axis=0)
    token_total = tokens[:, 0:1] * 256.0 + tokens[:, HEAD_DIM // 2 : HEAD_DIM // 2 + 1]
    norm = (16 * 16 * slots) / token_total
    factor = advantage * norm
    copies = []

    def put(ref, at, value, scale):
        cols = pl.ds(pl.multiple_of(at, HEAD_DIM), value.shape[1])
        ref[:, cols] = (value.astype(jnp.float32) * scale).astype(jnp.bfloat16)

    def send(source, to):
        copies.append(pltpu.make_async_copy(source, to, sems.at[len(copies)]))
        copies[-1].start()

    def put_queries(at, value):
        put(gq_ref, at, value, factor * SCALE)
        cols = pl.ds(pl.multiple_of(at, HEAD_DIM), value.shape[1])
        send(gq_ref.at[:, cols], gq_out.at[:, cols])

    other = 1 - core
    put_queries(other * wide, swap_0[...])
    put_queries(other * wide + LANES, swap_1[...])
    put(gk_ref, other * width, swap_kv[:, :width], factor * SCALE)
    put(gv_ref, other * width, swap_kv[:, width:], factor)
    for c in range(CORES):
        total = recv_ref[c, :, : 2 * width].astype(jnp.float32)
        for m in range(c + CORES, members, CORES):
            total = total + recv_ref[m, :, : 2 * width].astype(jnp.float32)
        total = total * norm
        far_k_ref[:, c * width : (c + 1) * width] = total[:, :width].astype(jnp.bfloat16)
        far_v_ref[:, c * width : (c + 1) * width] = total[:, width:].astype(jnp.bfloat16)
    send(far_k_ref, far_k_out)
    send(far_v_ref, far_v_out)
    load.wait()
    put_queries(core * wide, own_ref[:, :LANES])
    put_queries(core * wide + LANES, own_ref[:, LANES:wide])
    put(gk_ref, core * width, own_ref[:, wide : wide + width], factor * SCALE)
    put(gv_ref, core * width, own_ref[:, wide + width :], factor)
    send(gk_ref, gk_out)
    send(gv_ref, gv_out)
    for copy in copies:
        copy.wait()


def vmem():
    return pl.BlockSpec(memory_space=pltpu.VMEM)


def anywhere():
    return pl.BlockSpec(memory_space=pl.ANY)


def near_memory(x):
    return pltpu.with_memory_space_constraint(x, pltpu.VMEM)


def far_memory(x):
    return pltpu.with_memory_space_constraint(x, pltpu.HBM)


def call(kernel, in_specs, out_specs, out_shape, flops, nbytes, scratch=(), aliases=None):
    return pl.pallas_call(
        kernel,
        in_specs=in_specs,
        out_specs=out_specs,
        out_shape=out_shape,
        scratch_shapes=list(scratch),
        input_output_aliases=aliases or {},
        compiler_params=pltpu.CompilerParams(vmem_limit_bytes=VMEM),
        cost_estimate=pl.CostEstimate(flops=flops, bytes_accessed=nbytes, transcendentals=0),
    )


def body(
    prefix_keys, prefix_values, resp_queries, resp_keys, resp_values, grad_out, lengths, buckets
):
    slots = resp_queries.shape[2]
    own_rows = prefix_keys.shape[1]
    members = lax.axis_size("group")
    rows = own_rows * members
    heads = KV_HEADS // CORES
    width = heads * HEAD_DIM
    wide = heads * LANES
    jobs = heads * CORES
    q, g = resp_queries[0, 0], grad_out[0, 0]
    kn, vn = resp_keys[0, 0], resp_values[0, 0]
    f32, bf16 = jnp.float32, jnp.bfloat16
    pairs = [(i, i ^ 1) for i in range(members)]

    spread = call(
        spread_kernel,
        [anywhere()] * 4,
        anywhere(),
        pltpu.HBM((members, own_rows, 2 * width + HEAD_DIM), bf16),
        0, 1 << 20,
        [pltpu.VMEM((CORES, own_rows, 2 * width + HEAD_DIM), bf16),
         pltpu.VMEM((1, 1), jnp.int32), pltpu.VMEM((1, 1), jnp.int32),
         pltpu.SemaphoreType.DMA((6,)), pltpu.SemaphoreType.DMA((members,))],
    )(far_memory(prefix_keys[0]), far_memory(prefix_values[0]), buckets, lengths)
    gathered3 = lax.all_to_all(spread, "group", 0, 0, tiled=True)
    gathered = gathered3.reshape(rows, -1)

    lanes = lax.broadcasted_iota(jnp.int32, (8, HEAD_DIM), 1)
    meta = jnp.where(lanes < HEAD_DIM // 2, buckets, lengths).astype(f32)
    meta_in = lax.ppermute(meta, "group", pairs)
    swap = call(
        swap_kernel,
        [anywhere()] * 5,
        [vmem()] * 5,
        [pltpu.VMEM((slots, LANES), bf16)] * 4 + [pltpu.VMEM((slots, 2 * width), bf16)],
        0, 2 << 20,
        [pltpu.SemaphoreType.DMA((6,))],
    )(*(far_memory(x) for x in (q, g, kn, vn, spread)))
    swapped = [lax.ppermute(x, "group", pairs) for x in swap]

    qs, gs, ks, vs, near = call(
        near_kernel,
        [anywhere()] * 4 + [vmem()] * 7,
        [vmem()] * 5,
        [pltpu.VMEM((jobs, LANES, HEAD_DIM), bf16), pltpu.VMEM((jobs, LANES, HEAD_DIM), bf16),
         pltpu.VMEM((jobs, slots, HEAD_DIM), bf16), pltpu.VMEM((jobs, slots, HEAD_DIM), bf16),
         pltpu.VMEM((jobs, 8, LANES), f32)],
        2 * 2 * 4096 * 128 * 128, 3 << 20,
        [pltpu.VMEM((slots, 2 * wide + 2 * width), bf16), pltpu.SemaphoreType.DMA((4,))],
    )(*(far_memory(x) for x in (q, g, kn, vn)),
      *(near_memory(x) for x in (*swapped, meta_in, meta)))

    kept = (qs, gs, ks, vs)
    shared = [near_memory(x) for x in (meta, meta_in, near, gathered)]
    saved_shapes = [pltpu.HBM((jobs, rows, LANES), bf16), pltpu.HBM((jobs, 8, LANES), f32),
                    pltpu.HBM((rows, 2 * width + HEAD_DIM), bf16)]
    kept_shapes = [pltpu.VMEM((2, rows, HEAD_DIM), f32)]
    kept_shapes += [pltpu.VMEM(x.shape, x.dtype) for x in kept]
    scratch = [pltpu.VMEM((jobs, rows, LANES), bf16), pltpu.VMEM((jobs, 8, LANES), f32),
               pltpu.VMEM((rows, LANES), bf16), pltpu.VMEM((heads, 2, rows, HEAD_DIM), bf16),
               pltpu.SemaphoreType.DMA((2, jobs)), pltpu.SemaphoreType.DMA((heads, 2))]
    slopes, stats, part, *kept = call(
        first_far_kernel,
        [vmem()] * 8,
        [anywhere()] * 3 + [vmem()] * 5,
        saved_shapes + kept_shapes,
        2 * 2 * 4096 * 384 * 128, 4 << 20,
        scratch,
        {4 + n: 4 + n for n in range(4)},
    )(*shared, *(near_memory(x) for x in kept))

    dp = lax.axis_size("dp")
    payload, _ = lax.optimization_barrier((gathered3, stats))
    tokens = jnp.sum(payload[:, :8, 2 * width :].astype(f32), axis=0)
    pairs_dp = [
        (d * members + i, (d ^ (i % dp)) * members + i) for d in range(dp) for i in range(members)
    ]
    tokens = lax.ppermute(tokens, ("dp", "group"), pairs_dp)

    slopes, stats, part, _, *kept = call(
        second_far_kernel,
        [vmem()] * 4 + [anywhere()] * 3 + [vmem()] * 5,
        [anywhere()] * 3 + [vmem()] * 5,
        saved_shapes + kept_shapes,
        2 * 2 * 4096 * 384 * 128, 4 << 20,
        scratch,
        {4 + n: n for n in range(8)},
    )(*shared, *(far_memory(x) for x in (slopes, stats, part)), *(near_memory(x) for x in kept))

    part = call(
        tokens_kernel,
        [vmem(), anywhere()],
        anywhere(),
        saved_shapes[2],
        0, 1 << 17,
        [pltpu.VMEM((rows, HEAD_DIM), bf16), pltpu.SemaphoreType.DMA((1,))],
        {1: 0},
    )(near_memory(tokens), far_memory(part))

    recv = lax.all_to_all(part.reshape(members, own_rows, -1), "group", 0, 0, tiled=True)

    own, *swap_out = call(
        own_kernel,
        [vmem()] * 5 + [anywhere()] * 2,
        [anywhere()] + [vmem()] * 3,
        [pltpu.HBM((slots, wide + 2 * width), bf16), pltpu.VMEM((slots, LANES), bf16),
         pltpu.VMEM((slots, LANES), bf16), pltpu.VMEM((slots, 2 * width), bf16)],
        3 * 2 * 4096 * 512 * 128, 8 << 20,
        [pltpu.VMEM((slots, wide + 2 * width), bf16), pltpu.VMEM((jobs, rows, LANES), bf16),
         pltpu.VMEM((jobs, 8, LANES), f32), pltpu.SemaphoreType.DMA((2, jobs)),
         pltpu.SemaphoreType.DMA((1,))],
    )(*(near_memory(x) for x in (*kept, gathered)), far_memory(slopes), far_memory(stats))
    swap_in = [lax.ppermute(x, "group", pairs) for x in swap_out]

    outs = call(
        finish_kernel,
        [vmem()] * 4 + [anywhere()] + [vmem()] * 3,
        [anywhere()] * 5,
        [pltpu.HBM((slots, HEADS * HEAD_DIM), bf16),
         pltpu.HBM((slots, CORES * width), bf16), pltpu.HBM((slots, CORES * width), bf16),
         pltpu.HBM((own_rows, CORES * width), bf16), pltpu.HBM((own_rows, CORES * width), bf16)],
        0, 4 << 20,
        [pltpu.VMEM((slots, wide + 2 * width), bf16), pltpu.VMEM((slots, HEADS * HEAD_DIM), bf16),
         pltpu.VMEM((slots, CORES * width), bf16), pltpu.VMEM((slots, CORES * width), bf16),
         pltpu.VMEM((own_rows, CORES * width), bf16), pltpu.VMEM((own_rows, CORES * width), bf16),
         pltpu.SemaphoreType.DMA((1,)), pltpu.SemaphoreType.DMA((8,))],
    )(*(near_memory(x) for x in (meta, meta_in, gathered, recv)),
      far_memory(own), *(near_memory(x) for x in swap_in))
    gq, gk, gv, far_k, far_v = outs
    return gq[None, None], gk[None, None], gv[None, None], far_k[None], far_v[None]


def solution(mesh):
    in_specs = (
        P("dp", "group", None),
        P("dp", "group", None),
        P("dp", "group", None, None),
        P("dp", "group", None, None),
        P("dp", "group", None, None),
        P("dp", "group", None, None),
        P("dp", "group"),
        P("dp", "group"),
    )
    out_specs = (
        P("dp", "group", None, None),
        P("dp", "group", None, None),
        P("dp", "group", None, None),
        P("dp", "group", None),
        P("dp", "group", None),
    )
    return jax.shard_map(body, mesh=mesh, in_specs=in_specs, out_specs=out_specs, check_vma=False)
```

```python
import functools
import math

import jax
import jax.numpy as jnp
from jax import lax
from jax.experimental import pallas as pl
from jax.experimental.pallas import tpu as pltpu
from jax.sharding import PartitionSpec as P

HEADS = 32
KV_HEADS = 4
HEAD_DIM = 128
BUCKETS = 5
GROUP_HEADS = HEADS // KV_HEADS
LANES = GROUP_HEADS * HEAD_DIM
SCALE = 1.0 / math.sqrt(HEAD_DIM)
EXP2_SCALE = SCALE * math.log2(math.e)
VMEM = 16 * 1024 * 1024
CORES = 2


def dot_nt(a, b):
    return lax.dot_general(a, b, (((1,), (1,)), ((), ())), preferred_element_type=jnp.float32)


def dot_nn(a, b):
    return lax.dot_general(a, b, (((1,), (0,)), ((), ())), preferred_element_type=jnp.float32)


def dot_tn(a, b):
    return lax.dot_general(a, b, (((0,), (0,)), ((), ())), preferred_element_type=jnp.float32)


def causal(scores):
    slots = scores.shape[0]
    keys = lax.broadcasted_iota(jnp.int32, scores.shape, 0)
    queries = lax.broadcasted_iota(jnp.int32, scores.shape, 1) % slots
    return jnp.where(keys <= queries, scores, -jnp.inf)


def spread_kernel(k_ref, v_ref, meta_ref, out_ref, send_ref, in_sems, sems):
    half = k_ref.shape[1] // CORES
    loads = []
    for c in range(CORES):
        for n, ref in enumerate((k_ref, v_ref)):
            loads.append(
                pltpu.make_async_copy(
                    ref.at[:, pl.ds(c * half, half)],
                    send_ref.at[c, :, pl.ds(n * half, half)],
                    in_sems.at[2 * c + n],
                )
            )
            loads[-1].start()
    payload = jnp.broadcast_to(meta_ref[0:1], (k_ref.shape[0], HEAD_DIM)).astype(jnp.bfloat16)
    copies = []
    for c in range(CORES):
        send_ref[c, :, 2 * half :] = payload
        loads[2 * c].wait()
        loads[2 * c + 1].wait()
        for m in range(c, out_ref.shape[0], CORES):
            copies.append(pltpu.make_async_copy(send_ref.at[c], out_ref.at[m], sems.at[m]))
            copies[-1].start()
    for copy in copies:
        copy.wait()


def swap_kernel(q_ref, g_ref, k_ref, v_ref, _after, meta_ref, q_0, q_1, g_0, g_1, kv_ref, sems):
    other = 1 - lax.axis_index("group") % CORES
    copies = []
    for ref, outs in ((q_ref, (q_0, q_1)), (g_ref, (g_0, g_1))):
        for h, out in enumerate(outs):
            at = pl.multiple_of((other * len(outs) + h) * LANES, LANES)
            copies.append((ref.at[:, pl.ds(at, LANES)], out))
    half = k_ref.shape[1] // CORES
    cols = pl.ds(pl.multiple_of(other * half, half), half)
    copies.append((k_ref.at[:, cols], kv_ref.at[:, pl.ds(0, half)]))
    copies.append((v_ref.at[:, cols], kv_ref.at[:, pl.ds(half, half)]))
    copies = [pltpu.make_async_copy(a, b, sems.at[n]) for n, (a, b) in enumerate(copies)]
    for copy in copies:
        copy.start()
    payload = jnp.broadcast_to(meta_ref[0:1], (kv_ref.shape[0], HEAD_DIM))
    kv_ref[:, 2 * half :] = payload.astype(jnp.bfloat16)
    for copy in copies:
        copy.wait()


def near_jobs(r, length, pieces, qs_ref, gs_ref, ks_ref, vs_ref, stats_ref):
    slots = ks_ref.shape[1]
    rows = lax.broadcasted_iota(jnp.int32, (slots, HEAD_DIM), 0).astype(jnp.float32)
    mask = jnp.where(rows < length, 1.0, 0.0).astype(jnp.bfloat16)
    for h in range(KV_HEADS // CORES):
        i = h * CORES + r
        q_parts, g_parts, keys, values = pieces(h)
        queries = jnp.concatenate(q_parts, axis=0)
        grads = jnp.concatenate([g * mask for g in g_parts], axis=0)
        qs_ref[i], gs_ref[i], ks_ref[i], vs_ref[i] = queries, grads, keys, values
        scores = causal(dot_nt(keys, queries) * EXP2_SCALE)
        dprobs = dot_nt(values, grads)
        top = jnp.max(scores, axis=0, keepdims=True)
        terms = jnp.exp2(scores - top)
        stats_ref[i, 0:1] = top
        stats_ref[i, 1:2] = jnp.sum(terms, axis=0, keepdims=True)
        stats_ref[i, 2:3] = jnp.sum(terms * dprobs, axis=0, keepdims=True)


def near_own_kernel(
    own_q, own_g, own_k, own_v, _after, meta_ref,
    qs_ref, gs_ref, ks_ref, vs_ref, stats_ref, held_ref, sems,
):
    core = lax.axis_index("group") % CORES
    heads = KV_HEADS // CORES
    wide = heads * LANES
    at, copies = 0, []
    for i, ref in enumerate((own_q, own_g, own_k, own_v)):
        half = ref.shape[1] // CORES
        cols = pl.ds(pl.multiple_of(core * half, half), half)
        to = held_ref.at[:, pl.ds(at, half)]
        copies.append(pltpu.make_async_copy(ref.at[:, cols], to, sems.at[i]))
        copies[-1].start()
        at += half
    for copy in copies:
        copy.wait()

    def pieces(h):
        def piece(at):
            return held_ref[:, at : at + HEAD_DIM]

        spots = range(h * LANES, (h + 1) * LANES, HEAD_DIM)
        at = 2 * wide + h * HEAD_DIM
        return (
            [piece(n) for n in spots], [piece(wide + n) for n in spots],
            piece(at), piece(at + heads * HEAD_DIM),
        )

    near_jobs(0, meta_ref[0:1, 64:65], pieces, qs_ref, gs_ref, ks_ref, vs_ref, stats_ref)


def near_other_kernel(
    q_0, q_1, g_0, g_1, kv_ref, _qs, _gs, _ks, _vs, _stats,
    qs_ref, gs_ref, ks_ref, vs_ref, stats_ref, meta_ref,
):
    heads = KV_HEADS // CORES
    payload = kv_ref[0:16, 2 * heads * HEAD_DIM :].astype(jnp.float32)
    meta_ref[...] = payload[0:8]

    def pieces(h):
        def piece(ref, at):
            return ref[:, at : at + HEAD_DIM]

        spots = range(0, LANES, HEAD_DIM)
        at = h * HEAD_DIM
        return (
            [piece((q_0, q_1)[h], n) for n in spots], [piece((g_0, g_1)[h], n) for n in spots],
            piece(kv_ref, at), piece(kv_ref, at + heads * HEAD_DIM),
        )

    near_jobs(1, payload[0:1, 64:65], pieces, qs_ref, gs_ref, ks_ref, vs_ref, stats_ref)


def advantages(own_meta, swap_meta, extra):
    rows = extra.shape[0]
    members = 16
    unit = 1.0 / (BUCKETS - 1)
    sums = jnp.sum(extra.astype(jnp.float32), axis=0, keepdims=True)[:, 0:1]
    mean = sums * (unit / rows)
    own = own_meta[:, 0:1] * unit - mean
    other = swap_meta[:, 0:1] * unit - mean
    return own, other


def far_jobs(
    first, last, own_meta_ref, meta_ref, near_ref, gathered_ref, qs_ref, gs_ref,
    slopes_out, stats_out, send_ref, acc_ref, slopes_ref, stats_ref, probs_ref, sems,
):
    width = KV_HEADS // CORES * HEAD_DIM
    own_scale, other_scale = advantages(
        own_meta_ref[0:1], meta_ref[0:1], gathered_ref[:, 2 * width :]
    )

    def saves(i):
        return (
            pltpu.make_async_copy(slopes_ref.at[i], slopes_out.at[i], sems.at[0, i]),
            pltpu.make_async_copy(stats_ref.at[i], stats_out.at[i], sems.at[1, i]),
        )

    def job(i, _):
        h, r = i // CORES, i % CORES
        keys = gathered_ref[:, pl.ds(pl.multiple_of(h * HEAD_DIM, HEAD_DIM), HEAD_DIM)]
        values = gathered_ref[:, pl.ds(pl.multiple_of(width + h * HEAD_DIM, HEAD_DIM), HEAD_DIM)]
        scores = dot_nt(keys, qs_ref[i]) * EXP2_SCALE
        dprobs = dot_nt(values, gs_ref[i])
        near_top = near_ref[i, 0:1]
        top = jnp.maximum(jnp.max(scores, axis=0, keepdims=True), near_top)
        shift = jnp.exp2(near_top - top)
        terms = jnp.exp2(scores - top)
        total = jnp.sum(terms, axis=0, keepdims=True) + near_ref[i, 1:2] * shift
        delta = jnp.sum(terms * dprobs, axis=0, keepdims=True) + near_ref[i, 2:3] * shift
        inverse = 1.0 / total
        delta = delta * inverse
        probs = terms * inverse
        probs_ref[...] = probs.astype(jnp.bfloat16)
        slopes_ref[i] = (probs * (dprobs - delta)).astype(jnp.bfloat16)
        stats_ref[i, 0:1] = top
        stats_ref[i, 1:2] = inverse
        stats_ref[i, 2:3] = delta
        for copy in saves(i):
            copy.start()
        scale = jnp.where(r == 0, own_scale, other_scale)
        key_part = dot_nn(slopes_ref[i], qs_ref[i]) * (scale * SCALE)
        value_part = dot_nn(probs_ref[...], gs_ref[i]) * scale

        @pl.when(r == 0)
        def _():
            acc_ref[0], acc_ref[1] = key_part, value_part

        @pl.when(r == 1)
        def _():
            send_ref[h, 0] = (acc_ref[0] + key_part).astype(jnp.bfloat16)
            send_ref[h, 1] = (acc_ref[1] + value_part).astype(jnp.bfloat16)

        return 0

    def drain(i, _):
        for copy in saves(i):
            copy.wait()
        return 0

    lax.fori_loop(first, last, job, 0)
    lax.fori_loop(first, last, drain, 0)


def jobs_before():
    z = lax.axis_index("dp") // 2
    return jnp.where(z < 2, 2, jnp.where(z < 4, 1, 0))


def first_far_kernel(
    own_meta_ref, meta_ref, near_ref, gathered_ref, _qs, _gs, _ks, _vs,
    slopes_out, stats_out, send_ref, acc_ref, qs_ref, gs_ref, _ks_out, _vs_out, *scratch,
):
    far_jobs(
        0, jobs_before(), own_meta_ref, meta_ref, near_ref, gathered_ref, qs_ref, gs_ref,
        slopes_out, stats_out, send_ref, acc_ref, *scratch,
    )


def second_far_kernel(
    own_meta_ref, meta_ref, near_ref, gathered_ref, _slopes, _stats,
    _send, _acc, _qs, _gs, _ks, _vs,
    slopes_out, stats_out, send_ref, acc_ref, qs_ref, gs_ref, _ks_out, _vs_out, *scratch,
):
    far_jobs(
        jobs_before(), KV_HEADS, own_meta_ref, meta_ref, near_ref, gathered_ref, qs_ref, gs_ref,
        slopes_out, stats_out, send_ref, acc_ref, *scratch,
    )


def part_kernel(tokens_ref, send_ref, part_ref, payload_ref, sems):
    heads = send_ref.shape[0]
    copies = []
    for h in range(heads):
        for n in range(2):
            at = (n * heads + h) * HEAD_DIM
            copies.append((send_ref.at[h, n], at))
    tokens = jnp.broadcast_to(tokens_ref[0:1, HEAD_DIM // 2 : HEAD_DIM // 2 + 1], (1, HEAD_DIM))
    high = jnp.floor(tokens * (1.0 / 256.0))
    lanes = lax.broadcasted_iota(jnp.int32, tokens.shape, 1)
    tokens = jnp.where(lanes < HEAD_DIM // 2, high, tokens - high * 256.0)
    payload_ref[...] = jnp.broadcast_to(tokens, payload_ref.shape).astype(jnp.bfloat16)
    copies.append((payload_ref, 2 * heads * HEAD_DIM))
    copies = [
        pltpu.make_async_copy(source, part_ref.at[:, pl.ds(at, HEAD_DIM)], sems.at[n])
        for n, (source, at) in enumerate(copies)
    ]
    for copy in copies:
        copy.start()
    for copy in copies:
        copy.wait()


def own_kernel(
    qs_ref, gs_ref, ks_ref, vs_ref, gathered_ref, slopes_in, stats_in, own_out, swap_0, swap_1, swap_kv, own_ref, slopes_ref, stats_ref, sems, out_sems,
):
    heads = KV_HEADS // CORES
    slots = ks_ref.shape[1]
    loads = {}
    for r in (1, 0):
        for h in range(heads):
            i = h * CORES + r
            loads[i] = (
                pltpu.make_async_copy(slopes_in.at[i], slopes_ref.at[i], sems.at[0, i]),
                pltpu.make_async_copy(stats_in.at[i], stats_ref.at[i], sems.at[1, i]),
            )
            for load in loads[i]:
                load.start()
    copies = []
    for r in (1, 0):
        for h in range(heads):
            i = h * CORES + r
            if r:
                gq_ref, gq_at, kv_ref, kv_at = (swap_0, swap_1)[h], 0, swap_kv, 0
            else:
                gq_ref, gq_at, kv_ref, kv_at = own_ref, h * LANES, own_ref, heads * LANES
            queries, grads = qs_ref[i], gs_ref[i]
            keys, values = ks_ref[i], vs_ref[i]
            scores = causal(dot_nt(keys, queries) * EXP2_SCALE)
            dprobs = dot_nt(values, grads)
            loads[i][1].wait()
            top, inverse, delta = stats_ref[i, 0:1], stats_ref[i, 1:2], stats_ref[i, 2:3]
            probs = jnp.exp2(scores - top) * inverse
            slopes = (probs * (dprobs - delta)).astype(jnp.bfloat16)
            far_keys = gathered_ref[:, h * HEAD_DIM : (h + 1) * HEAD_DIM]
            loads[i][0].wait()
            gq = dot_tn(far_keys, slopes_ref[i]) + dot_tn(keys, slopes)
            for n in range(GROUP_HEADS):
                at = gq_at + n * HEAD_DIM
                gq_ref[:, at : at + HEAD_DIM] = gq[:, n * slots : (n + 1) * slots].T.astype(
                    jnp.bfloat16
                )
            at = kv_at + h * HEAD_DIM
            kv_ref[:, at : at + HEAD_DIM] = dot_nn(slopes, queries).astype(jnp.bfloat16)
            at += heads * HEAD_DIM
            kv_ref[:, at : at + HEAD_DIM] = dot_nn(probs.astype(jnp.bfloat16), grads).astype(
                jnp.bfloat16
            )
    copy = pltpu.make_async_copy(own_ref, own_out, out_sems.at[0])
    copy.start()
    copy.wait()


def finish_kernel(
    own_meta_ref, meta_ref, gathered_ref, recv_ref, own_in, swap_0, swap_1, swap_kv,
    gq_out, gk_out, gv_out, far_k_out, far_v_out,
    own_ref, gq_ref, gk_ref, gv_ref, far_k_ref, far_v_ref, in_sem, sems,
):
    load = pltpu.make_async_copy(own_in, own_ref, in_sem.at[0])
    load.start()
    core = lax.axis_index("group") % CORES
    members = recv_ref.shape[0]
    width = gk_ref.shape[1] // CORES
    slots = own_ref.shape[0]
    wide = gq_ref.shape[1] // CORES
    advantage, _ = advantages(own_meta_ref[0:1], meta_ref[0:1], gathered_ref[:, 2 * width :])
    tokens = jnp.sum(recv_ref[:, 0:1, 2 * width :].astype(jnp.float32), axis=0)
    token_total = tokens[:, 0:1] * 256.0 + tokens[:, HEAD_DIM // 2 : HEAD_DIM // 2 + 1]
    norm = (16 * 16 * slots) / token_total
    factor = advantage * norm
    copies = []

    def put(ref, at, value, scale):
        cols = pl.ds(pl.multiple_of(at, HEAD_DIM), value.shape[1])
        ref[:, cols] = (value.astype(jnp.float32) * scale).astype(jnp.bfloat16)

    def send(source, to):
        copies.append(pltpu.make_async_copy(source, to, sems.at[len(copies)]))
        copies[-1].start()

    def put_queries(at, value):
        put(gq_ref, at, value, factor * SCALE)
        cols = pl.ds(pl.multiple_of(at, HEAD_DIM), value.shape[1])
        send(gq_ref.at[:, cols], gq_out.at[:, cols])

    other = 1 - core
    put_queries(other * wide, swap_0[...])
    put_queries(other * wide + LANES, swap_1[...])
    put(gk_ref, other * width, swap_kv[:, :width], factor * SCALE)
    put(gv_ref, other * width, swap_kv[:, width:], factor)
    for c in range(CORES):
        total = recv_ref[c, :, : 2 * width].astype(jnp.float32)
        for m in range(c + CORES, members, CORES):
            total = total + recv_ref[m, :, : 2 * width].astype(jnp.float32)
        total = total * norm
        far_k_ref[:, c * width : (c + 1) * width] = total[:, :width].astype(jnp.bfloat16)
        far_v_ref[:, c * width : (c + 1) * width] = total[:, width:].astype(jnp.bfloat16)
    send(far_k_ref, far_k_out)
    send(far_v_ref, far_v_out)
    load.wait()
    put_queries(core * wide, own_ref[:, :LANES])
    put_queries(core * wide + LANES, own_ref[:, LANES:wide])
    put(gk_ref, core * width, own_ref[:, wide : wide + width], factor * SCALE)
    put(gv_ref, core * width, own_ref[:, wide + width :], factor)
    send(gk_ref, gk_out)
    send(gv_ref, gv_out)
    for copy in copies:
        copy.wait()


def vmem():
    return pl.BlockSpec(memory_space=pltpu.VMEM)


def anywhere():
    return pl.BlockSpec(memory_space=pl.ANY)


def near_memory(x):
    return pltpu.with_memory_space_constraint(x, pltpu.VMEM)


def far_memory(x):
    return pltpu.with_memory_space_constraint(x, pltpu.HBM)


def call(kernel, in_specs, out_specs, out_shape, flops, nbytes, scratch=(), aliases=None):
    return pl.pallas_call(
        kernel,
        in_specs=in_specs,
        out_specs=out_specs,
        out_shape=out_shape,
        scratch_shapes=list(scratch),
        input_output_aliases=aliases or {},
        compiler_params=pltpu.CompilerParams(vmem_limit_bytes=VMEM),
        cost_estimate=pl.CostEstimate(flops=flops, bytes_accessed=nbytes, transcendentals=0),
    )


def body(
    prefix_keys, prefix_values, resp_queries, resp_keys, resp_values, grad_out, lengths, buckets
):
    slots = resp_queries.shape[2]
    own_rows = prefix_keys.shape[1]
    members = lax.axis_size("group")
    rows = own_rows * members
    heads = KV_HEADS // CORES
    width = heads * HEAD_DIM
    wide = heads * LANES
    jobs = heads * CORES
    q, g = resp_queries[0, 0], grad_out[0, 0]
    kn, vn = resp_keys[0, 0], resp_values[0, 0]
    f32, bf16 = jnp.float32, jnp.bfloat16
    pairs = [(i, i ^ 1) for i in range(members)]

    meta = jnp.pad(buckets.astype(f32), ((0, 7), (0, HEAD_DIM - 1)))
    meta += jnp.pad(lengths.astype(f32), ((0, 7), (HEAD_DIM // 2, HEAD_DIM // 2 - 1)))
    spread = call(
        spread_kernel,
        [anywhere(), anywhere(), vmem()],
        anywhere(),
        pltpu.HBM((members, own_rows, 2 * width + HEAD_DIM), bf16),
        0, 1 << 20,
        [pltpu.VMEM((CORES, own_rows, 2 * width + HEAD_DIM), bf16),
         pltpu.SemaphoreType.DMA((4,)), pltpu.SemaphoreType.DMA((members,))],
    )(far_memory(prefix_keys[0]), far_memory(prefix_values[0]), near_memory(meta))
    gathered3 = lax.all_to_all(spread, "group", 0, 0, tiled=True)
    gathered = gathered3.reshape(rows, -1)

    swap = call(
        swap_kernel,
        [anywhere()] * 5 + [vmem()],
        [vmem()] * 5,
        [pltpu.VMEM((slots, LANES), bf16)] * 4 + [pltpu.VMEM((slots, 2 * width + HEAD_DIM), bf16)],
        0, 2 << 20,
        [pltpu.SemaphoreType.DMA((6,))],
    )(*(far_memory(x) for x in (q, g, kn, vn, spread)), near_memory(meta))
    swapped = [lax.ppermute(x, "group", pairs) for x in swap]

    near_shapes = [
        pltpu.VMEM((jobs, LANES, HEAD_DIM), bf16), pltpu.VMEM((jobs, LANES, HEAD_DIM), bf16),
        pltpu.VMEM((jobs, slots, HEAD_DIM), bf16), pltpu.VMEM((jobs, slots, HEAD_DIM), bf16),
        pltpu.VMEM((jobs, 8, LANES), f32),
    ]
    nears = call(
        near_own_kernel,
        [anywhere()] * 5 + [vmem()],
        [vmem()] * 5,
        near_shapes,
        2 * 4096 * 128 * 128, 2 << 20,
        [pltpu.VMEM((slots, 2 * wide + 2 * width), bf16), pltpu.SemaphoreType.DMA((4,))],
    )(*(far_memory(x) for x in (q, g, kn, vn, spread)), near_memory(meta))
    qs, gs, ks, vs, near, meta_in = call(
        near_other_kernel,
        [vmem()] * 10,
        [vmem()] * 6,
        near_shapes + [pltpu.VMEM((8, HEAD_DIM), f32)],
        2 * 4096 * 128 * 128, 2 << 20,
        (),
        {5 + n: n for n in range(5)},
    )(*(near_memory(x) for x in (*swapped, *nears)))

    kept = (qs, gs, ks, vs)
    shared = [near_memory(x) for x in (meta, meta_in, near, gathered)]
    saved_shapes = [pltpu.HBM((jobs, rows, LANES), bf16), pltpu.HBM((jobs, 8, LANES), f32)]
    kept_shapes = [pltpu.VMEM((heads, 2, rows, HEAD_DIM), bf16),
                   pltpu.VMEM((2, rows, HEAD_DIM), f32)]
    kept_shapes += [pltpu.VMEM(x.shape, x.dtype) for x in kept]
    scratch = [pltpu.VMEM((jobs, rows, LANES), bf16), pltpu.VMEM((jobs, 8, LANES), f32),
               pltpu.VMEM((rows, LANES), bf16), pltpu.SemaphoreType.DMA((2, jobs))]
    slopes, stats, *kept = call(
        first_far_kernel,
        [vmem()] * 8,
        [anywhere()] * 2 + [vmem()] * 6,
        saved_shapes + kept_shapes,
        2 * 2 * 4096 * 384 * 128, 4 << 20,
        scratch,
        {4 + n: 4 + n for n in range(4)},
    )(*shared, *(near_memory(x) for x in kept))

    dp = lax.axis_size("dp")
    payload, _ = lax.optimization_barrier((gathered3, stats))
    tokens = jnp.sum(payload[:, :8, 2 * width :].astype(f32), axis=0)
    pairs_dp = [
        (d * members + i, (d ^ (i % dp)) * members + i) for d in range(dp) for i in range(members)
    ]
    tokens = lax.ppermute(tokens, ("dp", "group"), pairs_dp)

    slopes, stats, send, _, *kept = call(
        second_far_kernel,
        [vmem()] * 4 + [anywhere()] * 2 + [vmem()] * 6,
        [anywhere()] * 2 + [vmem()] * 6,
        saved_shapes + kept_shapes,
        2 * 2 * 4096 * 384 * 128, 4 << 20,
        scratch,
        {4 + n: n for n in range(8)},
    )(*shared, far_memory(slopes), far_memory(stats), *(near_memory(x) for x in kept))

    part = call(
        part_kernel,
        [vmem()] * 2,
        anywhere(),
        pltpu.HBM((rows, 2 * width + HEAD_DIM), bf16),
        0, 1 << 19,
        [pltpu.VMEM((rows, HEAD_DIM), bf16), pltpu.SemaphoreType.DMA((2 * heads + 1,))],
    )(near_memory(tokens), near_memory(send))

    recv = lax.all_to_all(part.reshape(members, own_rows, -1), "group", 0, 0, tiled=True)

    own, *swap_out = call(
        own_kernel,
        [vmem()] * 5 + [anywhere()] * 2,
        [anywhere()] + [vmem()] * 3,
        [pltpu.HBM((slots, wide + 2 * width), bf16), pltpu.VMEM((slots, LANES), bf16),
         pltpu.VMEM((slots, LANES), bf16), pltpu.VMEM((slots, 2 * width), bf16)],
        3 * 2 * 4096 * 512 * 128, 8 << 20,
        [pltpu.VMEM((slots, wide + 2 * width), bf16), pltpu.VMEM((jobs, rows, LANES), bf16),
         pltpu.VMEM((jobs, 8, LANES), f32), pltpu.SemaphoreType.DMA((2, jobs)),
         pltpu.SemaphoreType.DMA((1,))],
    )(*(near_memory(x) for x in (*kept, gathered)), far_memory(slopes), far_memory(stats))
    swap_in = [lax.ppermute(x, "group", pairs) for x in swap_out]

    outs = call(
        finish_kernel,
        [vmem()] * 4 + [anywhere()] + [vmem()] * 3,
        [anywhere()] * 5,
        [pltpu.HBM((slots, HEADS * HEAD_DIM), bf16),
         pltpu.HBM((slots, CORES * width), bf16), pltpu.HBM((slots, CORES * width), bf16),
         pltpu.HBM((own_rows, CORES * width), bf16), pltpu.HBM((own_rows, CORES * width), bf16)],
        0, 4 << 20,
        [pltpu.VMEM((slots, wide + 2 * width), bf16), pltpu.VMEM((slots, HEADS * HEAD_DIM), bf16),
         pltpu.VMEM((slots, CORES * width), bf16), pltpu.VMEM((slots, CORES * width), bf16),
         pltpu.VMEM((own_rows, CORES * width), bf16), pltpu.VMEM((own_rows, CORES * width), bf16),
         pltpu.SemaphoreType.DMA((1,)), pltpu.SemaphoreType.DMA((8,))],
    )(*(near_memory(x) for x in (meta, meta_in, gathered, recv)),
      far_memory(own), *(near_memory(x) for x in swap_in))
    gq, gk, gv, far_k, far_v = outs
    return gq[None, None], gk[None, None], gv[None, None], far_k[None], far_v[None]


def solution(mesh):
    in_specs = (
        P("dp", "group", None),
        P("dp", "group", None),
        P("dp", "group", None, None),
        P("dp", "group", None, None),
        P("dp", "group", None, None),
        P("dp", "group", None, None),
        P("dp", "group"),
        P("dp", "group"),
    )
    out_specs = (
        P("dp", "group", None, None),
        P("dp", "group", None, None),
        P("dp", "group", None, None),
        P("dp", "group", None),
        P("dp", "group", None),
    )
    return jax.shard_map(body, mesh=mesh, in_specs=in_specs, out_specs=out_specs, check_vma=False)
```

```python
import functools
import math

import jax
import jax.numpy as jnp
from jax import lax
from jax.experimental import pallas as pl
from jax.experimental.pallas import tpu as pltpu
from jax.sharding import PartitionSpec as P

HEADS = 32
KV_HEADS = 4
HEAD_DIM = 128
BUCKETS = 5
GROUP_HEADS = HEADS // KV_HEADS
LANES = GROUP_HEADS * HEAD_DIM
SCALE = 1.0 / math.sqrt(HEAD_DIM)
EXP2_SCALE = SCALE * math.log2(math.e)
VMEM = 16 * 1024 * 1024
CORES = 2


def dot_nt(a, b):
    return lax.dot_general(a, b, (((1,), (1,)), ((), ())), preferred_element_type=jnp.float32)


def dot_nn(a, b):
    return lax.dot_general(a, b, (((1,), (0,)), ((), ())), preferred_element_type=jnp.float32)


def dot_tn(a, b):
    return lax.dot_general(a, b, (((0,), (0,)), ((), ())), preferred_element_type=jnp.float32)


def causal(scores):
    slots = scores.shape[0]
    keys = lax.broadcasted_iota(jnp.int32, scores.shape, 0)
    queries = lax.broadcasted_iota(jnp.int32, scores.shape, 1) % slots
    return jnp.where(keys <= queries, scores, -jnp.inf)


def spread_kernel(k_ref, v_ref, meta_ref, out_ref, send_ref, in_sems, sems):
    half = k_ref.shape[1] // CORES
    loads = []
    for c in range(CORES):
        for n, ref in enumerate((k_ref, v_ref)):
            loads.append(
                pltpu.make_async_copy(
                    ref.at[:, pl.ds(c * half, half)],
                    send_ref.at[c, :, pl.ds(n * half, half)],
                    in_sems.at[2 * c + n],
                )
            )
            loads[-1].start()
    payload = jnp.broadcast_to(meta_ref[0:1], (k_ref.shape[0], HEAD_DIM)).astype(jnp.bfloat16)
    copies = []
    for c in range(CORES):
        send_ref[c, :, 2 * half :] = payload
        loads[2 * c].wait()
        loads[2 * c + 1].wait()
        for m in range(c, out_ref.shape[0], CORES):
            copies.append(pltpu.make_async_copy(send_ref.at[c], out_ref.at[m], sems.at[m]))
            copies[-1].start()
    for copy in copies:
        copy.wait()


def swap_kernel(q_ref, g_ref, k_ref, v_ref, _after, meta_ref, q_0, q_1, g_0, g_1, kv_ref, sems):
    other = 1 - lax.axis_index("group") % CORES
    copies = []
    for ref, outs in ((q_ref, (q_0, q_1)), (g_ref, (g_0, g_1))):
        for h, out in enumerate(outs):
            at = pl.multiple_of((other * len(outs) + h) * LANES, LANES)
            copies.append((ref.at[:, pl.ds(at, LANES)], out))
    half = k_ref.shape[1] // CORES
    cols = pl.ds(pl.multiple_of(other * half, half), half)
    copies.append((k_ref.at[:, cols], kv_ref.at[:, pl.ds(0, half)]))
    copies.append((v_ref.at[:, cols], kv_ref.at[:, pl.ds(half, half)]))
    copies = [pltpu.make_async_copy(a, b, sems.at[n]) for n, (a, b) in enumerate(copies)]
    for copy in copies:
        copy.start()
    payload = jnp.broadcast_to(meta_ref[0:1], (kv_ref.shape[0], HEAD_DIM))
    kv_ref[:, 2 * half :] = payload.astype(jnp.bfloat16)
    for copy in copies:
        copy.wait()


def near_jobs(r, length, pieces, qs_ref, gs_ref, ks_ref, vs_ref, stats_ref):
    slots = ks_ref.shape[1]
    rows = lax.broadcasted_iota(jnp.int32, (slots, HEAD_DIM), 0).astype(jnp.float32)
    mask = jnp.where(rows < length, 1.0, 0.0).astype(jnp.bfloat16)
    for h in range(KV_HEADS // CORES):
        i = h * CORES + r
        q_parts, g_parts, keys, values = pieces(h)
        queries = jnp.concatenate(q_parts, axis=0)
        grads = jnp.concatenate([g * mask for g in g_parts], axis=0)
        qs_ref[i], gs_ref[i], ks_ref[i], vs_ref[i] = queries, grads, keys, values
        scores = causal(dot_nt(keys, queries) * EXP2_SCALE)
        dprobs = dot_nt(values, grads)
        top = jnp.max(scores, axis=0, keepdims=True)
        terms = jnp.exp2(scores - top)
        stats_ref[i, 0:1] = top
        stats_ref[i, 1:2] = jnp.sum(terms, axis=0, keepdims=True)
        stats_ref[i, 2:3] = jnp.sum(terms * dprobs, axis=0, keepdims=True)


def near_own_kernel(
    own_q, own_g, own_k, own_v, _after, meta_ref,
    qs_ref, gs_ref, ks_ref, vs_ref, stats_ref, held_ref, sems,
):
    core = lax.axis_index("group") % CORES
    heads = KV_HEADS // CORES
    wide = heads * LANES
    at, copies = 0, []
    for i, ref in enumerate((own_q, own_g, own_k, own_v)):
        half = ref.shape[1] // CORES
        cols = pl.ds(pl.multiple_of(core * half, half), half)
        to = held_ref.at[:, pl.ds(at, half)]
        copies.append(pltpu.make_async_copy(ref.at[:, cols], to, sems.at[i]))
        copies[-1].start()
        at += half
    for copy in copies:
        copy.wait()

    def pieces(h):
        def piece(at):
            return held_ref[:, at : at + HEAD_DIM]

        spots = range(h * LANES, (h + 1) * LANES, HEAD_DIM)
        at = 2 * wide + h * HEAD_DIM
        return (
            [piece(n) for n in spots], [piece(wide + n) for n in spots],
            piece(at), piece(at + heads * HEAD_DIM),
        )

    near_jobs(0, meta_ref[0:1, 64:65], pieces, qs_ref, gs_ref, ks_ref, vs_ref, stats_ref)


def near_other_kernel(
    q_0, q_1, g_0, g_1, kv_ref, _qs, _gs, _ks, _vs, _stats,
    qs_ref, gs_ref, ks_ref, vs_ref, stats_ref, meta_ref,
):
    heads = KV_HEADS // CORES
    payload = kv_ref[0:16, 2 * heads * HEAD_DIM :].astype(jnp.float32)
    meta_ref[...] = payload[0:8]

    def pieces(h):
        def piece(ref, at):
            return ref[:, at : at + HEAD_DIM]

        spots = range(0, LANES, HEAD_DIM)
        at = h * HEAD_DIM
        return (
            [piece((q_0, q_1)[h], n) for n in spots], [piece((g_0, g_1)[h], n) for n in spots],
            piece(kv_ref, at), piece(kv_ref, at + heads * HEAD_DIM),
        )

    near_jobs(1, payload[0:1, 64:65], pieces, qs_ref, gs_ref, ks_ref, vs_ref, stats_ref)


def advantages(own_meta, swap_meta, extra):
    rows = extra.shape[0]
    members = 16
    unit = 1.0 / (BUCKETS - 1)
    sums = jnp.sum(extra.astype(jnp.float32), axis=0, keepdims=True)[:, 0:1]
    mean = sums * (unit / rows)
    own = own_meta[:, 0:1] * unit - mean
    other = swap_meta[:, 0:1] * unit - mean
    return own, other


def far_jobs(
    first, last, own_meta_ref, meta_ref, near_ref, gathered_ref, qs_ref, gs_ref,
    slopes_out, stats_out, send_ref, acc_ref, slopes_ref, stats_ref, probs_ref, sems,
):
    width = KV_HEADS // CORES * HEAD_DIM
    own_scale, other_scale = advantages(
        own_meta_ref[0:1], meta_ref[0:1], gathered_ref[:, 2 * width :]
    )

    def saves(i):
        return (
            pltpu.make_async_copy(slopes_ref.at[i], slopes_out.at[i], sems.at[0, i]),
            pltpu.make_async_copy(stats_ref.at[i], stats_out.at[i], sems.at[1, i]),
        )

    def job(i, _):
        h, r = i // CORES, i % CORES
        keys = gathered_ref[:, pl.ds(pl.multiple_of(h * HEAD_DIM, HEAD_DIM), HEAD_DIM)]
        values = gathered_ref[:, pl.ds(pl.multiple_of(width + h * HEAD_DIM, HEAD_DIM), HEAD_DIM)]
        scores = dot_nt(keys, qs_ref[i]) * EXP2_SCALE
        dprobs = dot_nt(values, gs_ref[i])
        near_top = near_ref[i, 0:1]
        top = jnp.maximum(jnp.max(scores, axis=0, keepdims=True), near_top)
        shift = jnp.exp2(near_top - top)
        terms = jnp.exp2(scores - top)
        total = jnp.sum(terms, axis=0, keepdims=True) + near_ref[i, 1:2] * shift
        delta = jnp.sum(terms * dprobs, axis=0, keepdims=True) + near_ref[i, 2:3] * shift
        inverse = 1.0 / total
        delta = delta * inverse
        probs = terms * inverse
        probs_ref[...] = probs.astype(jnp.bfloat16)
        slopes_ref[i] = (probs * (dprobs - delta)).astype(jnp.bfloat16)
        stats_ref[i, 0:1] = top
        stats_ref[i, 1:2] = inverse
        stats_ref[i, 2:3] = delta
        for copy in saves(i):
            copy.start()
        scale = jnp.where(r == 0, own_scale, other_scale)
        key_part = dot_nn(slopes_ref[i], qs_ref[i]) * (scale * SCALE)
        value_part = dot_nn(probs_ref[...], gs_ref[i]) * scale

        @pl.when(r == 0)
        def _():
            acc_ref[0], acc_ref[1] = key_part, value_part

        @pl.when(r == 1)
        def _():
            send_ref[h, 0] = (acc_ref[0] + key_part).astype(jnp.bfloat16)
            send_ref[h, 1] = (acc_ref[1] + value_part).astype(jnp.bfloat16)

        return 0

    def drain(i, _):
        for copy in saves(i):
            copy.wait()
        return 0

    lax.fori_loop(first, last, job, 0)
    lax.fori_loop(first, last, drain, 0)


def jobs_before():
    z = lax.axis_index("dp") // 2
    return jnp.where(z < 2, 2, jnp.where(z < 4, 1, 0))


def first_far_kernel(
    own_meta_ref, meta_ref, near_ref, gathered_ref, _qs, _gs, _ks, _vs,
    slopes_out, stats_out, send_ref, acc_ref, qs_ref, gs_ref, _ks_out, _vs_out, *scratch,
):
    far_jobs(
        0, jobs_before(), own_meta_ref, meta_ref, near_ref, gathered_ref, qs_ref, gs_ref,
        slopes_out, stats_out, send_ref, acc_ref, *scratch,
    )


def second_far_kernel(
    own_meta_ref, meta_ref, near_ref, gathered_ref, _slopes, _stats,
    _send, _acc, _qs, _gs, _ks, _vs,
    slopes_out, stats_out, send_ref, acc_ref, qs_ref, gs_ref, _ks_out, _vs_out, *scratch,
):
    far_jobs(
        jobs_before(), KV_HEADS, own_meta_ref, meta_ref, near_ref, gathered_ref, qs_ref, gs_ref,
        slopes_out, stats_out, send_ref, acc_ref, *scratch,
    )


def part_kernel(tokens_ref, send_ref, part_ref, payload_ref, sems):
    heads = send_ref.shape[0]
    copies = []
    for h in range(heads):
        for n in range(2):
            at = (n * heads + h) * HEAD_DIM
            copies.append((send_ref.at[h, n], at))
    tokens = jnp.broadcast_to(tokens_ref[0:1, HEAD_DIM // 2 : HEAD_DIM // 2 + 1], (1, HEAD_DIM))
    high = jnp.floor(tokens * (1.0 / 256.0))
    lanes = lax.broadcasted_iota(jnp.int32, tokens.shape, 1)
    tokens = jnp.where(lanes < HEAD_DIM // 2, high, tokens - high * 256.0)
    payload_ref[...] = jnp.broadcast_to(tokens, payload_ref.shape).astype(jnp.bfloat16)
    copies.append((payload_ref, 2 * heads * HEAD_DIM))
    copies = [
        pltpu.make_async_copy(source, part_ref.at[:, pl.ds(at, HEAD_DIM)], sems.at[n])
        for n, (source, at) in enumerate(copies)
    ]
    for copy in copies:
        copy.start()
    for copy in copies:
        copy.wait()


def own_kernel(
    qs_ref, gs_ref, ks_ref, vs_ref, gathered_ref, slopes_in, stats_in, own_out, swap_0, swap_1, swap_kv, own_ref, slopes_ref, stats_ref, sems, out_sems,
):
    heads = KV_HEADS // CORES
    slots = ks_ref.shape[1]
    loads = {}
    for r in (1, 0):
        for h in range(heads):
            i = h * CORES + r
            loads[i] = (
                pltpu.make_async_copy(slopes_in.at[i], slopes_ref.at[i], sems.at[0, i]),
                pltpu.make_async_copy(stats_in.at[i], stats_ref.at[i], sems.at[1, i]),
            )
            for load in loads[i]:
                load.start()
    copies = []
    for r in (1, 0):
        for h in range(heads):
            i = h * CORES + r
            if r:
                gq_ref, gq_at, kv_ref, kv_at = (swap_0, swap_1)[h], 0, swap_kv, 0
            else:
                gq_ref, gq_at, kv_ref, kv_at = own_ref, h * LANES, own_ref, heads * LANES
            queries, grads = qs_ref[i], gs_ref[i]
            keys, values = ks_ref[i], vs_ref[i]
            scores = causal(dot_nt(keys, queries) * EXP2_SCALE)
            dprobs = dot_nt(values, grads)
            loads[i][1].wait()
            top, inverse, delta = stats_ref[i, 0:1], stats_ref[i, 1:2], stats_ref[i, 2:3]
            probs = jnp.exp2(scores - top) * inverse
            slopes = (probs * (dprobs - delta)).astype(jnp.bfloat16)
            far_keys = gathered_ref[:, h * HEAD_DIM : (h + 1) * HEAD_DIM]
            loads[i][0].wait()
            gq = dot_tn(far_keys, slopes_ref[i]) + dot_tn(keys, slopes)
            for n in range(GROUP_HEADS):
                at = gq_at + n * HEAD_DIM
                gq_ref[:, at : at + HEAD_DIM] = gq[:, n * slots : (n + 1) * slots].T.astype(
                    jnp.bfloat16
                )
            at = kv_at + h * HEAD_DIM
            kv_ref[:, at : at + HEAD_DIM] = dot_nn(slopes, queries).astype(jnp.bfloat16)
            at += heads * HEAD_DIM
            kv_ref[:, at : at + HEAD_DIM] = dot_nn(probs.astype(jnp.bfloat16), grads).astype(
                jnp.bfloat16
            )
    copy = pltpu.make_async_copy(own_ref, own_out, out_sems.at[0])
    copy.start()
    copy.wait()


def finish_kernel(
    own_meta_ref, meta_ref, gathered_ref, recv_ref, own_in, swap_0, swap_1, swap_kv,
    gq_out, gk_out, gv_out, far_k_out, far_v_out,
    own_ref, gq_ref, gk_ref, gv_ref, far_k_ref, far_v_ref, in_sem, sems,
):
    load = pltpu.make_async_copy(own_in, own_ref, in_sem.at[0])
    load.start()
    core = lax.axis_index("group") % CORES
    members = recv_ref.shape[0]
    width = gk_ref.shape[1] // CORES
    slots = own_ref.shape[0]
    wide = gq_ref.shape[1] // CORES
    advantage, _ = advantages(own_meta_ref[0:1], meta_ref[0:1], gathered_ref[:, 2 * width :])
    tokens = jnp.sum(recv_ref[:, 0:1, 2 * width :].astype(jnp.float32), axis=0)
    token_total = tokens[:, 0:1] * 256.0 + tokens[:, HEAD_DIM // 2 : HEAD_DIM // 2 + 1]
    norm = (16 * 16 * slots) / token_total
    factor = advantage * norm
    copies = []

    def put(ref, at, value, scale):
        cols = pl.ds(pl.multiple_of(at, HEAD_DIM), value.shape[1])
        ref[:, cols] = (value.astype(jnp.float32) * scale).astype(jnp.bfloat16)

    def send(source, to):
        copies.append(pltpu.make_async_copy(source, to, sems.at[len(copies)]))
        copies[-1].start()

    def put_queries(at, value):
        put(gq_ref, at, value, factor * SCALE)
        cols = pl.ds(pl.multiple_of(at, HEAD_DIM), value.shape[1])
        send(gq_ref.at[:, cols], gq_out.at[:, cols])

    other = 1 - core
    put_queries(other * wide, swap_0[...])
    put_queries(other * wide + LANES, swap_1[...])
    put(gk_ref, other * width, swap_kv[:, :width], factor * SCALE)
    put(gv_ref, other * width, swap_kv[:, width:], factor)
    for c in range(CORES):
        total = recv_ref[c, :, : 2 * width].astype(jnp.float32)
        for m in range(c + CORES, members, CORES):
            total = total + recv_ref[m, :, : 2 * width].astype(jnp.float32)
        total = total * norm
        far_k_ref[:, c * width : (c + 1) * width] = total[:, :width].astype(jnp.bfloat16)
        far_v_ref[:, c * width : (c + 1) * width] = total[:, width:].astype(jnp.bfloat16)
    send(far_k_ref, far_k_out)
    send(far_v_ref, far_v_out)
    load.wait()
    put_queries(core * wide, own_ref[:, :LANES])
    put_queries(core * wide + LANES, own_ref[:, LANES:wide])
    put(gk_ref, core * width, own_ref[:, wide : wide + width], factor * SCALE)
    put(gv_ref, core * width, own_ref[:, wide + width :], factor)
    send(gk_ref, gk_out)
    send(gv_ref, gv_out)
    for copy in copies:
        copy.wait()


def vmem():
    return pl.BlockSpec(memory_space=pltpu.VMEM)


def anywhere():
    return pl.BlockSpec(memory_space=pl.ANY)


def near_memory(x):
    return pltpu.with_memory_space_constraint(x, pltpu.VMEM)


def far_memory(x):
    return pltpu.with_memory_space_constraint(x, pltpu.HBM)


def call(kernel, in_specs, out_specs, out_shape, flops, nbytes, scratch=(), aliases=None):
    return pl.pallas_call(
        kernel,
        in_specs=in_specs,
        out_specs=out_specs,
        out_shape=out_shape,
        scratch_shapes=list(scratch),
        input_output_aliases=aliases or {},
        compiler_params=pltpu.CompilerParams(vmem_limit_bytes=VMEM),
        cost_estimate=pl.CostEstimate(flops=flops, bytes_accessed=nbytes, transcendentals=0),
    )


def body(
    prefix_keys, prefix_values, resp_queries, resp_keys, resp_values, grad_out, lengths, buckets
):
    slots = resp_queries.shape[2]
    own_rows = prefix_keys.shape[1]
    members = lax.axis_size("group")
    rows = own_rows * members
    heads = KV_HEADS // CORES
    width = heads * HEAD_DIM
    wide = heads * LANES
    jobs = heads * CORES
    q, g = resp_queries[0, 0], grad_out[0, 0]
    kn, vn = resp_keys[0, 0], resp_values[0, 0]
    f32, bf16 = jnp.float32, jnp.bfloat16
    pairs = [(i, i ^ 1) for i in range(members)]

    meta = jnp.pad(buckets.astype(f32), ((0, 7), (0, HEAD_DIM - 1)))
    meta += jnp.pad(lengths.astype(f32), ((0, 7), (HEAD_DIM // 2, HEAD_DIM // 2 - 1)))
    spread = call(
        spread_kernel,
        [anywhere(), anywhere(), vmem()],
        anywhere(),
        pltpu.HBM((members, own_rows, 2 * width + HEAD_DIM), bf16),
        0, 1 << 20,
        [pltpu.VMEM((CORES, own_rows, 2 * width + HEAD_DIM), bf16),
         pltpu.SemaphoreType.DMA((4,)), pltpu.SemaphoreType.DMA((members,))],
    )(far_memory(prefix_keys[0]), far_memory(prefix_values[0]), near_memory(meta))
    gathered3 = lax.all_to_all(spread, "group", 0, 0, tiled=True)
    gathered = gathered3.reshape(rows, -1)

    swap = call(
        swap_kernel,
        [anywhere()] * 5 + [vmem()],
        [vmem()] * 5,
        [pltpu.VMEM((slots, LANES), bf16)] * 4 + [pltpu.VMEM((slots, 2 * width + HEAD_DIM), bf16)],
        0, 2 << 20,
        [pltpu.SemaphoreType.DMA((6,))],
    )(*(far_memory(x) for x in (q, g, kn, vn, spread)), near_memory(meta))
    swapped = [lax.ppermute(x, "group", pairs) for x in swap]

    near_shapes = [
        pltpu.VMEM((jobs, LANES, HEAD_DIM), bf16), pltpu.VMEM((jobs, LANES, HEAD_DIM), bf16),
        pltpu.VMEM((jobs, slots, HEAD_DIM), bf16), pltpu.VMEM((jobs, slots, HEAD_DIM), bf16),
        pltpu.VMEM((jobs, 8, LANES), f32),
    ]
    nears = call(
        near_own_kernel,
        [anywhere()] * 5 + [vmem()],
        [vmem()] * 5,
        near_shapes,
        2 * 4096 * 128 * 128, 2 << 20,
        [pltpu.VMEM((slots, 2 * wide + 2 * width), bf16), pltpu.SemaphoreType.DMA((4,))],
    )(*(far_memory(x) for x in (q, g, kn, vn, spread)), near_memory(meta))
    qs, gs, ks, vs, near, meta_in = call(
        near_other_kernel,
        [vmem()] * 10,
        [vmem()] * 6,
        near_shapes + [pltpu.VMEM((8, HEAD_DIM), f32)],
        2 * 4096 * 128 * 128, 2 << 20,
        (),
        {5 + n: n for n in range(5)},
    )(*(near_memory(x) for x in (*swapped, *nears)))

    kept = (qs, gs, ks, vs)
    shared = [near_memory(x) for x in (meta, meta_in, near, gathered)]
    saved_shapes = [pltpu.HBM((jobs, rows, LANES), bf16), pltpu.HBM((jobs, 8, LANES), f32)]
    kept_shapes = [pltpu.VMEM((heads, 2, rows, HEAD_DIM), bf16),
                   pltpu.VMEM((2, rows, HEAD_DIM), f32)]
    kept_shapes += [pltpu.VMEM(x.shape, x.dtype) for x in kept]
    scratch = [pltpu.VMEM((jobs, rows, LANES), bf16), pltpu.VMEM((jobs, 8, LANES), f32),
               pltpu.VMEM((rows, LANES), bf16), pltpu.SemaphoreType.DMA((2, jobs))]
    slopes, stats, *kept = call(
        first_far_kernel,
        [vmem()] * 8,
        [anywhere()] * 2 + [vmem()] * 6,
        saved_shapes + kept_shapes,
        2 * 2 * 4096 * 384 * 128, 4 << 20,
        scratch,
        {4 + n: 4 + n for n in range(4)},
    )(*shared, *(near_memory(x) for x in kept))

    dp = lax.axis_size("dp")
    payload, _ = lax.optimization_barrier((gathered3, stats))
    tokens = jnp.sum(payload[:, :8, 2 * width :].astype(f32), axis=0)
    turns = (0, 4, 9, 7, 15, 11, 1, 12, 2, 14, 6, 10, 8, 3, 13, 5)
    pairs_dp = [
        (d * members + i, (d ^ turns[i % dp]) * members + i)
        for d in range(dp)
        for i in range(members)
    ]
    tokens = lax.ppermute(tokens, ("dp", "group"), pairs_dp)

    slopes, stats, send, _, *kept = call(
        second_far_kernel,
        [vmem()] * 4 + [anywhere()] * 2 + [vmem()] * 6,
        [anywhere()] * 2 + [vmem()] * 6,
        saved_shapes + kept_shapes,
        2 * 2 * 4096 * 384 * 128, 4 << 20,
        scratch,
        {4 + n: n for n in range(8)},
    )(*shared, far_memory(slopes), far_memory(stats), *(near_memory(x) for x in kept))

    part = call(
        part_kernel,
        [vmem()] * 2,
        anywhere(),
        pltpu.HBM((rows, 2 * width + HEAD_DIM), bf16),
        0, 1 << 19,
        [pltpu.VMEM((rows, HEAD_DIM), bf16), pltpu.SemaphoreType.DMA((2 * heads + 1,))],
    )(near_memory(tokens), near_memory(send))

    recv = lax.all_to_all(part.reshape(members, own_rows, -1), "group", 0, 0, tiled=True)

    own, *swap_out = call(
        own_kernel,
        [vmem()] * 5 + [anywhere()] * 2,
        [anywhere()] + [vmem()] * 3,
        [pltpu.HBM((slots, wide + 2 * width), bf16), pltpu.VMEM((slots, LANES), bf16),
         pltpu.VMEM((slots, LANES), bf16), pltpu.VMEM((slots, 2 * width), bf16)],
        3 * 2 * 4096 * 512 * 128, 8 << 20,
        [pltpu.VMEM((slots, wide + 2 * width), bf16), pltpu.VMEM((jobs, rows, LANES), bf16),
         pltpu.VMEM((jobs, 8, LANES), f32), pltpu.SemaphoreType.DMA((2, jobs)),
         pltpu.SemaphoreType.DMA((1,))],
    )(*(near_memory(x) for x in (*kept, gathered)), far_memory(slopes), far_memory(stats))
    swap_in = [lax.ppermute(x, "group", pairs) for x in swap_out]

    outs = call(
        finish_kernel,
        [vmem()] * 4 + [anywhere()] + [vmem()] * 3,
        [anywhere()] * 5,
        [pltpu.HBM((slots, HEADS * HEAD_DIM), bf16),
         pltpu.HBM((slots, CORES * width), bf16), pltpu.HBM((slots, CORES * width), bf16),
         pltpu.HBM((own_rows, CORES * width), bf16), pltpu.HBM((own_rows, CORES * width), bf16)],
        0, 4 << 20,
        [pltpu.VMEM((slots, wide + 2 * width), bf16), pltpu.VMEM((slots, HEADS * HEAD_DIM), bf16),
         pltpu.VMEM((slots, CORES * width), bf16), pltpu.VMEM((slots, CORES * width), bf16),
         pltpu.VMEM((own_rows, CORES * width), bf16), pltpu.VMEM((own_rows, CORES * width), bf16),
         pltpu.SemaphoreType.DMA((1,)), pltpu.SemaphoreType.DMA((8,))],
    )(*(near_memory(x) for x in (meta, meta_in, gathered, recv)),
      far_memory(own), *(near_memory(x) for x in swap_in))
    gq, gk, gv, far_k, far_v = outs
    return gq[None, None], gk[None, None], gv[None, None], far_k[None], far_v[None]


def solution(mesh):
    in_specs = (
        P("dp", "group", None),
        P("dp", "group", None),
        P("dp", "group", None, None),
        P("dp", "group", None, None),
        P("dp", "group", None, None),
        P("dp", "group", None, None),
        P("dp", "group"),
        P("dp", "group"),
    )
    out_specs = (
        P("dp", "group", None, None),
        P("dp", "group", None, None),
        P("dp", "group", None, None),
        P("dp", "group", None),
        P("dp", "group", None),
    )
    return jax.shard_map(body, mesh=mesh, in_specs=in_specs, out_specs=out_specs, check_vma=False)
```

```python
import functools
import math

import jax
import jax.numpy as jnp
from jax import lax
from jax.experimental import pallas as pl
from jax.experimental.pallas import tpu as pltpu
from jax.sharding import PartitionSpec as P

HEADS = 32
KV_HEADS = 4
HEAD_DIM = 128
BUCKETS = 5
GROUP_HEADS = HEADS // KV_HEADS
LANES = GROUP_HEADS * HEAD_DIM
SCALE = 1.0 / math.sqrt(HEAD_DIM)
EXP2_SCALE = SCALE * math.log2(math.e)
VMEM = 16 * 1024 * 1024
CORES = 2


def dot_nt(a, b):
    return lax.dot_general(a, b, (((1,), (1,)), ((), ())), preferred_element_type=jnp.float32)


def dot_nn(a, b):
    return lax.dot_general(a, b, (((1,), (0,)), ((), ())), preferred_element_type=jnp.float32)


def dot_tn(a, b):
    return lax.dot_general(a, b, (((0,), (0,)), ((), ())), preferred_element_type=jnp.float32)


def causal(scores):
    slots = scores.shape[0]
    keys = lax.broadcasted_iota(jnp.int32, scores.shape, 0)
    queries = lax.broadcasted_iota(jnp.int32, scores.shape, 1) % slots
    return jnp.where(keys <= queries, scores, -jnp.inf)


def spread_kernel(k_ref, v_ref, meta_ref, out_ref, send_ref, in_sems, sems):
    half = k_ref.shape[1] // CORES
    loads = []
    for c in range(CORES):
        for n, ref in enumerate((k_ref, v_ref)):
            loads.append(
                pltpu.make_async_copy(
                    ref.at[:, pl.ds(c * half, half)],
                    send_ref.at[c, :, pl.ds(n * half, half)],
                    in_sems.at[2 * c + n],
                )
            )
            loads[-1].start()
    payload = jnp.broadcast_to(meta_ref[0:1], (k_ref.shape[0], HEAD_DIM)).astype(jnp.bfloat16)
    copies = []
    for c in range(CORES):
        send_ref[c, :, 2 * half :] = payload
        loads[2 * c].wait()
        loads[2 * c + 1].wait()
        for m in range(c, out_ref.shape[0], CORES):
            copies.append(pltpu.make_async_copy(send_ref.at[c], out_ref.at[m], sems.at[m]))
            copies[-1].start()
    for copy in copies:
        copy.wait()


def swap_kernel(q_ref, g_ref, k_ref, v_ref, _after, meta_ref, q_0, q_1, g_0, g_1, kv_ref, sems):
    other = 1 - lax.axis_index("group") % CORES
    copies = []
    for ref, outs in ((q_ref, (q_0, q_1)), (g_ref, (g_0, g_1))):
        for h, out in enumerate(outs):
            at = pl.multiple_of((other * len(outs) + h) * LANES, LANES)
            copies.append((ref.at[:, pl.ds(at, LANES)], out))
    half = k_ref.shape[1] // CORES
    cols = pl.ds(pl.multiple_of(other * half, half), half)
    copies.append((k_ref.at[:, cols], kv_ref.at[:, pl.ds(0, half)]))
    copies.append((v_ref.at[:, cols], kv_ref.at[:, pl.ds(half, half)]))
    copies = [pltpu.make_async_copy(a, b, sems.at[n]) for n, (a, b) in enumerate(copies)]
    for copy in copies:
        copy.start()
    payload = jnp.broadcast_to(meta_ref[0:1], (kv_ref.shape[0], HEAD_DIM))
    kv_ref[:, 2 * half :] = payload.astype(jnp.bfloat16)
    for copy in copies:
        copy.wait()


def near_jobs(r, length, pieces, qs_ref, gs_ref, ks_ref, vs_ref, stats_ref):
    slots = ks_ref.shape[1]
    rows = lax.broadcasted_iota(jnp.int32, (slots, HEAD_DIM), 0).astype(jnp.float32)
    mask = jnp.where(rows < length, 1.0, 0.0).astype(jnp.bfloat16)
    for h in range(KV_HEADS // CORES):
        i = h * CORES + r
        q_parts, g_parts, keys, values = pieces(h)
        queries = jnp.concatenate(q_parts, axis=0)
        grads = jnp.concatenate([g * mask for g in g_parts], axis=0)
        qs_ref[i], gs_ref[i], ks_ref[i], vs_ref[i] = queries, grads, keys, values
        scores = causal(dot_nt(keys, queries) * EXP2_SCALE)
        dprobs = dot_nt(values, grads)
        top = jnp.max(scores, axis=0, keepdims=True)
        terms = jnp.exp2(scores - top)
        stats_ref[i, 0:1] = top
        stats_ref[i, 1:2] = jnp.sum(terms, axis=0, keepdims=True)
        stats_ref[i, 2:3] = jnp.sum(terms * dprobs, axis=0, keepdims=True)


def near_own_kernel(
    own_q, own_g, own_k, own_v, _after, meta_ref,
    qs_ref, gs_ref, ks_ref, vs_ref, stats_ref, held_ref, sems,
):
    core = lax.axis_index("group") % CORES
    heads = KV_HEADS // CORES
    wide = heads * LANES
    at, copies = 0, []
    for i, ref in enumerate((own_q, own_g, own_k, own_v)):
        half = ref.shape[1] // CORES
        cols = pl.ds(pl.multiple_of(core * half, half), half)
        to = held_ref.at[:, pl.ds(at, half)]
        copies.append(pltpu.make_async_copy(ref.at[:, cols], to, sems.at[i]))
        copies[-1].start()
        at += half
    for copy in copies:
        copy.wait()

    def pieces(h):
        def piece(at):
            return held_ref[:, at : at + HEAD_DIM]

        spots = range(h * LANES, (h + 1) * LANES, HEAD_DIM)
        at = 2 * wide + h * HEAD_DIM
        return (
            [piece(n) for n in spots], [piece(wide + n) for n in spots],
            piece(at), piece(at + heads * HEAD_DIM),
        )

    near_jobs(0, meta_ref[0:1, 64:65], pieces, qs_ref, gs_ref, ks_ref, vs_ref, stats_ref)


def near_other_kernel(
    q_0, q_1, g_0, g_1, kv_ref, _qs, _gs, _ks, _vs, _stats,
    qs_ref, gs_ref, ks_ref, vs_ref, stats_ref, meta_ref,
):
    heads = KV_HEADS // CORES
    payload = kv_ref[0:16, 2 * heads * HEAD_DIM :].astype(jnp.float32)
    meta_ref[...] = payload[0:8]

    def pieces(h):
        def piece(ref, at):
            return ref[:, at : at + HEAD_DIM]

        spots = range(0, LANES, HEAD_DIM)
        at = h * HEAD_DIM
        return (
            [piece((q_0, q_1)[h], n) for n in spots], [piece((g_0, g_1)[h], n) for n in spots],
            piece(kv_ref, at), piece(kv_ref, at + heads * HEAD_DIM),
        )

    near_jobs(1, payload[0:1, 64:65], pieces, qs_ref, gs_ref, ks_ref, vs_ref, stats_ref)


def advantages(own_meta, swap_meta, extra):
    rows = extra.shape[0]
    members = 16
    unit = 1.0 / (BUCKETS - 1)
    sums = jnp.sum(extra.astype(jnp.float32), axis=0, keepdims=True)[:, 0:1]
    mean = sums * (unit / rows)
    own = own_meta[:, 0:1] * unit - mean
    other = swap_meta[:, 0:1] * unit - mean
    return own, other


def far_jobs(
    first, last, own_meta_ref, meta_ref, near_ref, gathered_ref, qs_ref, gs_ref,
    slopes_out, stats_out, send_ref, acc_ref, slopes_ref, stats_ref, probs_ref, sems,
):
    width = KV_HEADS // CORES * HEAD_DIM
    own_scale, other_scale = advantages(
        own_meta_ref[0:1], meta_ref[0:1], gathered_ref[:, 2 * width :]
    )

    def saves(i):
        return (
            pltpu.make_async_copy(slopes_ref.at[i], slopes_out.at[i], sems.at[0, i]),
            pltpu.make_async_copy(stats_ref.at[i], stats_out.at[i], sems.at[1, i]),
        )

    def job(i, _):
        h, r = i // CORES, i % CORES
        keys = gathered_ref[:, pl.ds(pl.multiple_of(h * HEAD_DIM, HEAD_DIM), HEAD_DIM)]
        values = gathered_ref[:, pl.ds(pl.multiple_of(width + h * HEAD_DIM, HEAD_DIM), HEAD_DIM)]
        scores = dot_nt(keys, qs_ref[i]) * EXP2_SCALE
        dprobs = dot_nt(values, gs_ref[i])
        near_top = near_ref[i, 0:1]
        top = jnp.maximum(jnp.max(scores, axis=0, keepdims=True), near_top)
        shift = jnp.exp2(near_top - top)
        terms = jnp.exp2(scores - top)
        total = jnp.sum(terms, axis=0, keepdims=True) + near_ref[i, 1:2] * shift
        delta = jnp.sum(terms * dprobs, axis=0, keepdims=True) + near_ref[i, 2:3] * shift
        inverse = 1.0 / total
        delta = delta * inverse
        probs = terms * inverse
        probs_ref[...] = probs.astype(jnp.bfloat16)
        slopes_ref[i] = (probs * (dprobs - delta)).astype(jnp.bfloat16)
        stats_ref[i, 0:1] = top
        stats_ref[i, 1:2] = inverse
        stats_ref[i, 2:3] = delta
        for copy in saves(i):
            copy.start()
        scale = jnp.where(r == 0, own_scale, other_scale)
        key_part = dot_nn(slopes_ref[i], qs_ref[i]) * (scale * SCALE)
        value_part = dot_nn(probs_ref[...], gs_ref[i]) * scale

        @pl.when(r == 0)
        def _():
            acc_ref[0], acc_ref[1] = key_part, value_part

        @pl.when(r == 1)
        def _():
            send_ref[h, 0] = (acc_ref[0] + key_part).astype(jnp.bfloat16)
            send_ref[h, 1] = (acc_ref[1] + value_part).astype(jnp.bfloat16)

        return 0

    def drain(i, _):
        for copy in saves(i):
            copy.wait()
        return 0

    lax.fori_loop(first, last, job, 0)
    lax.fori_loop(first, last, drain, 0)


def jobs_before():
    z = lax.axis_index("dp") // 2
    return jnp.where(z < 2, 2, jnp.where(z < 4, 1, 0))


def first_far_kernel(
    own_meta_ref, meta_ref, near_ref, gathered_ref, _qs, _gs, _ks, _vs,
    slopes_out, stats_out, send_ref, acc_ref, qs_ref, gs_ref, _ks_out, _vs_out, *scratch,
):
    far_jobs(
        0, jobs_before(), own_meta_ref, meta_ref, near_ref, gathered_ref, qs_ref, gs_ref,
        slopes_out, stats_out, send_ref, acc_ref, *scratch,
    )


def second_far_kernel(
    own_meta_ref, meta_ref, near_ref, gathered_ref, _slopes, _stats,
    _send, _acc, _qs, _gs, _ks, _vs,
    slopes_out, stats_out, send_ref, acc_ref, qs_ref, gs_ref, _ks_out, _vs_out, *scratch,
):
    far_jobs(
        jobs_before(), KV_HEADS, own_meta_ref, meta_ref, near_ref, gathered_ref, qs_ref, gs_ref,
        slopes_out, stats_out, send_ref, acc_ref, *scratch,
    )


def part_kernel(
    tokens_ref, send_ref, own_meta_ref, meta_ref, gathered_ref, part_ref, adv_ref, payload_ref, sems
):
    heads = send_ref.shape[0]
    copies = []
    for h in range(heads):
        for n in range(2):
            at = (n * heads + h) * HEAD_DIM
            copies.append((send_ref.at[h, n], at))
    tokens = jnp.broadcast_to(tokens_ref[0:1, HEAD_DIM // 2 : HEAD_DIM // 2 + 1], (1, HEAD_DIM))
    high = jnp.floor(tokens * (1.0 / 256.0))
    lanes = lax.broadcasted_iota(jnp.int32, tokens.shape, 1)
    tokens = jnp.where(lanes < HEAD_DIM // 2, high, tokens - high * 256.0)
    payload_ref[...] = jnp.broadcast_to(tokens, payload_ref.shape).astype(jnp.bfloat16)
    copies.append((payload_ref, 2 * heads * HEAD_DIM))
    copies = [
        pltpu.make_async_copy(source, part_ref.at[:, pl.ds(at, HEAD_DIM)], sems.at[n])
        for n, (source, at) in enumerate(copies)
    ]
    for copy in copies:
        copy.start()
    width = heads * HEAD_DIM
    own, _ = advantages(own_meta_ref[0:1], meta_ref[0:1], gathered_ref[:, 2 * width :])
    adv_ref[...] = jnp.broadcast_to(own, adv_ref.shape)
    for copy in copies:
        copy.wait()


def own_kernel(
    qs_ref, gs_ref, ks_ref, vs_ref, gathered_ref, slopes_in, stats_in, own_out, swap_0, swap_1, swap_kv, own_ref, slopes_ref, stats_ref, sems, out_sems,
):
    heads = KV_HEADS // CORES
    slots = ks_ref.shape[1]
    loads = {}
    for r in (1, 0):
        for h in range(heads):
            i = h * CORES + r
            loads[i] = (
                pltpu.make_async_copy(slopes_in.at[i], slopes_ref.at[i], sems.at[0, i]),
                pltpu.make_async_copy(stats_in.at[i], stats_ref.at[i], sems.at[1, i]),
            )
            for load in loads[i]:
                load.start()
    copies = []
    for r in (1, 0):
        for h in range(heads):
            i = h * CORES + r
            if r:
                gq_ref, gq_at, kv_ref, kv_at = (swap_0, swap_1)[h], 0, swap_kv, 0
            else:
                gq_ref, gq_at, kv_ref, kv_at = own_ref, h * LANES, own_ref, heads * LANES
            queries, grads = qs_ref[i], gs_ref[i]
            keys, values = ks_ref[i], vs_ref[i]
            scores = causal(dot_nt(keys, queries) * EXP2_SCALE)
            dprobs = dot_nt(values, grads)
            loads[i][1].wait()
            top, inverse, delta = stats_ref[i, 0:1], stats_ref[i, 1:2], stats_ref[i, 2:3]
            probs = jnp.exp2(scores - top) * inverse
            slopes = (probs * (dprobs - delta)).astype(jnp.bfloat16)
            far_keys = gathered_ref[:, h * HEAD_DIM : (h + 1) * HEAD_DIM]
            loads[i][0].wait()
            gq = dot_tn(far_keys, slopes_ref[i]) + dot_tn(keys, slopes)
            for n in range(GROUP_HEADS):
                at = gq_at + n * HEAD_DIM
                gq_ref[:, at : at + HEAD_DIM] = gq[:, n * slots : (n + 1) * slots].T.astype(
                    jnp.bfloat16
                )
            at = kv_at + h * HEAD_DIM
            kv_ref[:, at : at + HEAD_DIM] = dot_nn(slopes, queries).astype(jnp.bfloat16)
            at += heads * HEAD_DIM
            kv_ref[:, at : at + HEAD_DIM] = dot_nn(probs.astype(jnp.bfloat16), grads).astype(
                jnp.bfloat16
            )
    copy = pltpu.make_async_copy(own_ref, own_out, out_sems.at[0])
    copy.start()
    copy.wait()


def finish_kernel(
    adv_ref, recv_ref, own_in, swap_0, swap_1, swap_kv,
    gq_out, gk_out, gv_out, far_k_out, far_v_out,
    own_ref, gq_ref, gk_ref, gv_ref, far_k_ref, far_v_ref, in_sem, sems,
):
    load = pltpu.make_async_copy(own_in, own_ref, in_sem.at[0])
    load.start()
    core = lax.axis_index("group") % CORES
    members = recv_ref.shape[0]
    width = gk_ref.shape[1] // CORES
    slots = own_ref.shape[0]
    wide = gq_ref.shape[1] // CORES
    advantage = adv_ref[0:1, 0:1]
    tokens = jnp.sum(recv_ref[:, 0:1, 2 * width :].astype(jnp.float32), axis=0)
    token_total = tokens[:, 0:1] * 256.0 + tokens[:, HEAD_DIM // 2 : HEAD_DIM // 2 + 1]
    norm = (16 * 16 * slots) / token_total
    factor = advantage * norm
    copies = []

    def put(ref, at, value, scale):
        cols = pl.ds(pl.multiple_of(at, HEAD_DIM), value.shape[1])
        ref[:, cols] = (value.astype(jnp.float32) * scale).astype(jnp.bfloat16)

    def send(source, to):
        copies.append(pltpu.make_async_copy(source, to, sems.at[len(copies)]))
        copies[-1].start()

    def put_queries(at, value):
        put(gq_ref, at, value, factor * SCALE)
        cols = pl.ds(pl.multiple_of(at, HEAD_DIM), value.shape[1])
        send(gq_ref.at[:, cols], gq_out.at[:, cols])

    other = 1 - core
    put_queries(other * wide, swap_0[...])
    put_queries(other * wide + LANES, swap_1[...])
    put(gk_ref, other * width, swap_kv[:, :width], factor * SCALE)
    put(gv_ref, other * width, swap_kv[:, width:], factor)
    for c in range(CORES):
        total = recv_ref[c, :, : 2 * width].astype(jnp.float32)
        for m in range(c + CORES, members, CORES):
            total = total + recv_ref[m, :, : 2 * width].astype(jnp.float32)
        total = total * norm
        far_k_ref[:, c * width : (c + 1) * width] = total[:, :width].astype(jnp.bfloat16)
        far_v_ref[:, c * width : (c + 1) * width] = total[:, width:].astype(jnp.bfloat16)
    send(far_k_ref, far_k_out)
    send(far_v_ref, far_v_out)
    load.wait()
    put_queries(core * wide, own_ref[:, :LANES])
    put_queries(core * wide + LANES, own_ref[:, LANES:wide])
    put(gk_ref, core * width, own_ref[:, wide : wide + width], factor * SCALE)
    put(gv_ref, core * width, own_ref[:, wide + width :], factor)
    send(gk_ref, gk_out)
    send(gv_ref, gv_out)
    for copy in copies:
        copy.wait()


def vmem():
    return pl.BlockSpec(memory_space=pltpu.VMEM)


def anywhere():
    return pl.BlockSpec(memory_space=pl.ANY)


def near_memory(x):
    return pltpu.with_memory_space_constraint(x, pltpu.VMEM)


def far_memory(x):
    return pltpu.with_memory_space_constraint(x, pltpu.HBM)


def call(kernel, in_specs, out_specs, out_shape, flops, nbytes, scratch=(), aliases=None):
    return pl.pallas_call(
        kernel,
        in_specs=in_specs,
        out_specs=out_specs,
        out_shape=out_shape,
        scratch_shapes=list(scratch),
        input_output_aliases=aliases or {},
        compiler_params=pltpu.CompilerParams(vmem_limit_bytes=VMEM),
        cost_estimate=pl.CostEstimate(flops=flops, bytes_accessed=nbytes, transcendentals=0),
    )


def body(
    prefix_keys, prefix_values, resp_queries, resp_keys, resp_values, grad_out, lengths, buckets
):
    slots = resp_queries.shape[2]
    own_rows = prefix_keys.shape[1]
    members = lax.axis_size("group")
    rows = own_rows * members
    heads = KV_HEADS // CORES
    width = heads * HEAD_DIM
    wide = heads * LANES
    jobs = heads * CORES
    q, g = resp_queries[0, 0], grad_out[0, 0]
    kn, vn = resp_keys[0, 0], resp_values[0, 0]
    f32, bf16 = jnp.float32, jnp.bfloat16
    pairs = [(i, i ^ 1) for i in range(members)]

    meta = jnp.pad(buckets.astype(f32), ((0, 7), (0, HEAD_DIM - 1)))
    meta += jnp.pad(lengths.astype(f32), ((0, 7), (HEAD_DIM // 2, HEAD_DIM // 2 - 1)))
    spread = call(
        spread_kernel,
        [anywhere(), anywhere(), vmem()],
        anywhere(),
        pltpu.HBM((members, own_rows, 2 * width + HEAD_DIM), bf16),
        0, 1 << 20,
        [pltpu.VMEM((CORES, own_rows, 2 * width + HEAD_DIM), bf16),
         pltpu.SemaphoreType.DMA((4,)), pltpu.SemaphoreType.DMA((members,))],
    )(far_memory(prefix_keys[0]), far_memory(prefix_values[0]), near_memory(meta))
    gathered3 = lax.all_to_all(spread, "group", 0, 0, tiled=True)
    gathered = gathered3.reshape(rows, -1)

    swap = call(
        swap_kernel,
        [anywhere()] * 5 + [vmem()],
        [vmem()] * 5,
        [pltpu.VMEM((slots, LANES), bf16)] * 4 + [pltpu.VMEM((slots, 2 * width + HEAD_DIM), bf16)],
        0, 2 << 20,
        [pltpu.SemaphoreType.DMA((6,))],
    )(*(far_memory(x) for x in (q, g, kn, vn, spread)), near_memory(meta))
    swapped = [lax.ppermute(x, "group", pairs) for x in swap]

    near_shapes = [
        pltpu.VMEM((jobs, LANES, HEAD_DIM), bf16), pltpu.VMEM((jobs, LANES, HEAD_DIM), bf16),
        pltpu.VMEM((jobs, slots, HEAD_DIM), bf16), pltpu.VMEM((jobs, slots, HEAD_DIM), bf16),
        pltpu.VMEM((jobs, 8, LANES), f32),
    ]
    nears = call(
        near_own_kernel,
        [anywhere()] * 5 + [vmem()],
        [vmem()] * 5,
        near_shapes,
        2 * 4096 * 128 * 128, 2 << 20,
        [pltpu.VMEM((slots, 2 * wide + 2 * width), bf16), pltpu.SemaphoreType.DMA((4,))],
    )(*(far_memory(x) for x in (q, g, kn, vn, spread)), near_memory(meta))
    qs, gs, ks, vs, near, meta_in = call(
        near_other_kernel,
        [vmem()] * 10,
        [vmem()] * 6,
        near_shapes + [pltpu.VMEM((8, HEAD_DIM), f32)],
        2 * 4096 * 128 * 128, 2 << 20,
        (),
        {5 + n: n for n in range(5)},
    )(*(near_memory(x) for x in (*swapped, *nears)))

    kept = (qs, gs, ks, vs)
    shared = [near_memory(x) for x in (meta, meta_in, near, gathered)]
    saved_shapes = [pltpu.HBM((jobs, rows, LANES), bf16), pltpu.HBM((jobs, 8, LANES), f32)]
    kept_shapes = [pltpu.VMEM((heads, 2, rows, HEAD_DIM), bf16),
                   pltpu.VMEM((2, rows, HEAD_DIM), f32)]
    kept_shapes += [pltpu.VMEM(x.shape, x.dtype) for x in kept]
    scratch = [pltpu.VMEM((jobs, rows, LANES), bf16), pltpu.VMEM((jobs, 8, LANES), f32),
               pltpu.VMEM((rows, LANES), bf16), pltpu.SemaphoreType.DMA((2, jobs))]
    slopes, stats, *kept = call(
        first_far_kernel,
        [vmem()] * 8,
        [anywhere()] * 2 + [vmem()] * 6,
        saved_shapes + kept_shapes,
        2 * 2 * 4096 * 384 * 128, 4 << 20,
        scratch,
        {4 + n: 4 + n for n in range(4)},
    )(*shared, *(near_memory(x) for x in kept))

    dp = lax.axis_size("dp")
    payload, _ = lax.optimization_barrier((gathered3, stats))
    tokens = jnp.sum(payload[:, :8, 2 * width :].astype(f32), axis=0)
    turns = (0, 4, 9, 7, 15, 11, 1, 12, 2, 14, 6, 10, 8, 3, 13, 5)
    pairs_dp = [
        (d * members + i, (d ^ turns[i % dp]) * members + i)
        for d in range(dp)
        for i in range(members)
    ]
    tokens = lax.ppermute(tokens, ("dp", "group"), pairs_dp)

    slopes, stats, send, _, *kept = call(
        second_far_kernel,
        [vmem()] * 4 + [anywhere()] * 2 + [vmem()] * 6,
        [anywhere()] * 2 + [vmem()] * 6,
        saved_shapes + kept_shapes,
        2 * 2 * 4096 * 384 * 128, 4 << 20,
        scratch,
        {4 + n: n for n in range(8)},
    )(*shared, far_memory(slopes), far_memory(stats), *(near_memory(x) for x in kept))

    part, adv = call(
        part_kernel,
        [vmem()] * 5,
        [anywhere(), vmem()],
        [pltpu.HBM((rows, 2 * width + HEAD_DIM), bf16), pltpu.VMEM((8, HEAD_DIM), f32)],
        0, 1 << 19,
        [pltpu.VMEM((rows, HEAD_DIM), bf16), pltpu.SemaphoreType.DMA((2 * heads + 1,))],
    )(*(near_memory(x) for x in (tokens, send, meta, meta_in, gathered)))

    recv = lax.all_to_all(part.reshape(members, own_rows, -1), "group", 0, 0, tiled=True)

    own, *swap_out = call(
        own_kernel,
        [vmem()] * 5 + [anywhere()] * 2,
        [anywhere()] + [vmem()] * 3,
        [pltpu.HBM((slots, wide + 2 * width), bf16), pltpu.VMEM((slots, LANES), bf16),
         pltpu.VMEM((slots, LANES), bf16), pltpu.VMEM((slots, 2 * width), bf16)],
        3 * 2 * 4096 * 512 * 128, 8 << 20,
        [pltpu.VMEM((slots, wide + 2 * width), bf16), pltpu.VMEM((jobs, rows, LANES), bf16),
         pltpu.VMEM((jobs, 8, LANES), f32), pltpu.SemaphoreType.DMA((2, jobs)),
         pltpu.SemaphoreType.DMA((1,))],
    )(*(near_memory(x) for x in (*kept, gathered)), far_memory(slopes), far_memory(stats))
    swap_in = [lax.ppermute(x, "group", pairs) for x in swap_out]

    outs = call(
        finish_kernel,
        [vmem()] * 2 + [anywhere()] + [vmem()] * 3,
        [anywhere()] * 5,
        [pltpu.HBM((slots, HEADS * HEAD_DIM), bf16),
         pltpu.HBM((slots, CORES * width), bf16), pltpu.HBM((slots, CORES * width), bf16),
         pltpu.HBM((own_rows, CORES * width), bf16), pltpu.HBM((own_rows, CORES * width), bf16)],
        0, 4 << 20,
        [pltpu.VMEM((slots, wide + 2 * width), bf16), pltpu.VMEM((slots, HEADS * HEAD_DIM), bf16),
         pltpu.VMEM((slots, CORES * width), bf16), pltpu.VMEM((slots, CORES * width), bf16),
         pltpu.VMEM((own_rows, CORES * width), bf16), pltpu.VMEM((own_rows, CORES * width), bf16),
         pltpu.SemaphoreType.DMA((1,)), pltpu.SemaphoreType.DMA((8,))],
    )(*(near_memory(x) for x in (adv, recv)),
      far_memory(own), *(near_memory(x) for x in swap_in))
    gq, gk, gv, far_k, far_v = outs
    return gq[None, None], gk[None, None], gv[None, None], far_k[None], far_v[None]


def solution(mesh):
    in_specs = (
        P("dp", "group", None),
        P("dp", "group", None),
        P("dp", "group", None, None),
        P("dp", "group", None, None),
        P("dp", "group", None, None),
        P("dp", "group", None, None),
        P("dp", "group"),
        P("dp", "group"),
    )
    out_specs = (
        P("dp", "group", None, None),
        P("dp", "group", None, None),
        P("dp", "group", None, None),
        P("dp", "group", None),
        P("dp", "group", None),
    )
    return jax.shard_map(body, mesh=mesh, in_specs=in_specs, out_specs=out_specs, check_vma=False)
```

```python
import functools
import math

import jax
import jax.numpy as jnp
from jax import lax
from jax.experimental import pallas as pl
from jax.experimental.pallas import tpu as pltpu
from jax.sharding import PartitionSpec as P

HEADS = 32
KV_HEADS = 4
HEAD_DIM = 128
BUCKETS = 5
GROUP_HEADS = HEADS // KV_HEADS
LANES = GROUP_HEADS * HEAD_DIM
SCALE = 1.0 / math.sqrt(HEAD_DIM)
EXP2_SCALE = SCALE * math.log2(math.e)
VMEM = 16 * 1024 * 1024
CORES = 2


def dot_nt(a, b):
    return lax.dot_general(a, b, (((1,), (1,)), ((), ())), preferred_element_type=jnp.float32)


def dot_nn(a, b):
    return lax.dot_general(a, b, (((1,), (0,)), ((), ())), preferred_element_type=jnp.float32)


def dot_tn(a, b):
    return lax.dot_general(a, b, (((0,), (0,)), ((), ())), preferred_element_type=jnp.float32)


def causal(scores):
    slots = scores.shape[0]
    keys = lax.broadcasted_iota(jnp.int32, scores.shape, 0)
    queries = lax.broadcasted_iota(jnp.int32, scores.shape, 1) % slots
    return jnp.where(keys <= queries, scores, -jnp.inf)


def spread_kernel(k_ref, v_ref, meta_ref, out_ref, send_ref, in_sems, sems):
    half = k_ref.shape[1] // CORES
    loads = []
    for c in range(CORES):
        for n, ref in enumerate((k_ref, v_ref)):
            loads.append(
                pltpu.make_async_copy(
                    ref.at[:, pl.ds(c * half, half)],
                    send_ref.at[c, :, pl.ds(n * half, half)],
                    in_sems.at[2 * c + n],
                )
            )
            loads[-1].start()
    payload = jnp.broadcast_to(meta_ref[0:1], (k_ref.shape[0], HEAD_DIM)).astype(jnp.bfloat16)
    copies = []
    for c in range(CORES):
        send_ref[c, :, 2 * half :] = payload
        loads[2 * c].wait()
        loads[2 * c + 1].wait()
        for m in range(c, out_ref.shape[0], CORES):
            copies.append(pltpu.make_async_copy(send_ref.at[c], out_ref.at[m], sems.at[m]))
            copies[-1].start()
    for copy in copies:
        copy.wait()


def swap_kernel(q_ref, g_ref, k_ref, v_ref, _after, meta_ref, q_0, q_1, g_0, g_1, kv_ref, sems):
    other = 1 - lax.axis_index("group") % CORES
    copies = []
    for ref, outs in ((q_ref, (q_0, q_1)), (g_ref, (g_0, g_1))):
        for h, out in enumerate(outs):
            at = pl.multiple_of((other * len(outs) + h) * LANES, LANES)
            copies.append((ref.at[:, pl.ds(at, LANES)], out))
    half = k_ref.shape[1] // CORES
    cols = pl.ds(pl.multiple_of(other * half, half), half)
    copies.append((k_ref.at[:, cols], kv_ref.at[:, pl.ds(0, half)]))
    copies.append((v_ref.at[:, cols], kv_ref.at[:, pl.ds(half, half)]))
    copies = [pltpu.make_async_copy(a, b, sems.at[n]) for n, (a, b) in enumerate(copies)]
    for copy in copies:
        copy.start()
    payload = jnp.broadcast_to(meta_ref[0:1], (kv_ref.shape[0], HEAD_DIM))
    kv_ref[:, 2 * half :] = payload.astype(jnp.bfloat16)
    for copy in copies:
        copy.wait()


def near_jobs(r, length, pieces, qs_ref, gs_ref, ks_ref, vs_ref, stats_ref):
    slots = ks_ref.shape[1]
    rows = lax.broadcasted_iota(jnp.int32, (slots, HEAD_DIM), 0).astype(jnp.float32)
    mask = jnp.where(rows < length, 1.0, 0.0).astype(jnp.bfloat16)
    for h in range(KV_HEADS // CORES):
        i = h * CORES + r
        q_parts, g_parts, keys, values = pieces(h)
        queries = jnp.concatenate(q_parts, axis=0)
        grads = jnp.concatenate([g * mask for g in g_parts], axis=0)
        qs_ref[i], gs_ref[i], ks_ref[i], vs_ref[i] = queries, grads, keys, values
        scores = causal(dot_nt(keys, queries) * EXP2_SCALE)
        dprobs = dot_nt(values, grads)
        top = jnp.max(scores, axis=0, keepdims=True)
        terms = jnp.exp2(scores - top)
        stats_ref[i, 0:1] = top
        stats_ref[i, 1:2] = jnp.sum(terms, axis=0, keepdims=True)
        stats_ref[i, 2:3] = jnp.sum(terms * dprobs, axis=0, keepdims=True)


def near_own_kernel(
    own_q, own_g, own_k, own_v, _after, meta_ref,
    qs_ref, gs_ref, ks_ref, vs_ref, stats_ref, held_ref, sems,
):
    core = lax.axis_index("group") % CORES
    heads = KV_HEADS // CORES
    wide = heads * LANES
    at, copies = 0, []
    for i, ref in enumerate((own_q, own_g, own_k, own_v)):
        half = ref.shape[1] // CORES
        cols = pl.ds(pl.multiple_of(core * half, half), half)
        to = held_ref.at[:, pl.ds(at, half)]
        copies.append(pltpu.make_async_copy(ref.at[:, cols], to, sems.at[i]))
        copies[-1].start()
        at += half
    for copy in copies:
        copy.wait()

    def pieces(h):
        def piece(at):
            return held_ref[:, at : at + HEAD_DIM]

        spots = range(h * LANES, (h + 1) * LANES, HEAD_DIM)
        at = 2 * wide + h * HEAD_DIM
        return (
            [piece(n) for n in spots], [piece(wide + n) for n in spots],
            piece(at), piece(at + heads * HEAD_DIM),
        )

    near_jobs(0, meta_ref[0:1, 64:65], pieces, qs_ref, gs_ref, ks_ref, vs_ref, stats_ref)


def near_other_kernel(
    q_0, q_1, g_0, g_1, kv_ref, _qs, _gs, _ks, _vs, _stats,
    qs_ref, gs_ref, ks_ref, vs_ref, stats_ref, meta_ref,
):
    heads = KV_HEADS // CORES
    payload = kv_ref[0:16, 2 * heads * HEAD_DIM :].astype(jnp.float32)
    meta_ref[...] = payload[0:8]

    def pieces(h):
        def piece(ref, at):
            return ref[:, at : at + HEAD_DIM]

        spots = range(0, LANES, HEAD_DIM)
        at = h * HEAD_DIM
        return (
            [piece((q_0, q_1)[h], n) for n in spots], [piece((g_0, g_1)[h], n) for n in spots],
            piece(kv_ref, at), piece(kv_ref, at + heads * HEAD_DIM),
        )

    near_jobs(1, payload[0:1, 64:65], pieces, qs_ref, gs_ref, ks_ref, vs_ref, stats_ref)


def advantages(own_meta, swap_meta, extra):
    rows = extra.shape[0]
    members = 16
    unit = 1.0 / (BUCKETS - 1)
    sums = jnp.sum(extra.astype(jnp.float32), axis=0, keepdims=True)[:, 0:1]
    mean = sums * (unit / rows)
    own = own_meta[:, 0:1] * unit - mean
    other = swap_meta[:, 0:1] * unit - mean
    return own, other


def far_jobs(
    first, last, own_meta_ref, meta_ref, near_ref, gathered_ref, qs_ref, gs_ref,
    slopes_out, stats_out, send_ref, acc_ref, slopes_ref, stats_ref, probs_ref, sems,
):
    width = KV_HEADS // CORES * HEAD_DIM
    own_scale, other_scale = advantages(
        own_meta_ref[0:1], meta_ref[0:1], gathered_ref[:, 2 * width :]
    )

    def saves(i):
        return (
            pltpu.make_async_copy(slopes_ref.at[i], slopes_out.at[i], sems.at[0, i]),
            pltpu.make_async_copy(stats_ref.at[i], stats_out.at[i], sems.at[1, i]),
        )

    def job(i, _):
        h, r = i // CORES, i % CORES
        keys = gathered_ref[:, pl.ds(pl.multiple_of(h * HEAD_DIM, HEAD_DIM), HEAD_DIM)]
        values = gathered_ref[:, pl.ds(pl.multiple_of(width + h * HEAD_DIM, HEAD_DIM), HEAD_DIM)]
        scores = dot_nt(keys, qs_ref[i]) * EXP2_SCALE
        dprobs = dot_nt(values, gs_ref[i])
        near_top = near_ref[i, 0:1]
        top = jnp.maximum(jnp.max(scores, axis=0, keepdims=True), near_top)
        shift = jnp.exp2(near_top - top)
        terms = jnp.exp2(scores - top)
        total = jnp.sum(terms, axis=0, keepdims=True) + near_ref[i, 1:2] * shift
        delta = jnp.sum(terms * dprobs, axis=0, keepdims=True) + near_ref[i, 2:3] * shift
        inverse = 1.0 / total
        delta = delta * inverse
        probs = terms * inverse
        probs_ref[...] = probs.astype(jnp.bfloat16)
        slopes_ref[i] = (probs * (dprobs - delta)).astype(jnp.bfloat16)
        stats_ref[i, 0:1] = top
        stats_ref[i, 1:2] = inverse
        stats_ref[i, 2:3] = delta
        for copy in saves(i):
            copy.start()
        scale = jnp.where(r == 0, own_scale, other_scale)
        key_part = dot_nn(slopes_ref[i], qs_ref[i]) * (scale * SCALE)
        value_part = dot_nn(probs_ref[...], gs_ref[i]) * scale

        @pl.when(r == 0)
        def _():
            acc_ref[0], acc_ref[1] = key_part, value_part

        @pl.when(r == 1)
        def _():
            for n, part in enumerate((key_part, value_part)):
                cols = pl.ds(pl.multiple_of(n * width + h * HEAD_DIM, HEAD_DIM), HEAD_DIM)
                send_ref[:, cols] = (acc_ref[n] + part).astype(jnp.bfloat16)

        return 0

    def drain(i, _):
        for copy in saves(i):
            copy.wait()
        return 0

    lax.fori_loop(first, last, job, 0)
    lax.fori_loop(first, last, drain, 0)


def jobs_before():
    z = lax.axis_index("dp") // 2
    return jnp.where(z < 2, 2, jnp.where(z < 4, 1, 0))


def first_far_kernel(
    own_meta_ref, meta_ref, near_ref, gathered_ref, _qs, _gs, _ks, _vs,
    slopes_out, stats_out, send_ref, acc_ref, qs_ref, gs_ref, _ks_out, _vs_out, *scratch,
):
    far_jobs(
        0, jobs_before(), own_meta_ref, meta_ref, near_ref, gathered_ref, qs_ref, gs_ref,
        slopes_out, stats_out, send_ref, acc_ref, *scratch,
    )


def second_far_kernel(
    own_meta_ref, meta_ref, near_ref, gathered_ref, _slopes, _stats,
    _send, _acc, _qs, _gs, _ks, _vs,
    slopes_out, stats_out, send_ref, acc_ref, qs_ref, gs_ref, _ks_out, _vs_out, *scratch,
):
    far_jobs(
        jobs_before(), KV_HEADS, own_meta_ref, meta_ref, near_ref, gathered_ref, qs_ref, gs_ref,
        slopes_out, stats_out, send_ref, acc_ref, *scratch,
    )


def part_kernel(
    tokens_ref, own_meta_ref, meta_ref, gathered_ref, _send, part_ref, adv_ref, send_ref, sems
):
    rows, wide = send_ref.shape
    width = wide - HEAD_DIM
    tokens = jnp.broadcast_to(tokens_ref[0:1, HEAD_DIM // 2 : HEAD_DIM // 2 + 1], (1, HEAD_DIM))
    high = jnp.floor(tokens * (1.0 / 256.0))
    lanes = lax.broadcasted_iota(jnp.int32, tokens.shape, 1)
    tokens = jnp.where(lanes < HEAD_DIM // 2, high, tokens - high * 256.0)
    send_ref[:, width:] = jnp.broadcast_to(tokens, (rows, HEAD_DIM)).astype(jnp.bfloat16)
    step = rows // 8
    copies = []
    for n in range(8):
        block = pl.ds(n * step, step)
        copies.append(pltpu.make_async_copy(send_ref.at[block], part_ref.at[block], sems.at[n]))
        copies[n].start()
    own, _ = advantages(own_meta_ref[0:1], meta_ref[0:1], gathered_ref[:, width:])
    adv_ref[...] = jnp.broadcast_to(own, adv_ref.shape)
    for copy in copies:
        copy.wait()


def own_kernel(
    qs_ref, gs_ref, ks_ref, vs_ref, gathered_ref, slopes_in, stats_in, own_out, swap_0, swap_1, swap_kv, own_ref, slopes_ref, stats_ref, sems, out_sems,
):
    heads = KV_HEADS // CORES
    slots = ks_ref.shape[1]
    loads = {}
    for r in (1, 0):
        for h in range(heads):
            i = h * CORES + r
            loads[i] = (
                pltpu.make_async_copy(slopes_in.at[i], slopes_ref.at[i], sems.at[0, i]),
                pltpu.make_async_copy(stats_in.at[i], stats_ref.at[i], sems.at[1, i]),
            )
            for load in loads[i]:
                load.start()
    copies = []
    for r in (1, 0):
        for h in range(heads):
            i = h * CORES + r
            if r:
                gq_ref, gq_at, kv_ref, kv_at = (swap_0, swap_1)[h], 0, swap_kv, 0
            else:
                gq_ref, gq_at, kv_ref, kv_at = own_ref, h * LANES, own_ref, heads * LANES
            queries, grads = qs_ref[i], gs_ref[i]
            keys, values = ks_ref[i], vs_ref[i]
            scores = causal(dot_nt(keys, queries) * EXP2_SCALE)
            dprobs = dot_nt(values, grads)
            loads[i][1].wait()
            top, inverse, delta = stats_ref[i, 0:1], stats_ref[i, 1:2], stats_ref[i, 2:3]
            probs = jnp.exp2(scores - top) * inverse
            slopes = (probs * (dprobs - delta)).astype(jnp.bfloat16)
            far_keys = gathered_ref[:, h * HEAD_DIM : (h + 1) * HEAD_DIM]
            loads[i][0].wait()
            gq = dot_tn(far_keys, slopes_ref[i]) + dot_tn(keys, slopes)
            for n in range(GROUP_HEADS):
                at = gq_at + n * HEAD_DIM
                gq_ref[:, at : at + HEAD_DIM] = gq[:, n * slots : (n + 1) * slots].T.astype(
                    jnp.bfloat16
                )
            at = kv_at + h * HEAD_DIM
            kv_ref[:, at : at + HEAD_DIM] = dot_nn(slopes, queries).astype(jnp.bfloat16)
            at += heads * HEAD_DIM
            kv_ref[:, at : at + HEAD_DIM] = dot_nn(probs.astype(jnp.bfloat16), grads).astype(
                jnp.bfloat16
            )
    copy = pltpu.make_async_copy(own_ref, own_out, out_sems.at[0])
    copy.start()
    copy.wait()


def finish_kernel(
    adv_ref, recv_ref, own_in, swap_0, swap_1, swap_kv,
    gq_out, gk_out, gv_out, far_k_out, far_v_out,
    own_ref, gq_ref, gk_ref, gv_ref, far_k_ref, far_v_ref, in_sem, sems,
):
    load = pltpu.make_async_copy(own_in, own_ref, in_sem.at[0])
    load.start()
    core = lax.axis_index("group") % CORES
    members = recv_ref.shape[0]
    width = gk_ref.shape[1] // CORES
    slots = own_ref.shape[0]
    wide = gq_ref.shape[1] // CORES
    advantage = adv_ref[0:1, 0:1]
    tokens = jnp.sum(recv_ref[:, 0:1, 2 * width :].astype(jnp.float32), axis=0)
    token_total = tokens[:, 0:1] * 256.0 + tokens[:, HEAD_DIM // 2 : HEAD_DIM // 2 + 1]
    norm = (16 * 16 * slots) / token_total
    factor = advantage * norm
    copies = []

    def put(ref, at, value, scale):
        cols = pl.ds(pl.multiple_of(at, HEAD_DIM), value.shape[1])
        ref[:, cols] = (value.astype(jnp.float32) * scale).astype(jnp.bfloat16)

    def send(source, to):
        copies.append(pltpu.make_async_copy(source, to, sems.at[len(copies)]))
        copies[-1].start()

    def put_queries(at, value):
        put(gq_ref, at, value, factor * SCALE)
        cols = pl.ds(pl.multiple_of(at, HEAD_DIM), value.shape[1])
        send(gq_ref.at[:, cols], gq_out.at[:, cols])

    other = 1 - core
    put_queries(other * wide, swap_0[...])
    put_queries(other * wide + LANES, swap_1[...])
    put(gk_ref, other * width, swap_kv[:, :width], factor * SCALE)
    put(gv_ref, other * width, swap_kv[:, width:], factor)
    for c in range(CORES):
        total = recv_ref[c, :, : 2 * width].astype(jnp.float32)
        for m in range(c + CORES, members, CORES):
            total = total + recv_ref[m, :, : 2 * width].astype(jnp.float32)
        total = total * norm
        far_k_ref[:, c * width : (c + 1) * width] = total[:, :width].astype(jnp.bfloat16)
        far_v_ref[:, c * width : (c + 1) * width] = total[:, width:].astype(jnp.bfloat16)
    send(far_k_ref, far_k_out)
    send(far_v_ref, far_v_out)
    load.wait()
    put_queries(core * wide, own_ref[:, :LANES])
    put_queries(core * wide + LANES, own_ref[:, LANES:wide])
    put(gk_ref, core * width, own_ref[:, wide : wide + width], factor * SCALE)
    put(gv_ref, core * width, own_ref[:, wide + width :], factor)
    send(gk_ref, gk_out)
    send(gv_ref, gv_out)
    for copy in copies:
        copy.wait()


def vmem():
    return pl.BlockSpec(memory_space=pltpu.VMEM)


def anywhere():
    return pl.BlockSpec(memory_space=pl.ANY)


def near_memory(x):
    return pltpu.with_memory_space_constraint(x, pltpu.VMEM)


def far_memory(x):
    return pltpu.with_memory_space_constraint(x, pltpu.HBM)


def call(kernel, in_specs, out_specs, out_shape, flops, nbytes, scratch=(), aliases=None):
    return pl.pallas_call(
        kernel,
        in_specs=in_specs,
        out_specs=out_specs,
        out_shape=out_shape,
        scratch_shapes=list(scratch),
        input_output_aliases=aliases or {},
        compiler_params=pltpu.CompilerParams(vmem_limit_bytes=VMEM),
        cost_estimate=pl.CostEstimate(flops=flops, bytes_accessed=nbytes, transcendentals=0),
    )


def body(
    prefix_keys, prefix_values, resp_queries, resp_keys, resp_values, grad_out, lengths, buckets
):
    slots = resp_queries.shape[2]
    own_rows = prefix_keys.shape[1]
    members = lax.axis_size("group")
    rows = own_rows * members
    heads = KV_HEADS // CORES
    width = heads * HEAD_DIM
    wide = heads * LANES
    jobs = heads * CORES
    q, g = resp_queries[0, 0], grad_out[0, 0]
    kn, vn = resp_keys[0, 0], resp_values[0, 0]
    f32, bf16 = jnp.float32, jnp.bfloat16
    pairs = [(i, i ^ 1) for i in range(members)]

    meta = jnp.pad(buckets.astype(f32), ((0, 7), (0, HEAD_DIM - 1)))
    meta += jnp.pad(lengths.astype(f32), ((0, 7), (HEAD_DIM // 2, HEAD_DIM // 2 - 1)))
    spread = call(
        spread_kernel,
        [anywhere(), anywhere(), vmem()],
        anywhere(),
        pltpu.HBM((members, own_rows, 2 * width + HEAD_DIM), bf16),
        0, 1 << 20,
        [pltpu.VMEM((CORES, own_rows, 2 * width + HEAD_DIM), bf16),
         pltpu.SemaphoreType.DMA((4,)), pltpu.SemaphoreType.DMA((members,))],
    )(far_memory(prefix_keys[0]), far_memory(prefix_values[0]), near_memory(meta))
    gathered3 = lax.all_to_all(spread, "group", 0, 0, tiled=True)
    gathered = gathered3.reshape(rows, -1)

    swap = call(
        swap_kernel,
        [anywhere()] * 5 + [vmem()],
        [vmem()] * 5,
        [pltpu.VMEM((slots, LANES), bf16)] * 4 + [pltpu.VMEM((slots, 2 * width + HEAD_DIM), bf16)],
        0, 2 << 20,
        [pltpu.SemaphoreType.DMA((6,))],
    )(*(far_memory(x) for x in (q, g, kn, vn, spread)), near_memory(meta))
    swapped = [lax.ppermute(x, "group", pairs) for x in swap]

    near_shapes = [
        pltpu.VMEM((jobs, LANES, HEAD_DIM), bf16), pltpu.VMEM((jobs, LANES, HEAD_DIM), bf16),
        pltpu.VMEM((jobs, slots, HEAD_DIM), bf16), pltpu.VMEM((jobs, slots, HEAD_DIM), bf16),
        pltpu.VMEM((jobs, 8, LANES), f32),
    ]
    nears = call(
        near_own_kernel,
        [anywhere()] * 5 + [vmem()],
        [vmem()] * 5,
        near_shapes,
        2 * 4096 * 128 * 128, 2 << 20,
        [pltpu.VMEM((slots, 2 * wide + 2 * width), bf16), pltpu.SemaphoreType.DMA((4,))],
    )(*(far_memory(x) for x in (q, g, kn, vn, spread)), near_memory(meta))
    qs, gs, ks, vs, near, meta_in = call(
        near_other_kernel,
        [vmem()] * 10,
        [vmem()] * 6,
        near_shapes + [pltpu.VMEM((8, HEAD_DIM), f32)],
        2 * 4096 * 128 * 128, 2 << 20,
        (),
        {5 + n: n for n in range(5)},
    )(*(near_memory(x) for x in (*swapped, *nears)))

    kept = (qs, gs, ks, vs)
    shared = [near_memory(x) for x in (meta, meta_in, near, gathered)]
    saved_shapes = [pltpu.HBM((jobs, rows, LANES), bf16), pltpu.HBM((jobs, 8, LANES), f32)]
    kept_shapes = [pltpu.VMEM((rows, 2 * width + HEAD_DIM), bf16),
                   pltpu.VMEM((2, rows, HEAD_DIM), f32)]
    kept_shapes += [pltpu.VMEM(x.shape, x.dtype) for x in kept]
    scratch = [pltpu.VMEM((jobs, rows, LANES), bf16), pltpu.VMEM((jobs, 8, LANES), f32),
               pltpu.VMEM((rows, LANES), bf16), pltpu.SemaphoreType.DMA((2, jobs))]
    slopes, stats, *kept = call(
        first_far_kernel,
        [vmem()] * 8,
        [anywhere()] * 2 + [vmem()] * 6,
        saved_shapes + kept_shapes,
        2 * 2 * 4096 * 384 * 128, 4 << 20,
        scratch,
        {4 + n: 4 + n for n in range(4)},
    )(*shared, *(near_memory(x) for x in kept))

    dp = lax.axis_size("dp")
    payload, _ = lax.optimization_barrier((gathered3, stats))
    tokens = jnp.sum(payload[:, :8, 2 * width :].astype(f32), axis=0)
    turns = (0, 4, 9, 7, 15, 11, 1, 12, 2, 14, 6, 10, 8, 3, 13, 5)
    pairs_dp = [
        (d * members + i, (d ^ turns[i % dp]) * members + i)
        for d in range(dp)
        for i in range(members)
    ]
    tokens = lax.ppermute(tokens, ("dp", "group"), pairs_dp)

    slopes, stats, send, _, *kept = call(
        second_far_kernel,
        [vmem()] * 4 + [anywhere()] * 2 + [vmem()] * 6,
        [anywhere()] * 2 + [vmem()] * 6,
        saved_shapes + kept_shapes,
        2 * 2 * 4096 * 384 * 128, 4 << 20,
        scratch,
        {4 + n: n for n in range(8)},
    )(*shared, far_memory(slopes), far_memory(stats), *(near_memory(x) for x in kept))

    part, adv, _ = call(
        part_kernel,
        [vmem()] * 5,
        [anywhere(), vmem(), vmem()],
        [pltpu.HBM((rows, 2 * width + HEAD_DIM), bf16), pltpu.VMEM((8, HEAD_DIM), f32),
         pltpu.VMEM((rows, 2 * width + HEAD_DIM), bf16)],
        0, 1 << 19,
        [pltpu.SemaphoreType.DMA((8,))],
        {4: 2},
    )(*(near_memory(x) for x in (tokens, meta, meta_in, gathered, send)))

    recv = lax.all_to_all(part.reshape(members, own_rows, -1), "group", 0, 0, tiled=True)

    own, *swap_out = call(
        own_kernel,
        [vmem()] * 5 + [anywhere()] * 2,
        [anywhere()] + [vmem()] * 3,
        [pltpu.HBM((slots, wide + 2 * width), bf16), pltpu.VMEM((slots, LANES), bf16),
         pltpu.VMEM((slots, LANES), bf16), pltpu.VMEM((slots, 2 * width), bf16)],
        3 * 2 * 4096 * 512 * 128, 8 << 20,
        [pltpu.VMEM((slots, wide + 2 * width), bf16), pltpu.VMEM((jobs, rows, LANES), bf16),
         pltpu.VMEM((jobs, 8, LANES), f32), pltpu.SemaphoreType.DMA((2, jobs)),
         pltpu.SemaphoreType.DMA((1,))],
    )(*(near_memory(x) for x in (*kept, gathered)), far_memory(slopes), far_memory(stats))
    swap_in = [lax.ppermute(x, "group", pairs) for x in swap_out]

    outs = call(
        finish_kernel,
        [vmem()] * 2 + [anywhere()] + [vmem()] * 3,
        [anywhere()] * 5,
        [pltpu.HBM((slots, HEADS * HEAD_DIM), bf16),
         pltpu.HBM((slots, CORES * width), bf16), pltpu.HBM((slots, CORES * width), bf16),
         pltpu.HBM((own_rows, CORES * width), bf16), pltpu.HBM((own_rows, CORES * width), bf16)],
        0, 4 << 20,
        [pltpu.VMEM((slots, wide + 2 * width), bf16), pltpu.VMEM((slots, HEADS * HEAD_DIM), bf16),
         pltpu.VMEM((slots, CORES * width), bf16), pltpu.VMEM((slots, CORES * width), bf16),
         pltpu.VMEM((own_rows, CORES * width), bf16), pltpu.VMEM((own_rows, CORES * width), bf16),
         pltpu.SemaphoreType.DMA((1,)), pltpu.SemaphoreType.DMA((8,))],
    )(*(near_memory(x) for x in (adv, recv)),
      far_memory(own), *(near_memory(x) for x in swap_in))
    gq, gk, gv, far_k, far_v = outs
    return gq[None, None], gk[None, None], gv[None, None], far_k[None], far_v[None]


def solution(mesh):
    in_specs = (
        P("dp", "group", None),
        P("dp", "group", None),
        P("dp", "group", None, None),
        P("dp", "group", None, None),
        P("dp", "group", None, None),
        P("dp", "group", None, None),
        P("dp", "group"),
        P("dp", "group"),
    )
    out_specs = (
        P("dp", "group", None, None),
        P("dp", "group", None, None),
        P("dp", "group", None, None),
        P("dp", "group", None),
        P("dp", "group", None),
    )
    return jax.shard_map(body, mesh=mesh, in_specs=in_specs, out_specs=out_specs, check_vma=False)
```
